32 devices in a mesh: gx: 2 (over x), gy: 4 (over y, core), gz: 4 (over z).
Axes of the slice: x: 2, y: 2, z: 4, core: 2. Of those that a mesh axis runs over, the one named last changes fastest.
Arguments:
- estimate: float32 [32, 64, 1024], P('gx', 'gy', 'gz'), may hold values from 0.5 to 2
- raw_lines: float32 [2, 2, 16, 512, 256], P(None, 'gx', ('gy', 'gz')), may hold values from 0.2 to 3
- line_index: int32 [2, 2, 16, 512], P(None, 'gx', ('gy', 'gz')), may hold values from 0 to 256, as said below
- psf: float32 [2, 3, 33], replicated, may hold values from 0.05 to 1
- view_weight: int32 [2, 2, 4, 4], P(None, 'gx', 'gy', 'gz'), may hold values from 1 to 4
Outputs:
- updated: float32 [32, 64, 1024], P('gx', 'gy', 'gz')
The draws below stay inside these ranges and needn't reach their ends.
Inputs may be any that keep to these rules, and one draw needn't show every extreme that they name: `line_index`: 256 marks an empty slot; every other entry is a z-line of the destination block, and each z-line of a destination block gets at most one slot per view. In every view and every x-block, some owner sends all 32 slots filled to some destination, and some destination block receives all 16 * 16 z-lines; blocks receive different numbers of z-lines from different numbers of owners.
All inputs are finite; a program needn't handle non-finite values.
Results may differ from the reference program's by a relative error of at most 0.0001.
Values sent between devices are 32-bit elements; how exact they have to be, the bound alone decides.
No kernel may reach another device: no remote copies, remote signals or barrier semaphores. Data moves between devices by JAX's collectives and lax.ppermute only.
A program may use at most 64 MiB of HBM per device.

```python
import math
import jax
import jax.numpy as jnp
from jax import lax

BX = 16
BY = 16
BZ = 256
HALF = 16
VIEWS = 2
TAPS = 33
CAP = 32
NX = 32
NY = 64
NZ = 1024
N_GX = 2
N_GY = 4
N_GZ = 4


def draw_line_index(key, part):
    key = jax.random.fold_in(key, 11)
    group = N_GY * N_GZ
    block_lines = BX * BY
    keys = jax.random.split(jax.random.fold_in(key, 1), VIEWS * N_GX * group)
    perms = jax.vmap(lambda single: jax.random.permutation(single, block_lines))(keys).astype(jnp.int32)
    perms = perms.reshape(VIEWS, N_GX, group, block_lines)
    covered = block_lines - jax.random.randint(jax.random.fold_in(key, 2), (VIEWS, N_GX, group), 0, block_lines // 4 + 1)
    full_dest = jax.random.randint(jax.random.fold_in(key, 3), (VIEWS, N_GX, 1), 0, group)
    covered = jnp.where(jnp.arange(group, dtype=jnp.int32)[None, None, :] == full_dest, block_lines, covered).astype(jnp.int32)
    start = jax.random.randint(jax.random.fold_in(key, 4), (VIEWS, N_GX, group), 0, group).astype(jnp.int32)
    source = jnp.arange(group, dtype=jnp.int32)[:, None]
    slot = jnp.arange(CAP, dtype=jnp.int32)[None, :]
    rank = (source[None, None, None] - start[..., None, None]) % group * CAP + slot[None, None, None]
    padded = jnp.concatenate([perms, jnp.full((VIEWS, N_GX, group, group * CAP - block_lines), block_lines, jnp.int32)], axis=-1)
    picked = jnp.take_along_axis(padded, rank.reshape(VIEWS, N_GX, group, group * CAP), axis=-1)
    picked = picked.reshape(VIEWS, N_GX, group, group, CAP)
    picked = jnp.where(rank < covered[..., None, None], picked, block_lines)
    return picked.transpose(0, 1, 3, 2, 4).reshape(VIEWS, N_GX, group, group * CAP).astype(jnp.int32)


def plant(drawn, own_key, low, high):
    place = [jax.random.randint(jax.random.fold_in(own_key, axis), (), 0, length) for axis, length in enumerate(drawn.shape)]
    longest = drawn.shape.index(max(drawn.shape))
    neighbour = place[:longest] + [(place[longest] + 1) % drawn.shape[longest]] + place[longest + 1:]
    return drawn.at[tuple(place)].set(low).at[tuple(neighbour)].set(high)


def block_levels(rng, extent, pieces, low, high):
    def one(position, parts):
        heights = jax.random.uniform(jax.random.fold_in(jax.random.fold_in(rng, 6), position), (parts,), jnp.float32, low / len(pieces), high / len(pieces))
        return jnp.repeat(jnp.exp(heights), extent[position] // parts).reshape((-1,) + (1,) * (len(extent) - position - 1))

    level = one(*pieces[0])
    for cut in pieces[1:]:
        level = level * one(*cut)
    return level


def setup_inputs(seed: int = 0) -> dict:
    splits = jax.random.split(jax.random.key(seed), 6)
    return {
        "estimate": jnp.clip(0.5 + 1.5 * jax.random.uniform(splits[0], (NX, NY, NZ), jnp.float32) ** block_levels(splits[0], (NX, NY, NZ), ((0, 2), (1, 4), (2, 4)), -0.2, 0.2), 0.5, 2.0),
        "raw_lines": jnp.clip(0.2 + 2.8 * jax.random.uniform(splits[1], (VIEWS, N_GX, N_GY * N_GZ, N_GY * N_GZ * CAP, BZ), jnp.float32) ** block_levels(splits[1], (VIEWS, N_GX, N_GY * N_GZ, N_GY * N_GZ * CAP, BZ), ((1, 2), (2, 16)), -0.2, 0.2), 0.2, 3.0),
        "line_index": draw_line_index(jax.random.fold_in(splits[5], 71), 0),
        "psf": jnp.clip(jnp.exp(jax.random.uniform(splits[3], (VIEWS, 3, TAPS), jnp.float32, math.log(0.05), math.log(1.0))), 0.05, 1.0),
        "view_weight": plant(jax.random.randint(splits[4], (VIEWS, N_GX, N_GY, N_GZ), 1, 5), jax.random.fold_in(splits[4], 1), 1, 4).astype(jnp.int32),
    }


def correlate(vol, taps, axis):
    moved = jnp.moveaxis(vol, axis, -1)
    shape = moved.shape
    flat = moved.reshape(-1, 1, shape[-1])
    out = lax.conv_general_dilated(flat, taps.reshape(1, 1, -1), (1,), [(HALF, HALF)], precision=lax.Precision.HIGHEST)
    return jnp.moveaxis(out.reshape(shape), -1, axis)


def blur(vol, taps):
    out = correlate(vol, taps[2], 2)
    out = correlate(out, taps[1], 1)
    return correlate(out, taps[0], 0)


def reference(estimate, raw_lines, line_index, psf, view_weight):
    group = N_GY * N_GZ
    block_lines = BX * BY
    total = N_GX * group * block_lines
    est = estimate
    for view in range(VIEWS):
        index = line_index[view].reshape(N_GX, group, group, CAP)
        block_of = (jnp.arange(N_GX, dtype=jnp.int32)[:, None, None, None] * group
                    + jnp.arange(group, dtype=jnp.int32)[None, None, :, None])
        target = jnp.where(index == block_lines, total, block_of * block_lines + index).reshape(-1)
        values = raw_lines[view].reshape(-1, BZ)
        volume = jnp.zeros((total, BZ), est.dtype).at[target].set(values, mode="drop")
        volume = volume.reshape(N_GX, N_GY, N_GZ, BX, BY, BZ).transpose(0, 3, 1, 4, 2, 5).reshape(NX, NY, NZ)
        cover = jnp.zeros((total,), est.dtype).at[target].set(1.0, mode="drop")
        cover = cover.reshape(N_GX, N_GY, N_GZ, BX, BY).transpose(0, 3, 1, 4, 2).reshape(NX, NY, N_GZ)
        weight = view_weight[view].astype(est.dtype) * 0.25
        weight = jnp.repeat(jnp.repeat(weight, BX, axis=0), BY, axis=1)
        line_weight = jnp.repeat(weight * cover, BZ, axis=2)
        taps = psf[view] / jnp.sum(psf[view], axis=1, keepdims=True)
        blurred = blur(est, taps)
        ratio = 1.0 + line_weight * (volume / blurred - 1.0)
        est = est * blur(ratio, taps[:, ::-1])
    return est
```

```python
import functools

import jax
import jax.numpy as jnp
from jax import lax
from jax.experimental import pallas as pl
from jax.experimental.pallas import tpu as pltpu
from jax.sharding import PartitionSpec as P

F32, BF16 = jnp.float32, jnp.bfloat16
VMEM = pl.BlockSpec(memory_space=pltpu.VMEM)
SMEM = pl.BlockSpec(memory_space=pltpu.SMEM)
ALL = ("gx", "gy", "gz")
PLANE = ("gx", "gy")


def ring_place(x, y, z):
    place = 2 * x + (x ^ y)
    return place if z % 2 == 0 else 3 - place


def slab_of(device, z):
    x, gy = device // 4, device % 4
    place = ring_place(x, gy // 2, z)
    return 2 * place + ((gy % 2) ^ (place % 2))


def chain_pairs(planes):
    order = []
    for z in range(planes):
        by_slab = sorted(range(8), key=lambda device: slab_of(device, z))
        order += [device * planes + z for device in by_slab]
    far, near = [], []
    for k in range(len(order) - 1):
        pair = (order[k], order[k + 1])
        (near if k % 2 == 0 else far).extend([pair, pair[::-1]])
    return far, near


def split2(value):
    high = value.astype(BF16)
    return high, (value - high.astype(F32)).astype(BF16)


def split3(value):
    high = value.astype(BF16)
    rest = value - high.astype(F32)
    middle = rest.astype(BF16)
    return high, middle, (rest - middle.astype(F32)).astype(BF16)


def dot_nn(a, b):
    return lax.dot_general(a, b, (((1,), (0,)), ((), ())), preferred_element_type=F32)


def dot_nt(a, b):
    return lax.dot_general(a, b, (((1,), (1,)), ((), ())), preferred_element_type=F32)


def call(kernel, out_shapes, in_specs, scratch=(), flops=0, **kwargs):
    return pl.pallas_call(
        kernel,
        out_shape=out_shapes,
        in_specs=in_specs,
        out_specs=jax.tree.map(lambda _: VMEM, out_shapes),
        scratch_shapes=list(scratch),
        compiler_params=pltpu.CompilerParams(vmem_limit_bytes=40 * 1024 * 1024),
        cost_estimate=pl.CostEstimate(flops=flops, bytes_accessed=1 << 20, transcendentals=0),
        **kwargs,
    )


def est_kernel(planes, here, weight, est, out):
    turned = est[...].T
    z_odd = here[2] % 2
    rows = lax.broadcasted_iota(jnp.int32, (8, 256), 0)
    weights = jnp.where(
        rows == 0,
        weight[0, 0].astype(F32) * 0.25,
        jnp.where(rows == 1, weight[1, 0].astype(F32) * 0.25, 0.0),
    )
    for parity in range(2):
        @pl.when(z_odd == parity)
        def _():
            for device in range(8):
                slab = slab_of(device, parity)
                out[device, 0:32, :] = turned[slab * 32 : slab * 32 + 32, :]
    for device in range(8):
        out[device, 32:40, :] = weights


def lines_kernel(planes, here, raw, index, out0, out1):
    mine = here[2]
    chunk = lax.broadcasted_iota(jnp.int32, (8, 128), 1) // 32
    for z in range(planes):
        numbers = [jnp.zeros((8, 128), F32)] * 2
        rows = lax.broadcasted_iota(jnp.int32, (8, 128), 0)
        for place in range(4):
            block = lax.rem(place - mine + 4, 4)
            for view in range(2):
                row = index[pl.ds(view * 4 + block, 1), :].astype(F32)
                row = pltpu.roll(jnp.broadcast_to(row, (8, 128)), (32 * (place - z)) % 128, 1)
                numbers[view] = jnp.where(chunk == place, row, numbers[view])
        both = jnp.where(rows == 0, numbers[0], jnp.where(rows == 1, numbers[1], 0.0))
        for view, out in enumerate((out0, out1)):
            parts = []
            for place in range(4):
                block = lax.rem(place - mine + 4, 4)
                start = pl.multiple_of((block * planes + z) * 32, 32)
                parts.append(raw[view, pl.ds(start, 32), :])
            turned = jnp.concatenate(parts, axis=0).T
            for device in range(8):
                slab = slab_of(device, z)
                out[device * planes + z, 0:32, :] = turned[slab * 32 : slab * 32 + 32, :]
                if view == 0:
                    out[device * planes + z, 32:40, :] = both


def taps_kernel(psf, big_high, big_low, band, held):
    held[...] = jnp.zeros_like(held)
    held[0:3, 0:33] = psf[...]
    taps = held[...]
    total = jnp.sum(taps, axis=1, keepdims=True)
    taps = taps / jnp.where(total == 0.0, 1.0, total)

    def toeplitz(row, size):
        wide = jnp.broadcast_to(row, (size, 128))
        return pltpu.roll(wide, 0, 1, stride=1, stride_axis=0)

    lane_r = lax.broadcasted_iota(jnp.int32, (128, 128), 0)
    lane_c = lax.broadcasted_iota(jnp.int32, (128, 128), 1)
    turn = (lane_r + lane_c == 32).astype(BF16)
    pieces = split3(taps)
    reversed_taps = sum(dot_nn(piece, turn) for piece in pieces)
    for way, source in enumerate((taps, reversed_taps)):
        high, low = split2(toeplitz(source[2:3, :], 32))
        twice = high.astype(F32) + pltpu.roll(high.astype(F32), 64, 1)
        band[way, :, 0:128] = twice.astype(BF16)
        band[way, :, 128:256] = low
    tall_x = jnp.broadcast_to(toeplitz(taps[0:1, :], 16)[:, None, :], (16, 16, 128)).reshape(256, 128)
    tall_y = jnp.broadcast_to(toeplitz(taps[1:2, :], 16)[None], (16, 16, 128)).reshape(256, 128)
    from_row = lax.broadcasted_iota(jnp.int32, (128, 256), 0)
    to_lane = lax.broadcasted_iota(jnp.int32, (128, 256), 1)
    wide_x, wide_y = [], []
    for offset in range(3):
        pick_x = (from_row == to_lane // 16 + 16 * offset).astype(BF16)
        pick_y = (from_row == lax.rem(to_lane, 16) + 16 * offset).astype(BF16)
        wide_x.append(sum(dot_nn(piece, pick_x) for piece in split3(tall_x)))
        wide_y.append(sum(dot_nn(piece, pick_y) for piece in split3(tall_y)))
    for dx in range(3):
        for dy in range(3):
            high, low = split2(wide_x[dx] * wide_y[dy])
            big_high[dx * 3 + dy] = high
            big_low[dx * 3 + dy] = low


def scatter_kernel(view, recv0, recv1, slab, data, cover):
    chunk = lax.broadcasted_iota(jnp.int32, (40, 128), 1) // 32
    line = lax.broadcasted_iota(jnp.int32, (256, 512), 0).astype(F32)
    recv = recv1 if view else recv0
    ones = jnp.ones((16, 512), BF16)
    for x in range(2):
        for block in range(4):
            column = x * 4 + block
            numbers, values = [], []
            for t in range(4):
                tile = jnp.zeros((32, 128), F32)
                number = jnp.zeros((8, 128), F32)
                for place in range(4):
                    source = x * 16 + 4 * t + (place - block) % 4
                    tile = jnp.where(chunk[0:32] == place, recv[source, 0:32, :], tile)
                    number = jnp.where(chunk[0:8] == place, recv0[source, 32:40, :], number)
                values.append(tile)
                numbers.append(number)
            value = jnp.concatenate(values, axis=1)
            number = jnp.concatenate(numbers, axis=1)[view : view + 1, :]
            hot = (line == number).astype(BF16)
            left = jnp.concatenate([*split3(value), ones], axis=0)
            result = dot_nt(left, hot)
            data[column] = result[0:32] + result[32:64] + result[64:96]
            weight = slab[column, 32 + view : 33 + view, :]
            cover[column] = result[96:104] * weight


def payloads(here, value, far, near):
    upper = here[3]
    far[...] = value[:, pl.ds(pl.multiple_of(16 * upper, 16), 16), :]
    near[...] = value[:, pl.ds(pl.multiple_of(16 - 16 * upper, 16), 16), :]


def send_kernel(here, slab, far, near):
    payloads(here, slab, far, near)


def blurred_into(here, way, value, far, near, band, big_high, big_low, wide, flat, total):
    upper = here[3]
    wide[:, 16:48, :] = value[:, 0:32, :]
    wide[:, pl.ds(pl.multiple_of(48 * upper, 16), 16), :] = far[...]
    wide[:, pl.ds(pl.multiple_of(48 - 48 * upper, 16), 16), :] = near[...]
    weights = band[way]
    for column in range(8):
        high, low = split2(wide[column])
        stacked = jnp.concatenate([high, low, high, high], axis=0)
        flat[column * 32 : column * 32 + 32, :] = dot_nn(weights, stacked)
    high, low = split2(flat[...])

    def product(start, stop, dx, dy):
        if way == 0:
            at, dot = (dx + 1) * 3 + dy + 1, dot_nt
        else:
            at, dot = (1 - dx) * 3 + 1 - dy, dot_nn
        rows = stop - start
        both = dot(jnp.concatenate([high[start:stop], low[start:stop]], axis=0), big_high[at])
        return both[:rows] + both[rows:] + dot(high[start:stop], big_low[at])

    total[...] = product(0, 256, 0, 0)
    for dx in (-1, 0, 1):
        for dy in (-1, 0, 1):
            if dx == 0 and dy == 0:
                continue
            for x in range(2):
                if not 0 <= x + dx < 2:
                    continue
                first, last = max(0, -dy), min(4, 4 - dy)
                out = (x * 4 + first) * 32, (x * 4 + last) * 32
                shift = (dx * 4 + dy) * 32
                total[out[0] : out[1], :] += product(out[0] + shift, out[1] + shift, dx, dy)


def ratio_kernel(here, est, far, near, band, big_high, big_low, data, cover, ratio, next_far, next_near, wide, flat, total):
    blurred_into(here, 0, est, far, near, band, big_high, big_low, wide, flat, total)
    for column in range(8):
        blurred = total[column * 32 : column * 32 + 32, :]
        ratio[column] = 1.0 + cover[column, 0:1, :] * (data[column] / blurred - 1.0)
    payloads(here, ratio, next_far, next_near)


def update_kernel(here, ratio, far, near, band, big_high, big_low, est, new, next_far, next_near, wide, flat, total):
    blurred_into(here, 1, ratio, far, near, band, big_high, big_low, wide, flat, total)
    for column in range(8):
        new[column] = est[column, 0:32, :] * total[column * 32 : column * 32 + 32, :]
    if next_far is not None:
        payloads(here, new, next_far, next_near)


def last_kernel(here, ratio, far, near, band, big_high, big_low, est, new, wide, flat, total):
    update_kernel(here, ratio, far, near, band, big_high, big_low, est, new, None, None, wide, flat, total)


def join_kernel(here, parts, out, held):
    z_odd = here[2] % 2
    for parity in range(2):
        @pl.when(z_odd == parity)
        def _():
            for device in range(8):
                slab = slab_of(device, parity)
                held[slab * 32 : slab * 32 + 32, :] = parts[device]
    out[...] = held[...].T


def shape(*dims, dtype=F32):
    return jax.ShapeDtypeStruct(dims, dtype)


def slab_sweep(planes, estimate, raw_lines, line_index, psf, view_weight):
    x, gy, z = (lax.axis_index(axis) for axis in ALL)
    y, core = gy // 2, gy % 2
    place = 2 * x + (x ^ y)
    place = jnp.where(z % 2 == 0, place, 3 - place)
    here = jnp.stack([x, gy, z, core ^ (place % 2)]).astype(jnp.int32)
    far_pairs, near_pairs = chain_pairs(planes)

    def exchange(far, near):
        return (
            lax.ppermute(far, ALL, far_pairs),
            lax.ppermute(near, ALL, near_pairs),
        )

    pieces = call(
        functools.partial(est_kernel, planes),
        shape(8, 40, 256),
        [SMEM, SMEM, VMEM],
    )(here, view_weight.reshape(2, 1), estimate.reshape(256, 256))
    slab = lax.all_to_all(pieces, PLANE, split_axis=0, concat_axis=0, tiled=True)
    lines0, lines1 = call(
        functools.partial(lines_kernel, planes),
        (shape(8 * planes, 40, 128), shape(8 * planes, 32, 128)),
        [SMEM, VMEM, VMEM],
    )(here, raw_lines.reshape(2, 4 * planes * 32, 256), line_index.reshape(8, 128))
    lines0 = lax.all_to_all(lines0, ALL, split_axis=0, concat_axis=0, tiled=True)
    lines1 = lax.all_to_all(lines1, ALL, split_axis=0, concat_axis=0, tiled=True)
    half = shape(8, 16, 256)
    scratch = [pltpu.VMEM((8, 64, 256), F32), pltpu.VMEM((256, 256), F32), pltpu.VMEM((256, 256), F32)]
    far, near = call(send_kernel, (half, half), [SMEM, VMEM])(here, slab)
    est = slab
    for view in range(2):
        big_high, big_low, band = call(
            taps_kernel,
            (shape(9, 256, 256, dtype=BF16), shape(9, 256, 256, dtype=BF16), shape(2, 32, 256, dtype=BF16)),
            [VMEM],
            [pltpu.VMEM((8, 128), F32)],
            flops=1 << 30,
        )(psf[view])
        data, cover = call(
            functools.partial(scatter_kernel, view),
            (shape(8, 32, 256), shape(8, 8, 256)),
            [VMEM] * 3,
            flops=1 << 30,
        )(lines0, lines1, slab)
        mats = (band, big_high, big_low)
        ratio, far, near = call(
            ratio_kernel, (shape(8, 32, 256), half, half), [SMEM] + [VMEM] * 8, scratch, flops=1 << 30
        )(here, est, *exchange(far, near), *mats, data, cover)
        if view == 0:
            est, far, near = call(
                update_kernel, (shape(8, 32, 256), half, half), [SMEM] + [VMEM] * 7, scratch, flops=1 << 30
            )(here, ratio, *exchange(far, near), *mats, est)
        else:
            est = call(last_kernel, shape(8, 32, 256), [SMEM] + [VMEM] * 7, scratch, flops=1 << 30)(
                here, ratio, *exchange(far, near), *mats, est
            )
    parts = lax.all_to_all(est, PLANE, split_axis=0, concat_axis=0, tiled=True)
    out = call(join_kernel, shape(256, 256), [SMEM, VMEM], [pltpu.VMEM((256, 256), F32)])(here, parts)
    return out.reshape(16, 16, 256)


def padded(block, sides, width):
    for axis, dim in sides:
        count = lax.axis_size(axis)
        forward = [(i, i + 1) for i in range(count - 1)]
        backward = [(target, source) for source, target in forward]
        low = lax.ppermute(
            lax.slice_in_dim(block, block.shape[dim] - width, None, axis=dim), axis, forward
        )
        high = lax.ppermute(lax.slice_in_dim(block, 0, width, axis=dim), axis, backward)
        block = jnp.concatenate([low, block, high], axis=dim)
    return block


def band_matrix(taps, length):
    width = taps.shape[0]
    rows = lax.broadcasted_iota(jnp.int32, (length + width - 1, length), 0)
    cols = lax.broadcasted_iota(jnp.int32, (length + width - 1, length), 1)
    offset = rows - cols
    valid = (offset >= 0) & (offset < width)
    return jnp.where(valid, taps[jnp.clip(offset, 0, width - 1)], 0.0)


def along_x(extended, matrix_x):
    lead, size_y, size_z = extended.shape
    flat = extended.reshape(lead, size_y * size_z)
    result = jnp.dot(matrix_x.T, flat, precision=lax.Precision.HIGHEST)
    return result.reshape(matrix_x.shape[1], size_y, size_z)


def blur(field, taps):
    half_width = (taps.shape[1] - 1) // 2
    size_x, size_y, size_z = field.shape
    matrix_x = band_matrix(taps[0], size_x)
    matrix_y = band_matrix(taps[1], size_y)
    matrix_z = band_matrix(taps[2], size_z)
    highest = lax.Precision.HIGHEST
    extended = padded(field, (("gz", 2),), half_width)
    result = jnp.einsum("abj,jc->abc", extended, matrix_z, precision=highest)
    extended = padded(result, (("gy", 1),), half_width)
    result = jnp.einsum("ajc,jb->abc", extended, matrix_y, precision=highest)
    extended = padded(result, (("gx", 0),), half_width)
    result = along_x(extended, matrix_x)
    return result


def block_sweep(estimate, raw_lines, line_index, psf, view_weight):
    size_x, size_y, size_z = estimate.shape
    block_lines = size_x * size_y
    views = raw_lines.shape[0]
    group = lax.axis_size(("gy", "gz"))
    slots = line_index.shape[-1]
    capacity = slots // group
    lines = raw_lines.reshape(views, group, capacity, size_z)
    indices = line_index.reshape(views, group, capacity)
    lines, indices = (
        lax.all_to_all(lines, ("gy", "gz"), split_axis=1, concat_axis=1, tiled=True),
        lax.all_to_all(indices, ("gy", "gz"), split_axis=1, concat_axis=1, tiled=True),
    )
    est = estimate
    for view in range(views):
        flat_index = indices[view].reshape(-1)
        flat_lines = lines[view].reshape(-1, size_z)
        volume = (
            jnp.zeros((block_lines, size_z), jnp.float32)
            .at[flat_index]
            .set(flat_lines, mode="drop")
        )
        volume = volume.reshape(size_x, size_y, size_z)
        cover = jnp.zeros((block_lines,), jnp.float32).at[flat_index].set(1.0, mode="drop")
        cover = cover.reshape(size_x, size_y, 1)
        weight = view_weight[view].reshape(()).astype(jnp.float32) * 0.25
        taps = psf[view] / jnp.sum(psf[view], axis=1, keepdims=True)
        blurred = blur(est, taps)
        ratio = 1.0 + weight * cover * (volume / blurred - 1.0)
        est = est * blur(ratio, taps[:, ::-1])
    return est


def solution(mesh):
    placed = (
        P("gx", "gy", "gz"),
        P(None, "gx", ("gy", "gz"), None, None),
        P(None, "gx", ("gy", "gz"), None),
        P(),
        P(None, "gx", "gy", "gz"),
    )
    sizes = tuple(mesh.shape[axis] for axis in ALL)

    def on_device(estimate, raw_lines, line_index, psf, view_weight):
        capacity = line_index.shape[-1] // (sizes[1] * sizes[2])
        fits = (
            sizes == (2, 4, 4)
            and estimate.shape == (16, 16, 256)
            and raw_lines.shape[0] == 2
            and capacity == 32
            and psf.shape == (2, 3, 33)
        )
        plan = functools.partial(slab_sweep, sizes[2]) if fits else block_sweep
        return plan(estimate, raw_lines, line_index, psf, view_weight)

    return jax.shard_map(
        on_device, mesh=mesh, in_specs=placed, out_specs=P("gx", "gy", "gz"), check_vma=False
    )
```

```python
import functools

import jax
import jax.numpy as jnp
from jax import lax
from jax.experimental import pallas as pl
from jax.experimental.pallas import tpu as pltpu
from jax.sharding import PartitionSpec as P

F32, BF16 = jnp.float32, jnp.bfloat16
VMEM = pl.BlockSpec(memory_space=pltpu.VMEM)
SMEM = pl.BlockSpec(memory_space=pltpu.SMEM)
ALL = ("gx", "gy", "gz")


def ring_place(x, y, z):
    place = 2 * x + (x ^ y)
    return place if z % 2 == 0 else 3 - place


def slab_of(device, z):
    x, gy = device // 4, device % 4
    place = ring_place(x, gy // 2, z)
    return 2 * place + ((gy % 2) ^ (place % 2))


def chain_pairs(planes):
    order = []
    for z in range(planes):
        by_slab = sorted(range(8), key=lambda device: slab_of(device, z))
        order += [device * planes + z for device in by_slab]
    far, near = [], []
    for k in range(len(order) - 1):
        pair = (order[k], order[k + 1])
        (near if k % 2 == 0 else far).extend([pair, pair[::-1]])
    return far, near


def split2(value):
    high = value.astype(BF16)
    return high, (value - high.astype(F32)).astype(BF16)


def split3(value):
    high = value.astype(BF16)
    rest = value - high.astype(F32)
    middle = rest.astype(BF16)
    return high, middle, (rest - middle.astype(F32)).astype(BF16)


def dot_nn(a, b):
    return lax.dot_general(a, b, (((1,), (0,)), ((), ())), preferred_element_type=F32)


def dot_nt(a, b):
    return lax.dot_general(a, b, (((1,), (1,)), ((), ())), preferred_element_type=F32)


def call(kernel, out_shapes, in_specs, scratch=(), flops=0, **kwargs):
    return pl.pallas_call(
        kernel,
        out_shape=out_shapes,
        in_specs=in_specs,
        out_specs=jax.tree.map(lambda _: VMEM, out_shapes),
        scratch_shapes=list(scratch),
        compiler_params=pltpu.CompilerParams(vmem_limit_bytes=16 * 1024 * 1024),
        cost_estimate=pl.CostEstimate(flops=flops, bytes_accessed=1 << 20, transcendentals=0),
        **kwargs,
    )


def coordinates():
    x, gy, z = (lax.axis_index(axis) for axis in ALL)
    y, core = gy // 2, lax.rem(gy, 2)
    return x, y, core, z


def place_on_ring(x, y, z):
    place = 2 * x + lax.rem(x + y, 2)
    return jnp.where(lax.rem(z, 2) == 0, place, 3 - place)


def upper_half():
    x, y, core, z = coordinates()
    return lax.rem(core + place_on_ring(x, y, z), 2)


def chips():
    x, y, _, z = coordinates()
    for flip in range(4):
        other_x = 1 - x if flip // 2 else x
        other_y = 1 - y if flip % 2 else y
        yield flip, other_x, other_y, place_on_ring(other_x, other_y, z)


def est_kernel(weight, est, *refs):
    pieces, turned = refs[:4], refs[4]
    turned[...] = est[...].T
    rows = lax.broadcasted_iota(jnp.int32, (8, 256), 0)
    weights = jnp.where(
        rows == 0,
        weight[0].astype(F32) * 0.25,
        jnp.where(rows == 1, weight[1].astype(F32) * 0.25, 0.0),
    )
    for flip, _, _, place in chips():
        pieces[flip][0:64, :] = turned[pl.ds(pl.multiple_of(place * 64, 64), 64), :]
        pieces[flip][64:72, :] = weights


def slab_kernel(*refs):
    pieces, (slab, weights, far, near) = refs[:8], refs[8:]
    _, _, core, _ = coordinates()
    upper = upper_half()
    for flip, x, y, _ in chips():
        for turn in range(2):
            piece = pieces[4 * turn + flip]
            column = 4 * x + 2 * y + (core if turn == 0 else 1 - core)
            slab[column] = piece[pl.ds(pl.multiple_of(32 * upper, 32), 32), :]
            weights[column] = piece[64:72, :]
            far[column] = piece[pl.ds(pl.multiple_of(48 * upper, 16), 16), :]
            near[column] = piece[pl.ds(pl.multiple_of(32 - 16 * upper, 16), 16), :]


def lines_kernel(planes, raw, index, out):
    mine = lax.axis_index("gz")
    chunk = lax.broadcasted_iota(jnp.int32, (8, 128), 1) // 32
    rows = lax.broadcasted_iota(jnp.int32, (8, 128), 0)
    for z in range(planes):
        both = jnp.zeros((8, 128), F32)
        for view in range(2):
            parts = []
            for place in range(4):
                block = lax.rem(place - mine + 4, 4)
                start = pl.multiple_of((block * planes + z) * 32, 32)
                parts.append(raw[view, pl.ds(start, 32), :])
                row = index[pl.ds(view * 4 + block, 1), :].astype(F32)
                row = pltpu.roll(jnp.broadcast_to(row, (8, 128)), (32 * (place - z)) % 128, 1)
                both = jnp.where((chunk == place) & (rows == view), row, both)
            turned = jnp.concatenate(parts, axis=0).T
            for device in range(8):
                slab = slab_of(device, z)
                out[device * planes + z, 32 * view : 32 * view + 32, :] = turned[slab * 32 : slab * 32 + 32, :]
        for device in range(8):
            out[device * planes + z, 64:72, :] = both


def taps_kernel(view, psf, big_high, big_low, band, held):
    held[...] = jnp.zeros_like(held)
    held[0:3, 0:33] = psf[:, view, :]
    taps = held[...]
    total = jnp.sum(taps, axis=1, keepdims=True)
    taps = taps / jnp.where(total == 0.0, 1.0, total)

    def toeplitz(row, size):
        wide = jnp.broadcast_to(row, (size, 128))
        return pltpu.roll(wide, 0, 1, stride=1, stride_axis=0)

    lane_r = lax.broadcasted_iota(jnp.int32, (128, 128), 0)
    lane_c = lax.broadcasted_iota(jnp.int32, (128, 128), 1)
    turn = (lane_r + lane_c == 32).astype(BF16)
    pieces = split3(taps)
    reversed_taps = sum(dot_nn(piece, turn) for piece in pieces)
    for way, source in enumerate((taps, reversed_taps)):
        high, low = split2(toeplitz(source[2:3, :], 32))
        twice = high.astype(F32) + pltpu.roll(high.astype(F32), 64, 1)
        band[way, :, 0:128] = twice.astype(BF16)
        band[way, :, 128:256] = low
    tall_x = jnp.broadcast_to(toeplitz(taps[0:1, :], 16)[:, None, :], (16, 16, 128)).reshape(256, 128)
    tall_y = jnp.broadcast_to(toeplitz(taps[1:2, :], 16)[None], (16, 16, 128)).reshape(256, 128)
    from_row = lax.broadcasted_iota(jnp.int32, (128, 256), 0)
    to_lane = lax.broadcasted_iota(jnp.int32, (128, 256), 1)
    wide_x, wide_y = [], []
    for offset in range(3):
        pick_x = (from_row == to_lane // 16 + 16 * offset).astype(BF16)
        pick_y = (from_row == lax.rem(to_lane, 16) + 16 * offset).astype(BF16)
        wide_x.append(sum(dot_nn(piece, pick_x) for piece in split3(tall_x)))
        wide_y.append(sum(dot_nn(piece, pick_y) for piece in split3(tall_y)))
    for dx in range(3):
        for dy in range(3):
            high, low = split2(wide_x[dx] * wide_y[dy])
            big_high[dx * 3 + dy] = high
            big_low[dx * 3 + dy] = low


def scattered(view, slots, weights, column):
    chunk = lax.broadcasted_iota(jnp.int32, (32, 128), 1) // 32
    line = lax.broadcasted_iota(jnp.int32, (256, 512), 0).astype(F32)
    x, block = column // 4, column % 4
    numbers, values = [], []
    for t in range(4):
        tile = jnp.zeros((32, 128), F32)
        number = jnp.zeros((8, 128), F32)
        for place in range(4):
            source = x * 16 + 4 * t + (place - block) % 4
            tile = jnp.where(chunk == place, slots[source, 32 * view : 32 * view + 32, :], tile)
            number = jnp.where(chunk[0:8] == place, slots[source, 64:72, :], number)
        values.append(tile)
        numbers.append(number)
    value = jnp.concatenate(values, axis=1)
    number = jnp.concatenate(numbers, axis=1)[view : view + 1, :]
    hot = (line == number).astype(BF16)
    left = jnp.concatenate([*split3(value), jnp.ones((16, 512), BF16)], axis=0)
    result = dot_nt(left, hot)
    data = result[0:32] + result[32:64] + result[64:96]
    return data, result[96:97] * weights[column, view : view + 1, :]


def scatter_kernel(slots, weights, data, cover):
    for column in range(8):
        data[column], row = scattered(1, slots, weights, column)
        cover[column] = jnp.broadcast_to(row, (8, 256))


def payloads(value, far, near):
    upper = upper_half()
    far[...] = value[:, pl.ds(pl.multiple_of(16 * upper, 16), 16), :]
    near[...] = value[:, pl.ds(pl.multiple_of(16 - 16 * upper, 16), 16), :]


def blurred_into(way, value, far, near, band, big_high, big_low, wide, flat, total):
    upper = upper_half()
    wide[:, 16:48, :] = value[...]
    wide[:, pl.ds(pl.multiple_of(48 * upper, 16), 16), :] = far[...]
    wide[:, pl.ds(pl.multiple_of(48 - 48 * upper, 16), 16), :] = near[...]
    weights = band[way]
    for column in range(8):
        high, low = split2(wide[column])
        stacked = jnp.concatenate([high, low, high, high], axis=0)
        flat[column * 32 : column * 32 + 32, :] = dot_nn(weights, stacked)
    high, low = split2(flat[...])

    def product(start, stop, dx, dy):
        if way == 0:
            at, dot = (dx + 1) * 3 + dy + 1, dot_nt
        else:
            at, dot = (1 - dx) * 3 + 1 - dy, dot_nn
        rows = stop - start
        both = dot(jnp.concatenate([high[start:stop], low[start:stop]], axis=0), big_high[at])
        return both[:rows] + both[rows:] + dot(high[start:stop], big_low[at])

    total[...] = product(0, 256, 0, 0)
    for dx in (-1, 0, 1):
        for dy in (-1, 0, 1):
            if dx == 0 and dy == 0:
                continue
            for x in range(2):
                if not 0 <= x + dx < 2:
                    continue
                first, last = max(0, -dy), min(4, 4 - dy)
                out = (x * 4 + first) * 32, (x * 4 + last) * 32
                shift = (dx * 4 + dy) * 32
                total[out[0] : out[1], :] += product(out[0] + shift, out[1] + shift, dx, dy)


def blur_kernel(est, far, near, band, big_high, big_low, blurred, wide, flat):
    blurred_into(0, est, far, near, band, big_high, big_low, wide, flat, blurred)


def scatter_ratio_kernel(slots, weights, blurred, ratio, far, near):
    for column in range(8):
        data, cover = scattered(0, slots, weights, column)
        ratio[column] = 1.0 + cover * (data / blurred[column * 32 : column * 32 + 32, :] - 1.0)
    payloads(ratio, far, near)


def ratio_kernel(est, far, near, band, big_high, big_low, data, cover, ratio, next_far, next_near, wide, flat, total):
    blurred_into(0, est, far, near, band, big_high, big_low, wide, flat, total)
    for column in range(8):
        blurred = total[column * 32 : column * 32 + 32, :]
        ratio[column] = 1.0 + cover[column, 0:1, :] * (data[column] / blurred - 1.0)
    payloads(ratio, next_far, next_near)


def update_kernel(ratio, far, near, band, big_high, big_low, est, new, next_far, next_near, wide, flat, total):
    blurred_into(1, ratio, far, near, band, big_high, big_low, wide, flat, total)
    for column in range(8):
        new[column] = est[column] * total[column * 32 : column * 32 + 32, :]
    payloads(new, next_far, next_near)


def last_kernel(ratio, far, near, band, big_high, big_low, est, keep, give, wide, flat, total):
    blurred_into(1, ratio, far, near, band, big_high, big_low, wide, flat, total)
    _, _, core, _ = coordinates()
    for flip, x, y, _ in chips():
        for turn, out in enumerate((keep, give)):
            column = 4 * x + 2 * y + (core if turn == 0 else 1 - core)
            start = pl.multiple_of(column * 32, 32)
            out[flip] = est[column] * total[pl.ds(start, 32), :]


def merge_kernel(keep, got, *pieces):
    upper = upper_half()
    for flip in range(4):
        pieces[flip][pl.ds(pl.multiple_of(32 * upper, 32), 32), :] = keep[flip]
        pieces[flip][pl.ds(pl.multiple_of(32 - 32 * upper, 32), 32), :] = got[flip]


def join_kernel(*refs):
    pieces, (out, held) = refs[:4], refs[4:]
    for flip, _, _, place in chips():
        held[pl.ds(pl.multiple_of(64 * place, 64), 64), :] = pieces[flip][...]
    out[...] = held[...].T


def shape(*dims, dtype=F32):
    return jax.ShapeDtypeStruct(dims, dtype)


def swaps(planes):
    def flipped(by):
        return [(d * planes + z, (d ^ by) * planes + z) for d in range(8) for z in range(planes)]

    return [flipped(by) for by in (2, 4, 6)], flipped(1)


def slab_sweep(planes, estimate, raw_lines, line_index, psf, view_weight):
    far_pairs, near_pairs = chain_pairs(planes)
    to_chips, to_core = swaps(planes)

    def exchange(far, near):
        return (
            lax.ppermute(far, ALL, far_pairs),
            lax.ppermute(near, ALL, near_pairs),
        )

    own, *away = call(
        est_kernel, (shape(72, 256),) * 4, [SMEM, VMEM], [pltpu.VMEM((256, 256), F32)]
    )(view_weight.reshape(2), estimate.reshape(256, 256))
    here = [own] + [lax.ppermute(piece, ALL, pairs) for piece, pairs in zip(away, to_chips)]
    there = [lax.ppermute(piece, ALL, to_core) for piece in here]

    slots = call(functools.partial(lines_kernel, planes), shape(8 * planes, 72, 128), [VMEM, VMEM])(
        raw_lines.reshape(2, 4 * planes * 32, 256), line_index.reshape(8, 128)
    )
    slots = lax.all_to_all(slots, ALL, split_axis=0, concat_axis=0, tiled=True)
    half, full = shape(8, 16, 256), shape(8, 32, 256)
    work = [pltpu.VMEM((8, 64, 256), F32), pltpu.VMEM((256, 256), F32)]
    total = pltpu.VMEM((256, 256), F32)
    est, weights, far, near = call(slab_kernel, (full, shape(8, 8, 256), half, half), [VMEM] * 8)(
        *here, *there
    )
    far = lax.ppermute(far, ALL, far_pairs)
    mats = []
    for view in range(2):
        big_high, big_low, band = call(
            functools.partial(taps_kernel, view),
            (shape(9, 256, 256, dtype=BF16), shape(9, 256, 256, dtype=BF16), shape(2, 32, 256, dtype=BF16)),
            [VMEM],
            [pltpu.VMEM((8, 128), F32)],
            flops=1 << 30,
        )(psf.transpose(1, 0, 2))
        mats.append((band, big_high, big_low))
    blurred = call(blur_kernel, shape(256, 256), [VMEM] * 6, work, flops=1 << 30)(est, far, near, *mats[0])
    ratio, far, near = call(scatter_ratio_kernel, (full, half, half), [VMEM] * 3, flops=1 << 30)(
        slots, weights, blurred
    )
    est, far, near = call(update_kernel, (full, half, half), [VMEM] * 7, work + [total], flops=1 << 30)(
        ratio, *exchange(far, near), *mats[0], est
    )
    data, cover = call(scatter_kernel, (full, shape(8, 8, 256)), [VMEM] * 2, flops=1 << 30)(
        slots, weights
    )
    ratio, far, near = call(ratio_kernel, (full, half, half), [VMEM] * 8, work + [total], flops=1 << 30)(
        est, *exchange(far, near), *mats[1], data, cover
    )
    quarter = shape(4, 32, 256)
    keep, give = call(last_kernel, (quarter, quarter), [VMEM] * 7, work + [total], flops=1 << 30)(
        ratio, *exchange(far, near), *mats[1], est
    )
    got = lax.ppermute(give, ALL, to_core)
    own, *away = call(merge_kernel, (shape(64, 256),) * 4, [VMEM] * 2)(keep, got)
    parts = [own] + [lax.ppermute(piece, ALL, pairs) for piece, pairs in zip(away, to_chips)]
    out = call(join_kernel, shape(256, 256), [VMEM] * 4, [pltpu.VMEM((256, 256), F32)])(*parts)
    return out.reshape(16, 16, 256)


def padded(block, sides, width):
    for axis, dim in sides:
        count = lax.axis_size(axis)
        forward = [(i, i + 1) for i in range(count - 1)]
        backward = [(target, source) for source, target in forward]
        low = lax.ppermute(
            lax.slice_in_dim(block, block.shape[dim] - width, None, axis=dim), axis, forward
        )
        high = lax.ppermute(lax.slice_in_dim(block, 0, width, axis=dim), axis, backward)
        block = jnp.concatenate([low, block, high], axis=dim)
    return block


def band_matrix(taps, length):
    width = taps.shape[0]
    rows = lax.broadcasted_iota(jnp.int32, (length + width - 1, length), 0)
    cols = lax.broadcasted_iota(jnp.int32, (length + width - 1, length), 1)
    offset = rows - cols
    valid = (offset >= 0) & (offset < width)
    return jnp.where(valid, taps[jnp.clip(offset, 0, width - 1)], 0.0)


def along_x(extended, matrix_x):
    lead, size_y, size_z = extended.shape
    flat = extended.reshape(lead, size_y * size_z)
    result = jnp.dot(matrix_x.T, flat, precision=lax.Precision.HIGHEST)
    return result.reshape(matrix_x.shape[1], size_y, size_z)


def blur(field, taps):
    half_width = (taps.shape[1] - 1) // 2
    size_x, size_y, size_z = field.shape
    matrix_x = band_matrix(taps[0], size_x)
    matrix_y = band_matrix(taps[1], size_y)
    matrix_z = band_matrix(taps[2], size_z)
    highest = lax.Precision.HIGHEST
    extended = padded(field, (("gz", 2),), half_width)
    result = jnp.einsum("abj,jc->abc", extended, matrix_z, precision=highest)
    extended = padded(result, (("gy", 1),), half_width)
    result = jnp.einsum("ajc,jb->abc", extended, matrix_y, precision=highest)
    extended = padded(result, (("gx", 0),), half_width)
    result = along_x(extended, matrix_x)
    return result


def block_sweep(estimate, raw_lines, line_index, psf, view_weight):
    size_x, size_y, size_z = estimate.shape
    block_lines = size_x * size_y
    views = raw_lines.shape[0]
    group = lax.axis_size(("gy", "gz"))
    slots = line_index.shape[-1]
    capacity = slots // group
    lines = raw_lines.reshape(views, group, capacity, size_z)
    indices = line_index.reshape(views, group, capacity)
    lines, indices = (
        lax.all_to_all(lines, ("gy", "gz"), split_axis=1, concat_axis=1, tiled=True),
        lax.all_to_all(indices, ("gy", "gz"), split_axis=1, concat_axis=1, tiled=True),
    )
    est = estimate
    for view in range(views):
        flat_index = indices[view].reshape(-1)
        flat_lines = lines[view].reshape(-1, size_z)
        volume = (
            jnp.zeros((block_lines, size_z), jnp.float32)
            .at[flat_index]
            .set(flat_lines, mode="drop")
        )
        volume = volume.reshape(size_x, size_y, size_z)
        cover = jnp.zeros((block_lines,), jnp.float32).at[flat_index].set(1.0, mode="drop")
        cover = cover.reshape(size_x, size_y, 1)
        weight = view_weight[view].reshape(()).astype(jnp.float32) * 0.25
        taps = psf[view] / jnp.sum(psf[view], axis=1, keepdims=True)
        blurred = blur(est, taps)
        ratio = 1.0 + weight * cover * (volume / blurred - 1.0)
        est = est * blur(ratio, taps[:, ::-1])
    return est


def solution(mesh):
    placed = (
        P("gx", "gy", "gz"),
        P(None, "gx", ("gy", "gz"), None, None),
        P(None, "gx", ("gy", "gz"), None),
        P(),
        P(None, "gx", "gy", "gz"),
    )
    sizes = tuple(mesh.shape[axis] for axis in ALL)

    def on_device(estimate, raw_lines, line_index, psf, view_weight):
        capacity = line_index.shape[-1] // (sizes[1] * sizes[2])
        fits = (
            sizes == (2, 4, 4)
            and estimate.shape == (16, 16, 256)
            and raw_lines.shape[0] == 2
            and capacity == 32
            and psf.shape == (2, 3, 33)
        )
        plan = functools.partial(slab_sweep, sizes[2]) if fits else block_sweep
        return plan(estimate, raw_lines, line_index, psf, view_weight)

    return jax.shard_map(
        on_device, mesh=mesh, in_specs=placed, out_specs=P("gx", "gy", "gz"), check_vma=False
    )
```

```python
import functools

import jax
import jax.numpy as jnp
from jax import lax
from jax.experimental import pallas as pl
from jax.experimental.pallas import tpu as pltpu
from jax.sharding import PartitionSpec as P

F32, BF16 = jnp.float32, jnp.bfloat16
VMEM = pl.BlockSpec(memory_space=pltpu.VMEM)
SMEM = pl.BlockSpec(memory_space=pltpu.SMEM)
ALL = ("gx", "gy", "gz")


def ring_place(x, y, z):
    place = 2 * x + (x ^ y)
    return place if z % 2 == 0 else 3 - place


def slab_of(device, z):
    x, gy = device // 4, device % 4
    place = ring_place(x, gy // 2, z)
    return 2 * place + ((gy % 2) ^ (place % 2))


def chain_pairs(planes):
    order = []
    for z in range(planes):
        by_slab = sorted(range(8), key=lambda device: slab_of(device, z))
        order += [device * planes + z for device in by_slab]
    far, near = [], []
    for k in range(len(order) - 1):
        pair = (order[k], order[k + 1])
        (near if k % 2 == 0 else far).extend([pair, pair[::-1]])
    return far, near


def split2(value):
    high = value.astype(BF16)
    return high, (value - high.astype(F32)).astype(BF16)


def split3(value):
    high = value.astype(BF16)
    rest = value - high.astype(F32)
    middle = rest.astype(BF16)
    return high, middle, (rest - middle.astype(F32)).astype(BF16)


def dot_nn(a, b):
    return lax.dot_general(a, b, (((1,), (0,)), ((), ())), preferred_element_type=F32)


def dot_nt(a, b):
    return lax.dot_general(a, b, (((1,), (1,)), ((), ())), preferred_element_type=F32)


def call(kernel, out_shapes, in_specs, scratch=(), flops=0, **kwargs):
    return pl.pallas_call(
        kernel,
        out_shape=out_shapes,
        in_specs=in_specs,
        out_specs=jax.tree.map(lambda _: VMEM, out_shapes),
        scratch_shapes=list(scratch),
        compiler_params=pltpu.CompilerParams(vmem_limit_bytes=16 * 1024 * 1024),
        cost_estimate=pl.CostEstimate(flops=flops, bytes_accessed=1 << 20, transcendentals=0),
        **kwargs,
    )


def coordinates():
    x, gy, z = (lax.axis_index(axis) for axis in ALL)
    y, core = gy // 2, lax.rem(gy, 2)
    return x, y, core, z


def place_on_ring(x, y, z):
    place = 2 * x + lax.rem(x + y, 2)
    return jnp.where(lax.rem(z, 2) == 0, place, 3 - place)


def upper_half():
    x, y, core, z = coordinates()
    return lax.rem(core + place_on_ring(x, y, z), 2)


def chips():
    x, y, _, z = coordinates()
    for flip in range(4):
        other_x = 1 - x if flip // 2 else x
        other_y = 1 - y if flip % 2 else y
        yield flip, other_x, other_y, place_on_ring(other_x, other_y, z)


def est_kernel(weight, est, *refs):
    pieces, turned = refs[:4], refs[4]
    turned[...] = est[...].T
    rows = lax.broadcasted_iota(jnp.int32, (8, 256), 0)
    weights = jnp.where(
        rows == 0,
        weight[0].astype(F32) * 0.25,
        jnp.where(rows == 1, weight[1].astype(F32) * 0.25, 0.0),
    )
    for flip, _, _, place in chips():
        pieces[flip][0:64, :] = turned[pl.ds(pl.multiple_of(place * 64, 64), 64), :]
        pieces[flip][64:72, :] = weights


def slab_kernel(*refs):
    pieces, (slab, weights, far, near) = refs[:8], refs[8:]
    _, _, core, _ = coordinates()
    upper = upper_half()
    for flip, x, y, _ in chips():
        for turn in range(2):
            piece = pieces[4 * turn + flip]
            column = 4 * x + 2 * y + (core if turn == 0 else 1 - core)
            slab[column] = piece[pl.ds(pl.multiple_of(32 * upper, 32), 32), :]
            weights[column] = piece[64:72, :]
            far[column] = piece[pl.ds(pl.multiple_of(48 * upper, 16), 16), :]
            near[column] = piece[pl.ds(pl.multiple_of(32 - 16 * upper, 16), 16), :]


def lines_kernel(planes, raw, index, out):
    mine = lax.axis_index("gz")
    chunk = lax.broadcasted_iota(jnp.int32, (8, 128), 1) // 32
    rows = lax.broadcasted_iota(jnp.int32, (8, 128), 0)
    for z in range(planes):
        both = jnp.zeros((8, 128), F32)
        for view in range(2):
            parts = []
            for place in range(4):
                block = lax.rem(place - mine + 4, 4)
                start = pl.multiple_of((block * planes + z) * 32, 32)
                parts.append(raw[view, pl.ds(start, 32), :])
                row = index[pl.ds(view * 4 + block, 1), :].astype(F32)
                row = pltpu.roll(jnp.broadcast_to(row, (8, 128)), (32 * (place - z)) % 128, 1)
                both = jnp.where((chunk == place) & (rows == view), row, both)
            turned = jnp.concatenate(parts, axis=0).T
            for device in range(8):
                slab = slab_of(device, z)
                out[device * planes + z, 32 * view : 32 * view + 32, :] = turned[slab * 32 : slab * 32 + 32, :]
        for device in range(8):
            out[device * planes + z, 64:72, :] = both


def taps_kernel(view, way, psf, _, big_high, big_low, band, held):
    held[...] = jnp.zeros_like(held)
    held[0:3, 0:33] = psf[:, view, :]
    taps = held[...]
    total = jnp.sum(taps, axis=1, keepdims=True)
    taps = taps / jnp.where(total == 0.0, 1.0, total)

    def toeplitz(row, size):
        wide = jnp.broadcast_to(row, (size, 128))
        return pltpu.roll(wide, 0, 1, stride=1, stride_axis=0)

    from_lane = lax.broadcasted_iota(jnp.int32, (128, 128), 0)
    to_lane = lax.broadcasted_iota(jnp.int32, (128, 128), 1)
    turn = (from_lane + to_lane == 32).astype(BF16)
    turned = sum(dot_nn(piece, turn) for piece in split3(taps))
    along_z, along_xy = (taps, turned) if way == 0 else (turned, taps)
    high, low = split2(toeplitz(along_z[2:3, :], 32))
    twice = high.astype(F32) + pltpu.roll(high.astype(F32), 64, 1)
    band[:, 0:128] = twice.astype(BF16)
    band[:, 128:256] = low
    tall_x = jnp.broadcast_to(toeplitz(along_xy[0:1, :], 16)[:, None, :], (16, 16, 128)).reshape(256, 128)
    tall_y = jnp.broadcast_to(toeplitz(along_xy[1:2, :], 16)[None], (16, 16, 128)).reshape(256, 128)
    from_row = lax.broadcasted_iota(jnp.int32, (128, 256), 0)
    to_lane = lax.broadcasted_iota(jnp.int32, (128, 256), 1)
    wide_x, wide_y = [], []
    for offset in range(3):
        pick_x = (from_row == to_lane // 16 + 16 * offset).astype(BF16)
        pick_y = (from_row == lax.rem(to_lane, 16) + 16 * offset).astype(BF16)
        wide_x.append(sum(dot_nn(piece, pick_x) for piece in split3(tall_x)))
        wide_y.append(sum(dot_nn(piece, pick_y) for piece in split3(tall_y)))
    for dx in range(3):
        for dy in range(3):
            high, low = split2(wide_x[dx] * wide_y[dy])
            big_high[8 - dx * 3 - dy] = high
            big_low[8 - dx * 3 - dy] = low


def scattered(view, slots, weights, column):
    chunk = lax.broadcasted_iota(jnp.int32, (32, 128), 1) // 32
    line = lax.broadcasted_iota(jnp.int32, (256, 512), 0).astype(F32)
    x, block = column // 4, column % 4
    numbers, values = [], []
    for t in range(4):
        tile = jnp.zeros((32, 128), F32)
        number = jnp.zeros((8, 128), F32)
        for place in range(4):
            source = x * 16 + 4 * t + (place - block) % 4
            tile = jnp.where(chunk == place, slots[source, 32 * view : 32 * view + 32, :], tile)
            number = jnp.where(chunk[0:8] == place, slots[source, 64:72, :], number)
        values.append(tile)
        numbers.append(number)
    value = jnp.concatenate(values, axis=1)
    number = jnp.concatenate(numbers, axis=1)[view : view + 1, :]
    hot = (line == number).astype(BF16)
    left = jnp.concatenate([*split3(value), jnp.ones((16, 512), BF16)], axis=0)
    result = dot_nt(left, hot)
    data = result[0:32] + result[32:64] + result[64:96]
    return data, result[96:97] * weights[column, view : view + 1, :]


def scatter_kernel(slots, weights, data, cover):
    for column in range(8):
        data[column], row = scattered(1, slots, weights, column)
        cover[column] = jnp.broadcast_to(row, (8, 256))


def payloads(value, far, near):
    upper = upper_half()
    far[...] = value[:, pl.ds(pl.multiple_of(16 * upper, 16), 16), :]
    near[...] = value[:, pl.ds(pl.multiple_of(16 - 16 * upper, 16), 16), :]


def widened(wide, value, far, near, margin):
    rows, upper = value.shape[1], upper_half()
    wide[:, margin : margin + rows, :] = value[...]
    side = margin + rows
    wide[:, pl.ds(pl.multiple_of(side * upper, 16), margin), :] = far[...]
    wide[:, pl.ds(pl.multiple_of(side - side * upper, 16), margin), :] = near[...]


def blurred_into(wide, band, big_high, big_low, flat, total):
    rows = wide.shape[1] - 32
    weights = band[...]
    for column in range(8):
        for start in range(0, rows, 32):
            high, low = split2(wide[column, start : start + 64, :])
            stacked = jnp.concatenate([high, low, high, high], axis=0)
            at = column * rows + start
            flat[at : at + 32, :] = dot_nn(weights, stacked)
    high, low = split2(flat[...])

    def product(start, stop, dx, dy):
        at = (dx + 1) * 3 + dy + 1
        size = stop - start
        both = dot_nn(jnp.concatenate([high[start:stop], low[start:stop]], axis=0), big_high[at])
        return both[:size] + both[size:] + dot_nn(high[start:stop], big_low[at])

    total[...] = product(0, 8 * rows, 0, 0)
    for dx in (-1, 0, 1):
        for dy in (-1, 0, 1):
            if dx == 0 and dy == 0:
                continue
            for x in range(2):
                if not 0 <= x + dx < 2:
                    continue
                first, last = max(0, -dy), min(4, 4 - dy)
                start, stop = (x * 4 + first) * rows, (x * 4 + last) * rows
                shift = (dx * 4 + dy) * rows
                total[start:stop, :] += product(start + shift, stop + shift, dx, dy)


def blur_kernel(est, far, near, band, big_high, big_low, blurred, wide, flat):
    widened(wide, est, far, near, 16)
    blurred_into(wide, band, big_high, big_low, flat, blurred)


def ratio_from(ratio, data, cover, blurred):
    for column in range(8):
        here = blurred[column * 32 : column * 32 + 32, :]
        ratio[column] = 1.0 + cover[column, 0:1, :] * (data[column] / here - 1.0)


def scatter_ratio_kernel(slots, weights, blurred, ratio):
    for column in range(8):
        data, cover = scattered(0, slots, weights, column)
        ratio[column] = 1.0 + cover * (data / blurred[column * 32 : column * 32 + 32, :] - 1.0)


def middle_kernel(
    ratio, ratio_far, ratio_near, est, est_far, est_near, band0, high0, low0, band1, high1, low1,
    data, cover, new, next_ratio, far, near, wide, tall, flat, total, short,
):
    widened(wide, ratio, ratio_far, ratio_near, 32)
    widened(tall, est, est_far, est_near, 16)
    blurred_into(wide, band0, high0, low0, flat, total)
    for column in range(8):
        tall[column] = tall[column] * total[column * 64 : column * 64 + 64, :]
    new[...] = tall[:, 16:48, :]
    out = total.at[0:256, :]
    blurred_into(tall, band1, high1, low1, short, out)
    ratio_from(next_ratio, data, cover, out)
    payloads(next_ratio, far, near)


def last_kernel(ratio, far, near, band, big_high, big_low, est, keep, give, wide, flat, total):
    widened(wide, ratio, far, near, 16)
    blurred_into(wide, band, big_high, big_low, flat, total)
    _, _, core, _ = coordinates()
    for flip, x, y, _ in chips():
        for turn, out in enumerate((keep, give)):
            column = 4 * x + 2 * y + (core if turn == 0 else 1 - core)
            start = pl.multiple_of(column * 32, 32)
            out[flip] = est[column] * total[pl.ds(start, 32), :]


def merge_kernel(keep, got, *pieces):
    upper = upper_half()
    for flip in range(4):
        pieces[flip][pl.ds(pl.multiple_of(32 * upper, 32), 32), :] = keep[flip]
        pieces[flip][pl.ds(pl.multiple_of(32 - 32 * upper, 32), 32), :] = got[flip]


def join_kernel(*refs):
    pieces, (out, held) = refs[:4], refs[4:]
    for flip, _, _, place in chips():
        held[pl.ds(pl.multiple_of(64 * place, 64), 64), :] = pieces[flip][...]
    out[...] = held[...].T


def shape(*dims, dtype=F32):
    return jax.ShapeDtypeStruct(dims, dtype)


def swaps(planes):
    def flipped(by):
        return [(d * planes + z, (d ^ by) * planes + z) for d in range(8) for z in range(planes)]

    return [flipped(by) for by in (2, 4, 6)], flipped(1)


def slab_sweep(planes, estimate, raw_lines, line_index, psf, view_weight):
    far_pairs, near_pairs = chain_pairs(planes)
    to_chips, to_core = swaps(planes)

    def exchange(far, near):
        return (
            lax.ppermute(far, ALL, far_pairs),
            lax.ppermute(near, ALL, near_pairs),
        )

    own, *away = call(
        est_kernel, (shape(72, 256),) * 4, [SMEM, VMEM], [pltpu.VMEM((256, 256), F32)]
    )(view_weight.reshape(2), estimate.reshape(256, 256))
    here = [own] + [lax.ppermute(piece, ALL, pairs) for piece, pairs in zip(away, to_chips)]
    there = [lax.ppermute(piece, ALL, to_core) for piece in here]

    slots = call(functools.partial(lines_kernel, planes), shape(8 * planes, 72, 128), [VMEM, VMEM])(
        raw_lines.reshape(2, 4 * planes * 32, 256), line_index.reshape(8, 128)
    )
    slots = lax.all_to_all(slots, ALL, split_axis=0, concat_axis=0, tiled=True)
    half, full = shape(8, 16, 256), shape(8, 32, 256)

    def work(*dims):
        return pltpu.VMEM(dims, F32)

    est, weights, est_far, est_near = call(slab_kernel, (full, shape(8, 8, 256), half, half), [VMEM] * 8)(
        *here, *there
    )
    est_far = lax.ppermute(est_far, ALL, far_pairs)
    anywhere = pl.BlockSpec(memory_space=pl.ANY)

    def matrices(view, way, after):
        big = shape(9, 256, 256, dtype=BF16)
        big_high, big_low, band = call(
            functools.partial(taps_kernel, view, way),
            (big, big, shape(32, 256, dtype=BF16)),
            [VMEM, anywhere],
            [work(8, 128)],
            flops=1 << 30,
        )(psf.transpose(1, 0, 2), after)
        return band, big_high, big_low

    blurred = call(
        blur_kernel, shape(256, 256), [VMEM] * 6, [work(8, 64, 256), work(256, 256)], flops=1 << 30
    )(est, est_far, est_near, *matrices(0, 0, est))
    ratio = call(scatter_ratio_kernel, full, [VMEM] * 3, flops=1 << 30)(slots, weights, blurred)
    data, cover = call(scatter_kernel, (full, shape(8, 8, 256)), [VMEM] * 2, flops=1 << 30)(slots, weights)
    est, ratio, far, near = call(
        middle_kernel,
        (full, full, half, half),
        [VMEM] * 14,
        [work(8, 96, 256), work(8, 64, 256), work(512, 256), work(512, 256), work(256, 256)],
        flops=1 << 30,
    )(ratio, *exchange(ratio, ratio), est, est_far, est_near, *matrices(0, 1, slots), *matrices(1, 0, slots), data, cover)
    quarter = shape(4, 32, 256)
    keep, give = call(
        last_kernel,
        (quarter, quarter),
        [VMEM] * 7,
        [work(8, 64, 256), work(256, 256), work(256, 256)],
        flops=1 << 30,
    )(ratio, *exchange(far, near), *matrices(1, 1, ratio), est)
    got = lax.ppermute(give, ALL, to_core)
    own, *away = call(merge_kernel, (shape(64, 256),) * 4, [VMEM] * 2)(keep, got)
    parts = [own] + [lax.ppermute(piece, ALL, pairs) for piece, pairs in zip(away, to_chips)]
    out = call(join_kernel, shape(256, 256), [VMEM] * 4, [pltpu.VMEM((256, 256), F32)])(*parts)
    return out.reshape(16, 16, 256)


def padded(block, sides, width):
    for axis, dim in sides:
        count = lax.axis_size(axis)
        forward = [(i, i + 1) for i in range(count - 1)]
        backward = [(target, source) for source, target in forward]
        low = lax.ppermute(
            lax.slice_in_dim(block, block.shape[dim] - width, None, axis=dim), axis, forward
        )
        high = lax.ppermute(lax.slice_in_dim(block, 0, width, axis=dim), axis, backward)
        block = jnp.concatenate([low, block, high], axis=dim)
    return block


def band_matrix(taps, length):
    width = taps.shape[0]
    rows = lax.broadcasted_iota(jnp.int32, (length + width - 1, length), 0)
    cols = lax.broadcasted_iota(jnp.int32, (length + width - 1, length), 1)
    offset = rows - cols
    valid = (offset >= 0) & (offset < width)
    return jnp.where(valid, taps[jnp.clip(offset, 0, width - 1)], 0.0)


def along_x(extended, matrix_x):
    lead, size_y, size_z = extended.shape
    flat = extended.reshape(lead, size_y * size_z)
    result = jnp.dot(matrix_x.T, flat, precision=lax.Precision.HIGHEST)
    return result.reshape(matrix_x.shape[1], size_y, size_z)


def blur(field, taps):
    half_width = (taps.shape[1] - 1) // 2
    size_x, size_y, size_z = field.shape
    matrix_x = band_matrix(taps[0], size_x)
    matrix_y = band_matrix(taps[1], size_y)
    matrix_z = band_matrix(taps[2], size_z)
    highest = lax.Precision.HIGHEST
    extended = padded(field, (("gz", 2),), half_width)
    result = jnp.einsum("abj,jc->abc", extended, matrix_z, precision=highest)
    extended = padded(result, (("gy", 1),), half_width)
    result = jnp.einsum("ajc,jb->abc", extended, matrix_y, precision=highest)
    extended = padded(result, (("gx", 0),), half_width)
    result = along_x(extended, matrix_x)
    return result


def block_sweep(estimate, raw_lines, line_index, psf, view_weight):
    size_x, size_y, size_z = estimate.shape
    block_lines = size_x * size_y
    views = raw_lines.shape[0]
    group = lax.axis_size(("gy", "gz"))
    slots = line_index.shape[-1]
    capacity = slots // group
    lines = raw_lines.reshape(views, group, capacity, size_z)
    indices = line_index.reshape(views, group, capacity)
    lines, indices = (
        lax.all_to_all(lines, ("gy", "gz"), split_axis=1, concat_axis=1, tiled=True),
        lax.all_to_all(indices, ("gy", "gz"), split_axis=1, concat_axis=1, tiled=True),
    )
    est = estimate
    for view in range(views):
        flat_index = indices[view].reshape(-1)
        flat_lines = lines[view].reshape(-1, size_z)
        volume = (
            jnp.zeros((block_lines, size_z), jnp.float32)
            .at[flat_index]
            .set(flat_lines, mode="drop")
        )
        volume = volume.reshape(size_x, size_y, size_z)
        cover = jnp.zeros((block_lines,), jnp.float32).at[flat_index].set(1.0, mode="drop")
        cover = cover.reshape(size_x, size_y, 1)
        weight = view_weight[view].reshape(()).astype(jnp.float32) * 0.25
        taps = psf[view] / jnp.sum(psf[view], axis=1, keepdims=True)
        blurred = blur(est, taps)
        ratio = 1.0 + weight * cover * (volume / blurred - 1.0)
        est = est * blur(ratio, taps[:, ::-1])
    return est


def solution(mesh):
    placed = (
        P("gx", "gy", "gz"),
        P(None, "gx", ("gy", "gz"), None, None),
        P(None, "gx", ("gy", "gz"), None),
        P(),
        P(None, "gx", "gy", "gz"),
    )
    sizes = tuple(mesh.shape[axis] for axis in ALL)

    def on_device(estimate, raw_lines, line_index, psf, view_weight):
        capacity = line_index.shape[-1] // (sizes[1] * sizes[2])
        fits = (
            sizes == (2, 4, 4)
            and estimate.shape == (16, 16, 256)
            and raw_lines.shape[0] == 2
            and capacity == 32
            and psf.shape == (2, 3, 33)
        )
        plan = functools.partial(slab_sweep, sizes[2]) if fits else block_sweep
        return plan(estimate, raw_lines, line_index, psf, view_weight)

    return jax.shard_map(
        on_device, mesh=mesh, in_specs=placed, out_specs=P("gx", "gy", "gz"), check_vma=False
    )
```

```python
import functools

import jax
import jax.numpy as jnp
from jax import lax
from jax.experimental import pallas as pl
from jax.experimental.pallas import tpu as pltpu
from jax.sharding import PartitionSpec as P

F32, BF16 = jnp.float32, jnp.bfloat16
VMEM = pl.BlockSpec(memory_space=pltpu.VMEM)
SMEM = pl.BlockSpec(memory_space=pltpu.SMEM)
ALL = ("gx", "gy", "gz")


def ring_place(x, y, z):
    place = 2 * x + (x ^ y)
    return place if z % 2 == 0 else 3 - place


def slab_of(device, z):
    x, gy = device // 4, device % 4
    place = ring_place(x, gy // 2, z)
    return 2 * place + gy % 2


def chain_pairs(planes):
    order = []
    for z in range(planes):
        by_slab = sorted(range(8), key=lambda device: slab_of(device, z))
        order += [device * planes + z for device in by_slab]
    far, near = [], []
    for k in range(len(order) - 1):
        pair = (order[k], order[k + 1])
        (near if k % 2 == 0 else far).extend([pair, pair[::-1]])
    return far, near


def split2(value):
    high = value.astype(BF16)
    return high, (value - high.astype(F32)).astype(BF16)


def split3(value):
    high = value.astype(BF16)
    rest = value - high.astype(F32)
    middle = rest.astype(BF16)
    return high, middle, (rest - middle.astype(F32)).astype(BF16)


def dot_nn(a, b):
    return lax.dot_general(a, b, (((1,), (0,)), ((), ())), preferred_element_type=F32)


def dot_nt(a, b):
    return lax.dot_general(a, b, (((1,), (1,)), ((), ())), preferred_element_type=F32)


def call(kernel, out_shapes, in_specs, scratch=(), flops=0, out_specs=None, vmem=16):
    return pl.pallas_call(
        kernel,
        out_shape=out_shapes,
        in_specs=in_specs,
        out_specs=out_specs or jax.tree.map(lambda _: VMEM, out_shapes),
        scratch_shapes=list(scratch),
        compiler_params=pltpu.CompilerParams(vmem_limit_bytes=vmem * 1024 * 1024),
        cost_estimate=pl.CostEstimate(flops=flops, bytes_accessed=1 << 20, transcendentals=0),
    )


def coordinates():
    x, gy, z = (lax.axis_index(axis) for axis in ALL)
    y, core = gy // 2, lax.rem(gy, 2)
    return x, y, core, z


def place_on_ring(x, y, z):
    place = 2 * x + lax.rem(x + y, 2)
    return jnp.where(lax.rem(z, 2) == 0, place, 3 - place)


def upper_half():
    return coordinates()[2]


def chips():
    x, y, _, z = coordinates()
    for flip in range(4):
        other_x = 1 - x if flip // 2 else x
        other_y = 1 - y if flip % 2 else y
        yield flip, other_x, other_y, place_on_ring(other_x, other_y, z)


def est_kernel(weight, est, *refs):
    pieces, turned = refs[:4], refs[4]
    turned[...] = est[...].T
    rows = lax.broadcasted_iota(jnp.int32, (8, 256), 0)
    weights = jnp.where(
        rows == 0,
        weight[0].astype(F32) * 0.25,
        jnp.where(rows == 1, weight[1].astype(F32) * 0.25, 0.0),
    )
    for flip, _, _, place in chips():
        pieces[flip][0:64, :] = turned[pl.ds(pl.multiple_of(place * 64, 64), 64), :]
        pieces[flip][64:72, :] = weights


def slab_kernel(*refs):
    pieces, (slab, weights, far, near) = refs[:8], refs[8:]
    _, _, core, _ = coordinates()
    upper = upper_half()
    for flip, x, y, _ in chips():
        for turn in range(2):
            piece = pieces[4 * turn + flip]
            column = 4 * x + 2 * y + (core if turn == 0 else 1 - core)
            slab[column] = piece[pl.ds(pl.multiple_of(32 * upper, 32), 32), :]
            weights[column] = piece[64:72, :]
            far[column] = piece[pl.ds(pl.multiple_of(48 * upper, 16), 16), :]
            near[column] = piece[pl.ds(pl.multiple_of(32 - 16 * upper, 16), 16), :]


def lines_kernel(planes, raw, index, out, held, numbers, made, arrived, numbered, left):
    mine = lax.axis_index("gz")
    blocks = [lax.rem(place - mine + 4, 4) for place in range(4)]
    chunk = lax.broadcasted_iota(jnp.int32, (8, 128), 1) // 32
    rows = lax.broadcasted_iota(jnp.int32, (8, 128), 0)

    def load(z):
        return pltpu.make_async_copy(raw.at[:, :, z], held.at[z], arrived.at[z])

    def store(z):
        return pltpu.make_async_copy(made.at[z], out.at[:, z], left.at[z])

    load_numbers = pltpu.make_async_copy(index, numbers, numbered.at[0])
    for z in range(planes):
        load(z).start()
    load_numbers.start()
    for z in range(planes):
        load(z).wait()
        for view in range(2):
            lines = jnp.concatenate([held[z, view, block] for block in blocks], axis=0)
            turned = lines.T
            for device in range(8):
                slab = slab_of(device, z)
                made[z, device, 32 * view : 32 * view + 32, :] = turned[slab * 32 : slab * 32 + 32, :]
        if z == 0:
            load_numbers.wait()
        both = jnp.zeros((8, 128), F32)
        for place, block in enumerate(blocks):
            for view in range(2):
                row = numbers[pl.ds(view * 4 + block, 1), :].astype(F32)
                row = pltpu.roll(jnp.broadcast_to(row, (8, 128)), (32 * (place - z)) % 128, 1)
                both = jnp.where((chunk == place) & (rows == view), row, both)
        for device in range(8):
            made[z, device, 64:72, :] = both
        store(z).start()
    for z in range(planes):
        store(z).wait()


def taps_kernel(view, way, psf, _, big_high, big_low, band, held):
    held[...] = jnp.zeros_like(held)
    held[0:3, 0:33] = psf[:, view, :]
    taps = held[...]
    total = jnp.sum(taps, axis=1, keepdims=True)
    taps = taps / jnp.where(total == 0.0, 1.0, total)

    def toeplitz(row, size):
        wide = jnp.broadcast_to(row, (size, 128))
        return pltpu.roll(wide, 0, 1, stride=1, stride_axis=0)

    from_lane = lax.broadcasted_iota(jnp.int32, (128, 128), 0)
    to_lane = lax.broadcasted_iota(jnp.int32, (128, 128), 1)
    turn = (from_lane + to_lane == 32).astype(BF16)
    turned = sum(dot_nn(piece, turn) for piece in split3(taps))
    along_z, along_xy = (taps, turned) if way == 0 else (turned, taps)
    high, low = (part.astype(F32) for part in split2(toeplitz(along_z[2:3, :], 32)))
    band[0:32, :] = (high + pltpu.roll(high, 64, 1)).astype(BF16)
    band[32:64, :] = low.astype(BF16)
    tall_x = jnp.broadcast_to(toeplitz(along_xy[0:1, :], 16)[:, None, :], (16, 16, 128)).reshape(256, 128)
    tall_y = jnp.broadcast_to(toeplitz(along_xy[1:2, :], 16)[None], (16, 16, 128)).reshape(256, 128)
    from_row = lax.broadcasted_iota(jnp.int32, (128, 256), 0)
    to_lane = lax.broadcasted_iota(jnp.int32, (128, 256), 1)
    wide_x, wide_y = [], []
    for offset in range(3):
        pick_x = (from_row == to_lane // 16 + 16 * offset).astype(BF16)
        pick_y = (from_row == lax.rem(to_lane, 16) + 16 * offset).astype(BF16)
        wide_x.append(sum(dot_nn(piece, pick_x) for piece in split3(tall_x)))
        wide_y.append(sum(dot_nn(piece, pick_y) for piece in split3(tall_y)))
    for dx in range(3):
        for dy in range(3):
            high, low = split2(wide_x[dx] * wide_y[dy])
            big_high[8 - dx * 3 - dy] = high
            big_low[8 - dx * 3 - dy] = low


def scattered(view, slots, weights, column):
    chunk = lax.broadcasted_iota(jnp.int32, (32, 128), 1) // 32
    line = lax.broadcasted_iota(jnp.int32, (256, 512), 0).astype(F32)
    x, block = column // 4, column % 4
    numbers, values = [], []
    for t in range(4):
        tile = jnp.zeros((32, 128), F32)
        number = jnp.zeros((8, 128), F32)
        for place in range(4):
            source = x * 16 + 4 * t + (place - block) % 4
            tile = jnp.where(chunk == place, slots[source, 32 * view : 32 * view + 32, :], tile)
            number = jnp.where(chunk[0:8] == place, slots[source, 64:72, :], number)
        values.append(tile)
        numbers.append(number)
    value = jnp.concatenate(values, axis=1)
    number = jnp.concatenate(numbers, axis=1)[view : view + 1, :]
    hot = (line == number).astype(BF16)
    left = jnp.concatenate([*split3(value), jnp.ones((16, 512), BF16)], axis=0)
    result = dot_nt(left, hot)
    data = result[0:32] + result[32:64] + result[64:96]
    return data, result[96:97] * weights[column, view : view + 1, :]


def scatter_kernel(slots, weights, data, cover):
    for column in range(8):
        data[column], row = scattered(1, slots, weights, column)
        cover[column] = jnp.broadcast_to(row, (8, 256))


def payloads(value, far, near):
    upper = upper_half()
    far[...] = value[:, pl.ds(pl.multiple_of(16 * upper, 16), 16), :]
    near[...] = value[:, pl.ds(pl.multiple_of(16 - 16 * upper, 16), 16), :]


def widened(wide, value, far, near, margin):
    rows, upper = value.shape[1], upper_half()
    wide[:, margin : margin + rows, :] = value[...]
    side = margin + rows
    wide[:, pl.ds(pl.multiple_of(side * upper, 16), margin), :] = far[...]
    wide[:, pl.ds(pl.multiple_of(side - side * upper, 16), margin), :] = near[...]


def blurred_into(wide, band, big_high, big_low, flat, total):
    rows = wide.shape[1] - 32
    weights = band[...]
    for column in range(8):
        for start in range(0, rows, 32):
            stacked = jnp.concatenate(split2(wide[column, start : start + 64, :]), axis=0)
            both = dot_nn(weights, stacked)
            at = column * rows + start
            flat[at : at + 32, :] = both[0:32] + both[32:64]
    high, low = split2(flat[...])

    def product(start, stop, dx, dy):
        at = (dx + 1) * 3 + dy + 1
        size = stop - start
        both = dot_nn(jnp.concatenate([high[start:stop], low[start:stop]], axis=0), big_high[at])
        return both[:size] + both[size:] + dot_nn(high[start:stop], big_low[at])

    total[...] = product(0, 8 * rows, 0, 0)
    for dx in (-1, 0, 1):
        for dy in (-1, 0, 1):
            if dx == 0 and dy == 0:
                continue
            for x in range(2):
                if not 0 <= x + dx < 2:
                    continue
                first, last = max(0, -dy), min(4, 4 - dy)
                start, stop = (x * 4 + first) * rows, (x * 4 + last) * rows
                shift = (dx * 4 + dy) * rows
                total[start:stop, :] += product(start + shift, stop + shift, dx, dy)


def blur_kernel(est, far, near, band, big_high, big_low, blurred, wide, flat):
    widened(wide, est, far, near, 16)
    blurred_into(wide, band, big_high, big_low, flat, blurred)


def ratio_from(ratio, data, cover, blurred):
    for column in range(8):
        here = blurred[column * 32 : column * 32 + 32, :]
        ratio[column] = 1.0 + cover[column, 0:1, :] * (data[column] / here - 1.0)


def scatter_ratio_kernel(slots, weights, blurred, ratio):
    for column in range(8):
        data, cover = scattered(0, slots, weights, column)
        ratio[column] = 1.0 + cover * (data / blurred[column * 32 : column * 32 + 32, :] - 1.0)


def middle_kernel(
    ratio, ratio_far, ratio_near, est, est_far, est_near, band0, high0, low0, band1, high1, low1,
    data, cover, new, next_ratio, far, near, wide, tall, flat, total, short,
):
    widened(wide, ratio, ratio_far, ratio_near, 32)
    widened(tall, est, est_far, est_near, 16)
    blurred_into(wide, band0, high0, low0, flat, total)
    for column in range(8):
        tall[column] = tall[column] * total[column * 64 : column * 64 + 64, :]
    new[...] = tall[:, 16:48, :]
    out = total.at[0:256, :]
    blurred_into(tall, band1, high1, low1, short, out)
    ratio_from(next_ratio, data, cover, out)
    payloads(next_ratio, far, near)


def last_kernel(ratio, far, near, band, big_high, big_low, est, keep, give, wide, flat, total):
    widened(wide, ratio, far, near, 16)
    blurred_into(wide, band, big_high, big_low, flat, total)
    _, _, core, _ = coordinates()
    for flip, x, y, _ in chips():
        for turn, out in enumerate((keep, give)):
            column = 4 * x + 2 * y + (core if turn == 0 else 1 - core)
            start = pl.multiple_of(column * 32, 32)
            out[flip] = est[column] * total[pl.ds(start, 32), :]


def merge_kernel(keep, got, *pieces):
    upper = upper_half()
    for flip in range(4):
        pieces[flip][pl.ds(pl.multiple_of(32 * upper, 32), 32), :] = keep[flip]
        pieces[flip][pl.ds(pl.multiple_of(32 - 32 * upper, 32), 32), :] = got[flip]


def join_kernel(*refs):
    pieces, (out, held) = refs[:4], refs[4:]
    for flip, _, _, place in chips():
        held[pl.ds(pl.multiple_of(64 * place, 64), 64), :] = pieces[flip][...]
    out[...] = held[...].T


def shape(*dims, dtype=F32):
    return jax.ShapeDtypeStruct(dims, dtype)


def swaps(planes):
    def flipped(by):
        return [(d * planes + z, (d ^ by) * planes + z) for d in range(8) for z in range(planes)]

    return [flipped(by) for by in (2, 4, 6)], flipped(1)


def slab_sweep(planes, estimate, raw_lines, line_index, psf, view_weight):
    far_pairs, near_pairs = chain_pairs(planes)
    to_chips, to_core = swaps(planes)

    def exchange(far, near):
        return (
            lax.ppermute(far, ALL, far_pairs),
            lax.ppermute(near, ALL, near_pairs),
        )

    own, *away = call(
        est_kernel, (shape(72, 256),) * 4, [SMEM, VMEM], [pltpu.VMEM((256, 256), F32)]
    )(view_weight.reshape(2), estimate.reshape(256, 256))
    here = [own] + [lax.ppermute(piece, ALL, pairs) for piece, pairs in zip(away, to_chips)]
    there = [lax.ppermute(piece, ALL, to_core) for piece in here]

    anywhere = pl.BlockSpec(memory_space=pl.ANY)
    slots = call(
        functools.partial(lines_kernel, planes),
        shape(8, planes, 72, 128),
        [anywhere, anywhere],
        [
            pltpu.VMEM((planes, 2, 4, 32, 256), F32),
            pltpu.VMEM((8, 128), jnp.int32),
            pltpu.VMEM((planes, 8, 72, 128), F32),
            pltpu.SemaphoreType.DMA((planes,)),
            pltpu.SemaphoreType.DMA((1,)),
            pltpu.SemaphoreType.DMA((planes,)),
        ],
        out_specs=anywhere,
        vmem=56,
    )(raw_lines.reshape(2, 4, planes, 32, 256), line_index.reshape(8, 128))
    slots = slots.reshape(8 * planes, 72, 128)
    slots = lax.all_to_all(slots, ALL, split_axis=0, concat_axis=0, tiled=True)
    half, full = shape(8, 16, 256), shape(8, 32, 256)

    def work(*dims):
        return pltpu.VMEM(dims, F32)

    est, weights, est_far, est_near = call(slab_kernel, (full, shape(8, 8, 256), half, half), [VMEM] * 8)(
        *here, *there
    )
    est_far = lax.ppermute(est_far, ALL, far_pairs)
    def matrices(view, way, after):
        big = shape(9, 256, 256, dtype=BF16)
        big_high, big_low, band = call(
            functools.partial(taps_kernel, view, way),
            (big, big, shape(64, 128, dtype=BF16)),
            [VMEM, anywhere],
            [work(8, 128)],
            flops=1 << 30,
        )(psf.transpose(1, 0, 2), after)
        return band, big_high, big_low

    blurred = call(
        blur_kernel, shape(256, 256), [VMEM] * 6, [work(8, 64, 256), work(256, 256)], flops=1 << 30
    )(est, est_far, est_near, *matrices(0, 0, est))
    ratio = call(scatter_ratio_kernel, full, [VMEM] * 3, flops=1 << 30)(slots, weights, blurred)
    data, cover = call(scatter_kernel, (full, shape(8, 8, 256)), [VMEM] * 2, flops=1 << 30)(slots, weights)
    est, ratio, far, near = call(
        middle_kernel,
        (full, full, half, half),
        [VMEM] * 14,
        [work(8, 96, 256), work(8, 64, 256), work(512, 256), work(512, 256), work(256, 256)],
        flops=1 << 30,
    )(ratio, *exchange(ratio, ratio), est, est_far, est_near, *matrices(0, 1, slots), *matrices(1, 0, slots), data, cover)
    quarter = shape(4, 32, 256)
    keep, give = call(
        last_kernel,
        (quarter, quarter),
        [VMEM] * 7,
        [work(8, 64, 256), work(256, 256), work(256, 256)],
        flops=1 << 30,
    )(ratio, *exchange(far, near), *matrices(1, 1, ratio), est)
    got = lax.ppermute(give, ALL, to_core)
    own, *away = call(merge_kernel, (shape(64, 256),) * 4, [VMEM] * 2)(keep, got)
    parts = [own] + [lax.ppermute(piece, ALL, pairs) for piece, pairs in zip(away, to_chips)]
    out = call(join_kernel, shape(256, 256), [VMEM] * 4, [pltpu.VMEM((256, 256), F32)])(*parts)
    return out.reshape(16, 16, 256)


def padded(block, sides, width):
    for axis, dim in sides:
        count = lax.axis_size(axis)
        forward = [(i, i + 1) for i in range(count - 1)]
        backward = [(target, source) for source, target in forward]
        low = lax.ppermute(
            lax.slice_in_dim(block, block.shape[dim] - width, None, axis=dim), axis, forward
        )
        high = lax.ppermute(lax.slice_in_dim(block, 0, width, axis=dim), axis, backward)
        block = jnp.concatenate([low, block, high], axis=dim)
    return block


def band_matrix(taps, length):
    width = taps.shape[0]
    rows = lax.broadcasted_iota(jnp.int32, (length + width - 1, length), 0)
    cols = lax.broadcasted_iota(jnp.int32, (length + width - 1, length), 1)
    offset = rows - cols
    valid = (offset >= 0) & (offset < width)
    return jnp.where(valid, taps[jnp.clip(offset, 0, width - 1)], 0.0)


def along_x(extended, matrix_x):
    lead, size_y, size_z = extended.shape
    flat = extended.reshape(lead, size_y * size_z)
    result = jnp.dot(matrix_x.T, flat, precision=lax.Precision.HIGHEST)
    return result.reshape(matrix_x.shape[1], size_y, size_z)


def blur(field, taps):
    half_width = (taps.shape[1] - 1) // 2
    size_x, size_y, size_z = field.shape
    matrix_x = band_matrix(taps[0], size_x)
    matrix_y = band_matrix(taps[1], size_y)
    matrix_z = band_matrix(taps[2], size_z)
    highest = lax.Precision.HIGHEST
    extended = padded(field, (("gz", 2),), half_width)
    result = jnp.einsum("abj,jc->abc", extended, matrix_z, precision=highest)
    extended = padded(result, (("gy", 1),), half_width)
    result = jnp.einsum("ajc,jb->abc", extended, matrix_y, precision=highest)
    extended = padded(result, (("gx", 0),), half_width)
    result = along_x(extended, matrix_x)
    return result


def block_sweep(estimate, raw_lines, line_index, psf, view_weight):
    size_x, size_y, size_z = estimate.shape
    block_lines = size_x * size_y
    views = raw_lines.shape[0]
    group = lax.axis_size(("gy", "gz"))
    slots = line_index.shape[-1]
    capacity = slots // group
    lines = raw_lines.reshape(views, group, capacity, size_z)
    indices = line_index.reshape(views, group, capacity)
    lines, indices = (
        lax.all_to_all(lines, ("gy", "gz"), split_axis=1, concat_axis=1, tiled=True),
        lax.all_to_all(indices, ("gy", "gz"), split_axis=1, concat_axis=1, tiled=True),
    )
    est = estimate
    for view in range(views):
        flat_index = indices[view].reshape(-1)
        flat_lines = lines[view].reshape(-1, size_z)
        volume = (
            jnp.zeros((block_lines, size_z), jnp.float32)
            .at[flat_index]
            .set(flat_lines, mode="drop")
        )
        volume = volume.reshape(size_x, size_y, size_z)
        cover = jnp.zeros((block_lines,), jnp.float32).at[flat_index].set(1.0, mode="drop")
        cover = cover.reshape(size_x, size_y, 1)
        weight = view_weight[view].reshape(()).astype(jnp.float32) * 0.25
        taps = psf[view] / jnp.sum(psf[view], axis=1, keepdims=True)
        blurred = blur(est, taps)
        ratio = 1.0 + weight * cover * (volume / blurred - 1.0)
        est = est * blur(ratio, taps[:, ::-1])
    return est


def solution(mesh):
    placed = (
        P("gx", "gy", "gz"),
        P(None, "gx", ("gy", "gz"), None, None),
        P(None, "gx", ("gy", "gz"), None),
        P(),
        P(None, "gx", "gy", "gz"),
    )
    sizes = tuple(mesh.shape[axis] for axis in ALL)

    def on_device(estimate, raw_lines, line_index, psf, view_weight):
        capacity = line_index.shape[-1] // (sizes[1] * sizes[2])
        fits = (
            sizes == (2, 4, 4)
            and estimate.shape == (16, 16, 256)
            and raw_lines.shape[0] == 2
            and capacity == 32
            and psf.shape == (2, 3, 33)
        )
        plan = functools.partial(slab_sweep, sizes[2]) if fits else block_sweep
        return plan(estimate, raw_lines, line_index, psf, view_weight)

    return jax.shard_map(
        on_device, mesh=mesh, in_specs=placed, out_specs=P("gx", "gy", "gz"), check_vma=False
    )
```

```python
import functools

import jax
import jax.numpy as jnp
from jax import lax
from jax.experimental import pallas as pl
from jax.experimental.pallas import tpu as pltpu
from jax.sharding import PartitionSpec as P

F32, BF16 = jnp.float32, jnp.bfloat16
VMEM = pl.BlockSpec(memory_space=pltpu.VMEM)
SMEM = pl.BlockSpec(memory_space=pltpu.SMEM)
ALL = ("gx", "gy", "gz")


def ring_place(x, y, z):
    place = 2 * x + (x ^ y)
    return place if z % 2 == 0 else 3 - place


def slab_of(device, z):
    x, gy = device // 4, device % 4
    place = ring_place(x, gy // 2, z)
    return 2 * place + gy % 2


def chain_pairs(planes):
    order = []
    for z in range(planes):
        by_slab = sorted(range(8), key=lambda device: slab_of(device, z))
        order += [device * planes + z for device in by_slab]
    far, near = [], []
    for k in range(len(order) - 1):
        pair = (order[k], order[k + 1])
        (near if k % 2 == 0 else far).extend([pair, pair[::-1]])
    return far, near


def split2(value):
    high = value.astype(BF16)
    return high, (value - high.astype(F32)).astype(BF16)


def split3(value):
    high = value.astype(BF16)
    rest = value - high.astype(F32)
    middle = rest.astype(BF16)
    return high, middle, (rest - middle.astype(F32)).astype(BF16)


def dot_nn(a, b):
    return lax.dot_general(a, b, (((1,), (0,)), ((), ())), preferred_element_type=F32)


def dot_nt(a, b):
    return lax.dot_general(a, b, (((1,), (1,)), ((), ())), preferred_element_type=F32)


def call(kernel, out_shapes, in_specs, scratch=(), flops=0, out_specs=None, vmem=16):
    return pl.pallas_call(
        kernel,
        out_shape=out_shapes,
        in_specs=in_specs,
        out_specs=out_specs or jax.tree.map(lambda _: VMEM, out_shapes),
        scratch_shapes=list(scratch),
        compiler_params=pltpu.CompilerParams(vmem_limit_bytes=vmem * 1024 * 1024),
        cost_estimate=pl.CostEstimate(flops=flops, bytes_accessed=1 << 20, transcendentals=0),
    )


def coordinates():
    x, gy, z = (lax.axis_index(axis) for axis in ALL)
    y, core = gy // 2, lax.rem(gy, 2)
    return x, y, core, z


def place_on_ring(x, y, z):
    place = 2 * x + lax.rem(x + y, 2)
    return jnp.where(lax.rem(z, 2) == 0, place, 3 - place)


def upper_half():
    return coordinates()[2]


def chips():
    x, y, _, z = coordinates()
    for flip in range(4):
        other_x = 1 - x if flip // 2 else x
        other_y = 1 - y if flip % 2 else y
        yield flip, other_x, other_y, place_on_ring(other_x, other_y, z)


def est_kernel(weight, est, *refs):
    pieces, turned = refs[:4], refs[4]
    turned[...] = est[...].T
    rows = lax.broadcasted_iota(jnp.int32, (8, 256), 0)
    weights = jnp.where(
        rows == 0,
        weight[0].astype(F32) * 0.25,
        jnp.where(rows == 1, weight[1].astype(F32) * 0.25, 0.0),
    )
    for flip, _, _, place in chips():
        pieces[flip][0:64, :] = turned[pl.ds(pl.multiple_of(place * 64, 64), 64), :]
        pieces[flip][64:72, :] = weights


def slab_kernel(*refs):
    pieces, (slab, weights, far, near) = refs[:8], refs[8:]
    _, _, core, _ = coordinates()
    upper = upper_half()
    for flip, x, y, _ in chips():
        for turn in range(2):
            piece = pieces[4 * turn + flip]
            column = 4 * x + 2 * y + (core if turn == 0 else 1 - core)
            slab[column] = piece[pl.ds(pl.multiple_of(32 * upper, 32), 32), :]
            weights[column] = piece[64:72, :]
            far[column] = piece[pl.ds(pl.multiple_of(48 * upper, 16), 16), :]
            near[column] = piece[pl.ds(pl.multiple_of(32 - 16 * upper, 16), 16), :]


def lines_kernel(planes, raw, index, out, held, numbers, made, arrived, numbered, left):
    mine = lax.axis_index("gz")
    blocks = [lax.rem(place - mine + 4, 4) for place in range(4)]
    chunk = lax.broadcasted_iota(jnp.int32, (8, 128), 1) // 32
    rows = lax.broadcasted_iota(jnp.int32, (8, 128), 0)

    def load(z):
        return pltpu.make_async_copy(raw.at[:, :, z], held.at[z], arrived.at[z])

    def store(z):
        rows = pl.ds(64 * z, 64 if z < planes - 1 else 64 + 2 * planes)
        return pltpu.make_async_copy(made.at[:, rows], out.at[:, rows], left.at[z])

    load_numbers = pltpu.make_async_copy(index, numbers, numbered.at[0])
    for z in range(planes):
        load(z).start()
    load_numbers.start()
    for z in range(planes):
        load(z).wait()
        for view in range(2):
            lines = jnp.concatenate([held[z, view, block] for block in blocks], axis=0)
            turned = lines.T
            for device in range(8):
                slab = slab_of(device, z)
                at = 66 * z + 32 * view
                made[device, at : at + 32, :] = turned[slab * 32 : slab * 32 + 32, :]
        if z == 0:
            load_numbers.wait()
        both = jnp.zeros((8, 128), F32)
        for place, block in enumerate(blocks):
            for view in range(2):
                row = numbers[pl.ds(view * 4 + block, 1), :].astype(F32)
                row = pltpu.roll(jnp.broadcast_to(row, (8, 128)), (32 * (place - z)) % 128, 1)
                both = jnp.where((chunk == place) & (rows == view), row, both)
        for device in range(8):
            made[device, 66 * z + 64 : 66 * z + 66, :] = both[0:2, :]
        store(z).start()
    for z in range(planes):
        store(z).wait()


def taps_kernel(view, way, psf, _, big_high, big_low, band, held):
    held[...] = jnp.zeros_like(held)
    held[0:3, 0:33] = psf[:, view, :]
    taps = held[...]
    total = jnp.sum(taps, axis=1, keepdims=True)
    taps = taps / jnp.where(total == 0.0, 1.0, total)

    def toeplitz(row, size):
        wide = jnp.broadcast_to(row, (size, 128))
        return pltpu.roll(wide, 0, 1, stride=1, stride_axis=0)

    from_lane = lax.broadcasted_iota(jnp.int32, (128, 128), 0)
    to_lane = lax.broadcasted_iota(jnp.int32, (128, 128), 1)
    turn = (from_lane + to_lane == 32).astype(BF16)
    turned = sum(dot_nn(piece, turn) for piece in split3(taps))
    along_z, along_xy = (taps, turned) if way == 0 else (turned, taps)
    high, low = (part.astype(F32) for part in split2(toeplitz(along_z[2:3, :], 32)))
    band[0:32, :] = (high + pltpu.roll(high, 64, 1)).astype(BF16)
    band[32:64, :] = low.astype(BF16)
    tall_x = jnp.broadcast_to(toeplitz(along_xy[0:1, :], 16)[:, None, :], (16, 16, 128)).reshape(256, 128)
    tall_y = jnp.broadcast_to(toeplitz(along_xy[1:2, :], 16)[None], (16, 16, 128)).reshape(256, 128)
    from_row = lax.broadcasted_iota(jnp.int32, (128, 256), 0)
    to_lane = lax.broadcasted_iota(jnp.int32, (128, 256), 1)
    wide_x, wide_y = [], []
    for offset in range(3):
        pick_x = (from_row == to_lane // 16 + 16 * offset).astype(BF16)
        pick_y = (from_row == lax.rem(to_lane, 16) + 16 * offset).astype(BF16)
        wide_x.append(sum(dot_nn(piece, pick_x) for piece in split3(tall_x)))
        wide_y.append(sum(dot_nn(piece, pick_y) for piece in split3(tall_y)))
    for dx in range(3):
        for dy in range(3):
            high, low = split2(wide_x[dx] * wide_y[dy])
            big_high[8 - dx * 3 - dy] = high
            big_low[8 - dx * 3 - dy] = low


def scattered(view, slots, weights, column):
    chunk = lax.broadcasted_iota(jnp.int32, (32, 128), 1) // 32
    line = lax.broadcasted_iota(jnp.int32, (256, 512), 0).astype(F32)
    x, block = column // 4, column % 4
    numbers, values = [], []
    for t in range(4):
        tile = jnp.zeros((32, 128), F32)
        number = jnp.zeros((1, 128), F32)
        for place in range(4):
            device, at = 4 * x + t, 66 * ((place - block) % 4)
            tile = jnp.where(chunk == place, slots[device, at + 32 * view : at + 32 * view + 32, :], tile)
            row = slots[device, at + 64 + view : at + 65 + view, :]
            number = jnp.where(chunk[0:1] == place, row, number)
        values.append(tile)
        numbers.append(number)
    value = jnp.concatenate(values, axis=1)
    number = jnp.concatenate(numbers, axis=1)
    hot = (line == number).astype(BF16)
    left = jnp.concatenate([*split3(value), jnp.ones((16, 512), BF16)], axis=0)
    result = dot_nt(left, hot)
    data = result[0:32] + result[32:64] + result[64:96]
    return data, result[96:97] * weights[column, view : view + 1, :]


def scatter_kernel(slots, weights, data, cover):
    for column in range(8):
        data[column], row = scattered(1, slots, weights, column)
        cover[column] = jnp.broadcast_to(row, (8, 256))


def payloads(value, far, near):
    upper = upper_half()
    far[...] = value[:, pl.ds(pl.multiple_of(16 * upper, 16), 16), :]
    near[...] = value[:, pl.ds(pl.multiple_of(16 - 16 * upper, 16), 16), :]


def widened(wide, value, far, near, margin):
    rows, upper = value.shape[1], upper_half()
    wide[:, margin : margin + rows, :] = value[...]
    side = margin + rows
    wide[:, pl.ds(pl.multiple_of(side * upper, 16), margin), :] = far[...]
    wide[:, pl.ds(pl.multiple_of(side - side * upper, 16), margin), :] = near[...]


def blurred_into(wide, band, big_high, big_low, flat, total):
    rows = wide.shape[1] - 32
    weights = band[...]
    for column in range(8):
        for start in range(0, rows, 32):
            stacked = jnp.concatenate(split2(wide[column, start : start + 64, :]), axis=0)
            both = dot_nn(weights, stacked)
            at = column * rows + start
            flat[at : at + 32, :] = both[0:32] + both[32:64]
    high, low = split2(flat[...])

    def product(start, stop, dx, dy):
        at = (dx + 1) * 3 + dy + 1
        size = stop - start
        both = dot_nn(jnp.concatenate([high[start:stop], low[start:stop]], axis=0), big_high[at])
        return both[:size] + both[size:] + dot_nn(high[start:stop], big_low[at])

    total[...] = product(0, 8 * rows, 0, 0)
    for dx in (-1, 0, 1):
        for dy in (-1, 0, 1):
            if dx == 0 and dy == 0:
                continue
            for x in range(2):
                if not 0 <= x + dx < 2:
                    continue
                first, last = max(0, -dy), min(4, 4 - dy)
                start, stop = (x * 4 + first) * rows, (x * 4 + last) * rows
                shift = (dx * 4 + dy) * rows
                total[start:stop, :] += product(start + shift, stop + shift, dx, dy)


def blur_kernel(est, far, near, band, big_high, big_low, blurred, wide, flat):
    widened(wide, est, far, near, 16)
    blurred_into(wide, band, big_high, big_low, flat, blurred)


def ratio_from(ratio, data, cover, blurred):
    for column in range(8):
        here = blurred[column * 32 : column * 32 + 32, :]
        ratio[column] = 1.0 + cover[column, 0:1, :] * (data[column] / here - 1.0)


def scatter_ratio_kernel(slots, weights, blurred, ratio):
    for column in range(8):
        data, cover = scattered(0, slots, weights, column)
        ratio[column] = 1.0 + cover * (data / blurred[column * 32 : column * 32 + 32, :] - 1.0)


def middle_kernel(
    ratio, ratio_far, ratio_near, est, est_far, est_near, band0, high0, low0, band1, high1, low1,
    data, cover, new, next_ratio, far, near, wide, tall, flat, total, short,
):
    widened(wide, ratio, ratio_far, ratio_near, 32)
    widened(tall, est, est_far, est_near, 16)
    blurred_into(wide, band0, high0, low0, flat, total)
    for column in range(8):
        tall[column] = tall[column] * total[column * 64 : column * 64 + 64, :]
    new[...] = tall[:, 16:48, :]
    out = total.at[0:256, :]
    blurred_into(tall, band1, high1, low1, short, out)
    ratio_from(next_ratio, data, cover, out)
    payloads(next_ratio, far, near)


def last_kernel(ratio, far, near, band, big_high, big_low, est, keep, give, wide, flat, total):
    widened(wide, ratio, far, near, 16)
    blurred_into(wide, band, big_high, big_low, flat, total)
    _, _, core, _ = coordinates()
    for flip, x, y, _ in chips():
        for turn, out in enumerate((keep, give)):
            column = 4 * x + 2 * y + (core if turn == 0 else 1 - core)
            start = pl.multiple_of(column * 32, 32)
            out[flip] = est[column] * total[pl.ds(start, 32), :]


def merge_kernel(keep, got, *pieces):
    upper = upper_half()
    for flip in range(4):
        pieces[flip][pl.ds(pl.multiple_of(32 * upper, 32), 32), :] = keep[flip]
        pieces[flip][pl.ds(pl.multiple_of(32 - 32 * upper, 32), 32), :] = got[flip]


def join_kernel(*refs):
    pieces, (out, held) = refs[:4], refs[4:]
    for flip, _, _, place in chips():
        held[pl.ds(pl.multiple_of(64 * place, 64), 64), :] = pieces[flip][...]
    out[...] = held[...].T


def shape(*dims, dtype=F32):
    return jax.ShapeDtypeStruct(dims, dtype)


def swaps(planes):
    def flipped(by):
        return [(d * planes + z, (d ^ by) * planes + z) for d in range(8) for z in range(planes)]

    return [flipped(by) for by in (2, 4, 6)], flipped(1)


def slab_sweep(planes, estimate, raw_lines, line_index, psf, view_weight):
    far_pairs, near_pairs = chain_pairs(planes)
    to_chips, to_core = swaps(planes)

    def exchange(far, near):
        return (
            lax.ppermute(far, ALL, far_pairs),
            lax.ppermute(near, ALL, near_pairs),
        )

    own, *away = call(
        est_kernel, (shape(72, 256),) * 4, [SMEM, VMEM], [pltpu.VMEM((256, 256), F32)]
    )(view_weight.reshape(2), estimate.reshape(256, 256))
    here = [own] + [lax.ppermute(piece, ALL, pairs) for piece, pairs in zip(away, to_chips)]
    there = [lax.ppermute(piece, ALL, to_core) for piece in here]

    anywhere = pl.BlockSpec(memory_space=pl.ANY)
    slots = call(
        functools.partial(lines_kernel, planes),
        shape(8, 66 * planes, 128),
        [anywhere, anywhere],
        [
            pltpu.VMEM((planes, 2, 4, 32, 256), F32),
            pltpu.VMEM((8, 128), jnp.int32),
            pltpu.VMEM((8, 66 * planes, 128), F32),
            pltpu.SemaphoreType.DMA((planes,)),
            pltpu.SemaphoreType.DMA((1,)),
            pltpu.SemaphoreType.DMA((planes,)),
        ],
        out_specs=anywhere,
        vmem=56,
    )(raw_lines.reshape(2, 4, planes, 32, 256), line_index.reshape(8, 128))
    slots = slots.reshape(8 * planes, 1, 66 * 128)
    slots = lax.all_to_all(slots, ALL, split_axis=0, concat_axis=0, tiled=True)
    slots = slots.reshape(8, 66 * planes, 128)
    half, full = shape(8, 16, 256), shape(8, 32, 256)

    def work(*dims):
        return pltpu.VMEM(dims, F32)

    est, weights, est_far, est_near = call(slab_kernel, (full, shape(8, 8, 256), half, half), [VMEM] * 8)(
        *here, *there
    )
    est_far = lax.ppermute(est_far, ALL, far_pairs)
    def matrices(view, way, after):
        big = shape(9, 256, 256, dtype=BF16)
        big_high, big_low, band = call(
            functools.partial(taps_kernel, view, way),
            (big, big, shape(64, 128, dtype=BF16)),
            [VMEM, anywhere],
            [work(8, 128)],
            flops=1 << 30,
        )(psf.transpose(1, 0, 2), after)
        return band, big_high, big_low

    blurred = call(
        blur_kernel, shape(256, 256), [VMEM] * 6, [work(8, 64, 256), work(256, 256)], flops=1 << 30
    )(est, est_far, est_near, *matrices(0, 0, est))
    ratio = call(scatter_ratio_kernel, full, [VMEM] * 3, flops=1 << 30)(slots, weights, blurred)
    data, cover = call(scatter_kernel, (full, shape(8, 8, 256)), [VMEM] * 2, flops=1 << 30)(slots, weights)
    est, ratio, far, near = call(
        middle_kernel,
        (full, full, half, half),
        [VMEM] * 14,
        [work(8, 96, 256), work(8, 64, 256), work(512, 256), work(512, 256), work(256, 256)],
        flops=1 << 30,
    )(ratio, *exchange(ratio, ratio), est, est_far, est_near, *matrices(0, 1, slots), *matrices(1, 0, slots), data, cover)
    quarter = shape(4, 32, 256)
    keep, give = call(
        last_kernel,
        (quarter, quarter),
        [VMEM] * 7,
        [work(8, 64, 256), work(256, 256), work(256, 256)],
        flops=1 << 30,
    )(ratio, *exchange(far, near), *matrices(1, 1, ratio), est)
    got = lax.ppermute(give, ALL, to_core)
    own, *away = call(merge_kernel, (shape(64, 256),) * 4, [VMEM] * 2)(keep, got)
    parts = [own] + [lax.ppermute(piece, ALL, pairs) for piece, pairs in zip(away, to_chips)]
    out = call(join_kernel, shape(256, 256), [VMEM] * 4, [pltpu.VMEM((256, 256), F32)])(*parts)
    return out.reshape(16, 16, 256)


def padded(block, sides, width):
    for axis, dim in sides:
        count = lax.axis_size(axis)
        forward = [(i, i + 1) for i in range(count - 1)]
        backward = [(target, source) for source, target in forward]
        low = lax.ppermute(
            lax.slice_in_dim(block, block.shape[dim] - width, None, axis=dim), axis, forward
        )
        high = lax.ppermute(lax.slice_in_dim(block, 0, width, axis=dim), axis, backward)
        block = jnp.concatenate([low, block, high], axis=dim)
    return block


def band_matrix(taps, length):
    width = taps.shape[0]
    rows = lax.broadcasted_iota(jnp.int32, (length + width - 1, length), 0)
    cols = lax.broadcasted_iota(jnp.int32, (length + width - 1, length), 1)
    offset = rows - cols
    valid = (offset >= 0) & (offset < width)
    return jnp.where(valid, taps[jnp.clip(offset, 0, width - 1)], 0.0)


def along_x(extended, matrix_x):
    lead, size_y, size_z = extended.shape
    flat = extended.reshape(lead, size_y * size_z)
    result = jnp.dot(matrix_x.T, flat, precision=lax.Precision.HIGHEST)
    return result.reshape(matrix_x.shape[1], size_y, size_z)


def blur(field, taps):
    half_width = (taps.shape[1] - 1) // 2
    size_x, size_y, size_z = field.shape
    matrix_x = band_matrix(taps[0], size_x)
    matrix_y = band_matrix(taps[1], size_y)
    matrix_z = band_matrix(taps[2], size_z)
    highest = lax.Precision.HIGHEST
    extended = padded(field, (("gz", 2),), half_width)
    result = jnp.einsum("abj,jc->abc", extended, matrix_z, precision=highest)
    extended = padded(result, (("gy", 1),), half_width)
    result = jnp.einsum("ajc,jb->abc", extended, matrix_y, precision=highest)
    extended = padded(result, (("gx", 0),), half_width)
    result = along_x(extended, matrix_x)
    return result


def block_sweep(estimate, raw_lines, line_index, psf, view_weight):
    size_x, size_y, size_z = estimate.shape
    block_lines = size_x * size_y
    views = raw_lines.shape[0]
    group = lax.axis_size(("gy", "gz"))
    slots = line_index.shape[-1]
    capacity = slots // group
    lines = raw_lines.reshape(views, group, capacity, size_z)
    indices = line_index.reshape(views, group, capacity)
    lines, indices = (
        lax.all_to_all(lines, ("gy", "gz"), split_axis=1, concat_axis=1, tiled=True),
        lax.all_to_all(indices, ("gy", "gz"), split_axis=1, concat_axis=1, tiled=True),
    )
    est = estimate
    for view in range(views):
        flat_index = indices[view].reshape(-1)
        flat_lines = lines[view].reshape(-1, size_z)
        volume = (
            jnp.zeros((block_lines, size_z), jnp.float32)
            .at[flat_index]
            .set(flat_lines, mode="drop")
        )
        volume = volume.reshape(size_x, size_y, size_z)
        cover = jnp.zeros((block_lines,), jnp.float32).at[flat_index].set(1.0, mode="drop")
        cover = cover.reshape(size_x, size_y, 1)
        weight = view_weight[view].reshape(()).astype(jnp.float32) * 0.25
        taps = psf[view] / jnp.sum(psf[view], axis=1, keepdims=True)
        blurred = blur(est, taps)
        ratio = 1.0 + weight * cover * (volume / blurred - 1.0)
        est = est * blur(ratio, taps[:, ::-1])
    return est


def solution(mesh):
    placed = (
        P("gx", "gy", "gz"),
        P(None, "gx", ("gy", "gz"), None, None),
        P(None, "gx", ("gy", "gz"), None),
        P(),
        P(None, "gx", "gy", "gz"),
    )
    sizes = tuple(mesh.shape[axis] for axis in ALL)

    def on_device(estimate, raw_lines, line_index, psf, view_weight):
        capacity = line_index.shape[-1] // (sizes[1] * sizes[2])
        fits = (
            sizes == (2, 4, 4)
            and estimate.shape == (16, 16, 256)
            and raw_lines.shape[0] == 2
            and capacity == 32
            and psf.shape == (2, 3, 33)
        )
        plan = functools.partial(slab_sweep, sizes[2]) if fits else block_sweep
        return plan(estimate, raw_lines, line_index, psf, view_weight)

    return jax.shard_map(
        on_device, mesh=mesh, in_specs=placed, out_specs=P("gx", "gy", "gz"), check_vma=False
    )
```

```python
import functools

import jax
import jax.numpy as jnp
from jax import lax
from jax.experimental import pallas as pl
from jax.experimental.pallas import tpu as pltpu
from jax.sharding import PartitionSpec as P

F32, BF16 = jnp.float32, jnp.bfloat16
VMEM = pl.BlockSpec(memory_space=pltpu.VMEM)
SMEM = pl.BlockSpec(memory_space=pltpu.SMEM)
ALL = ("gx", "gy", "gz")


def ring_place(x, y, z):
    place = 2 * x + (x ^ y)
    return place if z % 2 == 0 else 3 - place


def slab_of(device, z):
    x, gy = device // 4, device % 4
    place = ring_place(x, gy // 2, z)
    return 2 * place + gy % 2


def chain_pairs(planes):
    order = []
    for z in range(planes):
        by_slab = sorted(range(8), key=lambda device: slab_of(device, z))
        order += [device * planes + z for device in by_slab]
    far, near = [], []
    for k in range(len(order) - 1):
        pair = (order[k], order[k + 1])
        (near if k % 2 == 0 else far).extend([pair, pair[::-1]])
    return far, near


def split2(value):
    high = value.astype(BF16)
    return high, (value - high.astype(F32)).astype(BF16)


def split3(value):
    high = value.astype(BF16)
    rest = value - high.astype(F32)
    middle = rest.astype(BF16)
    return high, middle, (rest - middle.astype(F32)).astype(BF16)


def dot_nn(a, b):
    return lax.dot_general(a, b, (((1,), (0,)), ((), ())), preferred_element_type=F32)


def dot_nt(a, b):
    return lax.dot_general(a, b, (((1,), (1,)), ((), ())), preferred_element_type=F32)


def call(kernel, out_shapes, in_specs, scratch=(), flops=0, out_specs=None, vmem=16):
    return pl.pallas_call(
        kernel,
        out_shape=out_shapes,
        in_specs=in_specs,
        out_specs=out_specs or jax.tree.map(lambda _: VMEM, out_shapes),
        scratch_shapes=list(scratch),
        compiler_params=pltpu.CompilerParams(vmem_limit_bytes=vmem * 1024 * 1024),
        cost_estimate=pl.CostEstimate(flops=flops, bytes_accessed=1 << 20, transcendentals=0),
    )


def coordinates():
    x, gy, z = (lax.axis_index(axis) for axis in ALL)
    y, core = gy // 2, lax.rem(gy, 2)
    return x, y, core, z


def place_on_ring(x, y, z):
    place = 2 * x + lax.rem(x + y, 2)
    return jnp.where(lax.rem(z, 2) == 0, place, 3 - place)


def upper_half():
    return coordinates()[2]


def chips():
    x, y, _, z = coordinates()
    for flip in range(4):
        other_x = 1 - x if flip // 2 else x
        other_y = 1 - y if flip % 2 else y
        yield flip, other_x, other_y, place_on_ring(other_x, other_y, z)


def est_kernel(weight, est, *refs):
    pieces, turned = refs[:4], refs[4]
    turned[...] = est[...].T
    rows = lax.broadcasted_iota(jnp.int32, (8, 256), 0)
    weights = jnp.where(
        rows == 0,
        weight[0].astype(F32) * 0.25,
        jnp.where(rows == 1, weight[1].astype(F32) * 0.25, 0.0),
    )
    for flip, _, _, place in chips():
        pieces[flip][0:64, :] = turned[pl.ds(pl.multiple_of(place * 64, 64), 64), :]
        pieces[flip][64:72, :] = weights


def slab_kernel(*refs):
    pieces, (slab, weights, far, near) = refs[:8], refs[8:]
    _, _, core, _ = coordinates()
    upper = upper_half()
    for flip, x, y, _ in chips():
        for turn in range(2):
            piece = pieces[4 * turn + flip]
            column = 4 * x + 2 * y + (core if turn == 0 else 1 - core)
            slab[column] = piece[pl.ds(pl.multiple_of(32 * upper, 32), 32), :]
            weights[column] = piece[64:72, :]
            far[column] = piece[pl.ds(pl.multiple_of(48 * upper, 16), 16), :]
            near[column] = piece[pl.ds(pl.multiple_of(32 - 16 * upper, 16), 16), :]


def lines_kernel(planes, raw, index, out, held, numbers, made, arrived, numbered, left):
    mine = lax.axis_index("gz")
    blocks = [lax.rem(place - mine + 4, 4) for place in range(4)]
    chunk = lax.broadcasted_iota(jnp.int32, (8, 128), 1) // 32
    rows = lax.broadcasted_iota(jnp.int32, (8, 128), 0)

    def load(z):
        return pltpu.make_async_copy(raw.at[:, :, z], held.at[z], arrived.at[z])

    def store(z):
        rows = pl.ds(64 * z, 64 if z < planes - 1 else 64 + 2 * planes)
        return pltpu.make_async_copy(made.at[:, rows], out.at[:, rows], left.at[z])

    load_numbers = pltpu.make_async_copy(index, numbers, numbered.at[0])
    for z in range(planes):
        load(z).start()
    load_numbers.start()
    for z in range(planes):
        load(z).wait()
        for view in range(2):
            lines = jnp.concatenate([held[z, view, block] for block in blocks], axis=0)
            turned = lines.T
            for device in range(8):
                slab = slab_of(device, z)
                at = 66 * z + 32 * view
                made[device, at : at + 32, :] = turned[slab * 32 : slab * 32 + 32, :]
        if z == 0:
            load_numbers.wait()
        both = jnp.zeros((8, 128), F32)
        for place, block in enumerate(blocks):
            for view in range(2):
                row = numbers[pl.ds(view * 4 + block, 1), :].astype(F32)
                row = pltpu.roll(jnp.broadcast_to(row, (8, 128)), (32 * (place - z)) % 128, 1)
                both = jnp.where((chunk == place) & (rows == view), row, both)
        for device in range(8):
            made[device, 66 * z + 64 : 66 * z + 66, :] = both[0:2, :]
        store(z).start()
    for z in range(planes):
        store(z).wait()


def taps_kernel(view, way, psf, _, big_high, big_low, band, held):
    held[...] = jnp.zeros_like(held)
    held[0:3, 0:33] = psf[:, view, :]
    taps = held[...]
    total = jnp.sum(taps, axis=1, keepdims=True)
    taps = taps / jnp.where(total == 0.0, 1.0, total)

    def toeplitz(row, size):
        wide = jnp.broadcast_to(row, (size, 128))
        return pltpu.roll(wide, 0, 1, stride=1, stride_axis=0)

    from_lane = lax.broadcasted_iota(jnp.int32, (128, 128), 0)
    to_lane = lax.broadcasted_iota(jnp.int32, (128, 128), 1)
    turn = (from_lane + to_lane == 32).astype(BF16)
    turned = sum(dot_nn(piece, turn) for piece in split3(taps))
    along_z, along_xy = (taps, turned) if way == 0 else (turned, taps)
    high, low = (part.astype(F32) for part in split2(toeplitz(along_z[2:3, :], 32)))
    band[0:32, :] = (high + pltpu.roll(high, 64, 1)).astype(BF16)
    band[32:64, :] = low.astype(BF16)
    small_x, small_y = split3(toeplitz(along_xy[0:1, :], 16)), split3(toeplitz(along_xy[1:2, :], 16))
    from_row = lax.broadcasted_iota(jnp.int32, (128, 256), 0)
    to_lane = lax.broadcasted_iota(jnp.int32, (128, 256), 1)
    wide_x, wide_y = [], []
    for offset in range(3):
        pick_x = (from_row == to_lane // 16 + 16 * offset).astype(BF16)
        pick_y = (from_row == lax.rem(to_lane, 16) + 16 * offset).astype(BF16)
        rows_x = sum(dot_nn(piece, pick_x) for piece in small_x)
        rows_y = sum(dot_nn(piece, pick_y) for piece in small_y)
        wide_x.append(jnp.broadcast_to(rows_x[:, None, :], (16, 16, 256)).reshape(256, 256))
        wide_y.append(jnp.broadcast_to(rows_y[None], (16, 16, 256)).reshape(256, 256))
    for dx in range(3):
        for dy in range(3):
            high, low = split2(wide_x[dx] * wide_y[dy])
            big_high[8 - dx * 3 - dy] = high
            big_low[8 - dx * 3 - dy] = low


def scattered(view, slots, weights, column):
    chunk = lax.broadcasted_iota(jnp.int32, (32, 128), 1) // 32
    line = lax.broadcasted_iota(jnp.int32, (256, 512), 0).astype(F32)
    x, block = column // 4, column % 4
    numbers, values = [], []
    for t in range(4):
        tile = jnp.zeros((32, 128), F32)
        number = jnp.zeros((1, 128), F32)
        for place in range(4):
            device, at = 4 * x + t, 66 * ((place - block) % 4)
            tile = jnp.where(chunk == place, slots[device, at + 32 * view : at + 32 * view + 32, :], tile)
            row = slots[device, at + 64 + view : at + 65 + view, :]
            number = jnp.where(chunk[0:1] == place, row, number)
        values.append(tile)
        numbers.append(number)
    value = jnp.concatenate(values, axis=1)
    number = jnp.concatenate(numbers, axis=1)
    hot = (line == number).astype(BF16)
    left = jnp.concatenate([*split3(value), jnp.ones((16, 512), BF16)], axis=0)
    result = dot_nt(left, hot)
    data = result[0:32] + result[32:64] + result[64:96]
    return data, result[96:97] * weights[column, view : view + 1, :]


def scatter_kernel(slots, weights, data, cover):
    for column in range(8):
        data[column], row = scattered(1, slots, weights, column)
        cover[column] = jnp.broadcast_to(row, (8, 256))


def payloads(value, far, near):
    upper = upper_half()
    far[...] = value[:, pl.ds(pl.multiple_of(16 * upper, 16), 16), :]
    near[...] = value[:, pl.ds(pl.multiple_of(16 - 16 * upper, 16), 16), :]


def at_end(planes):
    x, y, _, z = coordinates()
    slab = 2 * place_on_ring(x, y, z) + upper_half()
    return ((z == 0) & (slab == 0)) | ((z == planes - 1) & (slab == 7))


def widened(wide, value, far, near, margin):
    rows, upper = value.shape[1], upper_half()
    wide[:, margin : margin + rows, :] = value[...]
    side = margin + rows
    wide[:, pl.ds(pl.multiple_of(side * upper, 16), margin), :] = far
    wide[:, pl.ds(pl.multiple_of(side - side * upper, 16), margin), :] = near[...]


def blurred_into(wide, band, big_high, big_low, flat, total):
    rows = wide.shape[1] - 32
    weights = band[...]
    for column in range(8):
        for start in range(0, rows, 32):
            stacked = jnp.concatenate(split2(wide[column, start : start + 64, :]), axis=0)
            both = dot_nn(weights, stacked)
            at = column * rows + start
            flat[at : at + 32, :] = both[0:32] + both[32:64]
    high, low = split2(flat[...])

    def product(start, stop, dx, dy):
        at = (dx + 1) * 3 + dy + 1
        size = stop - start
        both = dot_nn(jnp.concatenate([high[start:stop], low[start:stop]], axis=0), big_high[at])
        return both[:size] + both[size:] + dot_nn(high[start:stop], big_low[at])

    total[...] = product(0, 8 * rows, 0, 0)
    for dx in (-1, 0, 1):
        for dy in (-1, 0, 1):
            if dx == 0 and dy == 0:
                continue
            for x in range(2):
                if not 0 <= x + dx < 2:
                    continue
                first, last = max(0, -dy), min(4, 4 - dy)
                start, stop = (x * 4 + first) * rows, (x * 4 + last) * rows
                shift = (dx * 4 + dy) * rows
                total[start:stop, :] += product(start + shift, stop + shift, dx, dy)


def blur_kernel(est, far, near, band, big_high, big_low, blurred, wide, flat):
    widened(wide, est, far[...], near, 16)
    blurred_into(wide, band, big_high, big_low, flat, blurred)


def ratio_from(ratio, data, cover, blurred):
    for column in range(8):
        here = blurred[column * 32 : column * 32 + 32, :]
        ratio[column] = 1.0 + cover[column, 0:1, :] * (data[column] / here - 1.0)


def scatter_ratio_kernel(slots, weights, blurred, ratio):
    for column in range(8):
        data, cover = scattered(0, slots, weights, column)
        ratio[column] = 1.0 + cover * (data / blurred[column * 32 : column * 32 + 32, :] - 1.0)


def update_kernel(planes, ratio, ratio_far, ratio_near, est, est_far, est_near, band, high, low, new, wide, flat, total):
    widened(wide, ratio, jnp.where(at_end(planes), 0.0, ratio_far[...]), ratio_near, 32)
    widened(new, est, est_far[...], est_near, 16)
    blurred_into(wide, band, high, low, flat, total)
    for column in range(8):
        new[column] = new[column] * total[column * 64 : column * 64 + 64, :]


def ratio_kernel(est, band, high, low, data, cover, ratio, far, near, flat, total):
    blurred_into(est, band, high, low, flat, total)
    ratio_from(ratio, data, cover, total)
    payloads(ratio, far, near)


def last_kernel(ratio, far, near, band, big_high, big_low, est, keep, give, wide, flat, total):
    widened(wide, ratio, far[...], near, 16)
    blurred_into(wide, band, big_high, big_low, flat, total)
    _, _, core, _ = coordinates()
    for flip, x, y, _ in chips():
        for turn, out in enumerate((keep, give)):
            column = 4 * x + 2 * y + (core if turn == 0 else 1 - core)
            start = pl.multiple_of(column * 32, 32)
            out[flip] = est[column, 16:48, :] * total[pl.ds(start, 32), :]


def merge_kernel(keep, got, *pieces):
    upper = upper_half()
    for flip in range(4):
        pieces[flip][pl.ds(pl.multiple_of(32 * upper, 32), 32), :] = keep[flip]
        pieces[flip][pl.ds(pl.multiple_of(32 - 32 * upper, 32), 32), :] = got[flip]


def join_kernel(*refs):
    pieces, (out, held) = refs[:4], refs[4:]
    for flip, _, _, place in chips():
        held[pl.ds(pl.multiple_of(64 * place, 64), 64), :] = pieces[flip][...]
    out[...] = held[...].T


def shape(*dims, dtype=F32):
    return jax.ShapeDtypeStruct(dims, dtype)


def swaps(planes):
    def flipped(by):
        return [(d * planes + z, (d ^ by) * planes + z) for d in range(8) for z in range(planes)]

    return [flipped(by) for by in (2, 4, 6)], flipped(1)


def slab_sweep(planes, estimate, raw_lines, line_index, psf, view_weight):
    far_pairs, near_pairs = chain_pairs(planes)
    to_chips, to_core = swaps(planes)
    ends = sorted(set(range(8 * planes)) - {source for source, _ in far_pairs})
    ring_pairs = far_pairs + [tuple(ends), tuple(ends[::-1])]

    def exchange(far, near):
        return (
            lax.ppermute(far, ALL, far_pairs),
            lax.ppermute(near, ALL, near_pairs),
        )

    own, *away = call(
        est_kernel, (shape(72, 256),) * 4, [SMEM, VMEM], [pltpu.VMEM((256, 256), F32)]
    )(view_weight.reshape(2), estimate.reshape(256, 256))
    here = [own] + [lax.ppermute(piece, ALL, pairs) for piece, pairs in zip(away, to_chips)]
    there = [lax.ppermute(piece, ALL, to_core) for piece in here]

    anywhere = pl.BlockSpec(memory_space=pl.ANY)
    slots = call(
        functools.partial(lines_kernel, planes),
        shape(8, 66 * planes, 128),
        [anywhere, anywhere],
        [
            pltpu.VMEM((planes, 2, 4, 32, 256), F32),
            pltpu.VMEM((8, 128), jnp.int32),
            pltpu.VMEM((8, 66 * planes, 128), F32),
            pltpu.SemaphoreType.DMA((planes,)),
            pltpu.SemaphoreType.DMA((1,)),
            pltpu.SemaphoreType.DMA((planes,)),
        ],
        out_specs=anywhere,
        vmem=56,
    )(raw_lines.reshape(2, 4, planes, 32, 256), line_index.reshape(8, 128))
    slots = slots.reshape(8 * planes, 1, 66 * 128)
    slots = lax.all_to_all(slots, ALL, split_axis=0, concat_axis=0, tiled=True)
    slots = slots.reshape(8, 66 * planes, 128)
    half, full = shape(8, 16, 256), shape(8, 32, 256)

    def work(*dims):
        return pltpu.VMEM(dims, F32)

    est, weights, est_far, est_near = call(slab_kernel, (full, shape(8, 8, 256), half, half), [VMEM] * 8)(
        *here, *there
    )
    est_far = lax.ppermute(est_far, ALL, far_pairs)
    def matrices(view, way, after):
        big = shape(9, 256, 256, dtype=BF16)
        big_high, big_low, band = call(
            functools.partial(taps_kernel, view, way),
            (big, big, shape(64, 128, dtype=BF16)),
            [VMEM, anywhere],
            [work(8, 128)],
            flops=1 << 30,
        )(psf.transpose(1, 0, 2), after)
        return band, big_high, big_low

    blurred = call(
        blur_kernel, shape(256, 256), [VMEM] * 6, [work(8, 64, 256), work(256, 256)], flops=1 << 30
    )(est, est_far, est_near, *matrices(0, 0, est))
    ratio = call(scatter_ratio_kernel, full, [VMEM] * 3, flops=1 << 30)(slots, weights, blurred)
    data, cover = call(scatter_kernel, (full, shape(8, 8, 256)), [VMEM] * 2, flops=1 << 30)(slots, weights)
    est = call(
        functools.partial(update_kernel, planes),
        shape(8, 64, 256),
        [VMEM] * 9,
        [work(8, 96, 256), work(512, 256), work(512, 256)],
        flops=1 << 30,
    )(ratio, lax.ppermute(ratio, ALL, ring_pairs), lax.ppermute(ratio, ALL, near_pairs), est, est_far, est_near, *matrices(0, 1, slots))
    ratio, far, near = call(
        ratio_kernel, (full, half, half), [VMEM] * 6, [work(256, 256), work(256, 256)], flops=1 << 30
    )(est, *matrices(1, 0, slots), data, cover)
    quarter = shape(4, 32, 256)
    keep, give = call(
        last_kernel,
        (quarter, quarter),
        [VMEM] * 7,
        [work(8, 64, 256), work(256, 256), work(256, 256)],
        flops=1 << 30,
    )(ratio, *exchange(far, near), *matrices(1, 1, ratio), est)
    got = lax.ppermute(give, ALL, to_core)
    own, *away = call(merge_kernel, (shape(64, 256),) * 4, [VMEM] * 2)(keep, got)
    parts = [own] + [lax.ppermute(piece, ALL, pairs) for piece, pairs in zip(away, to_chips)]
    out = call(join_kernel, shape(256, 256), [VMEM] * 4, [pltpu.VMEM((256, 256), F32)])(*parts)
    return out.reshape(16, 16, 256)


def padded(block, sides, width):
    for axis, dim in sides:
        count = lax.axis_size(axis)
        forward = [(i, i + 1) for i in range(count - 1)]
        backward = [(target, source) for source, target in forward]
        low = lax.ppermute(
            lax.slice_in_dim(block, block.shape[dim] - width, None, axis=dim), axis, forward
        )
        high = lax.ppermute(lax.slice_in_dim(block, 0, width, axis=dim), axis, backward)
        block = jnp.concatenate([low, block, high], axis=dim)
    return block


def band_matrix(taps, length):
    width = taps.shape[0]
    rows = lax.broadcasted_iota(jnp.int32, (length + width - 1, length), 0)
    cols = lax.broadcasted_iota(jnp.int32, (length + width - 1, length), 1)
    offset = rows - cols
    valid = (offset >= 0) & (offset < width)
    return jnp.where(valid, taps[jnp.clip(offset, 0, width - 1)], 0.0)


def along_x(extended, matrix_x):
    lead, size_y, size_z = extended.shape
    flat = extended.reshape(lead, size_y * size_z)
    result = jnp.dot(matrix_x.T, flat, precision=lax.Precision.HIGHEST)
    return result.reshape(matrix_x.shape[1], size_y, size_z)


def blur(field, taps):
    half_width = (taps.shape[1] - 1) // 2
    size_x, size_y, size_z = field.shape
    matrix_x = band_matrix(taps[0], size_x)
    matrix_y = band_matrix(taps[1], size_y)
    matrix_z = band_matrix(taps[2], size_z)
    highest = lax.Precision.HIGHEST
    extended = padded(field, (("gz", 2),), half_width)
    result = jnp.einsum("abj,jc->abc", extended, matrix_z, precision=highest)
    extended = padded(result, (("gy", 1),), half_width)
    result = jnp.einsum("ajc,jb->abc", extended, matrix_y, precision=highest)
    extended = padded(result, (("gx", 0),), half_width)
    result = along_x(extended, matrix_x)
    return result


def block_sweep(estimate, raw_lines, line_index, psf, view_weight):
    size_x, size_y, size_z = estimate.shape
    block_lines = size_x * size_y
    views = raw_lines.shape[0]
    group = lax.axis_size(("gy", "gz"))
    slots = line_index.shape[-1]
    capacity = slots // group
    lines = raw_lines.reshape(views, group, capacity, size_z)
    indices = line_index.reshape(views, group, capacity)
    lines, indices = (
        lax.all_to_all(lines, ("gy", "gz"), split_axis=1, concat_axis=1, tiled=True),
        lax.all_to_all(indices, ("gy", "gz"), split_axis=1, concat_axis=1, tiled=True),
    )
    est = estimate
    for view in range(views):
        flat_index = indices[view].reshape(-1)
        flat_lines = lines[view].reshape(-1, size_z)
        volume = (
            jnp.zeros((block_lines, size_z), jnp.float32)
            .at[flat_index]
            .set(flat_lines, mode="drop")
        )
        volume = volume.reshape(size_x, size_y, size_z)
        cover = jnp.zeros((block_lines,), jnp.float32).at[flat_index].set(1.0, mode="drop")
        cover = cover.reshape(size_x, size_y, 1)
        weight = view_weight[view].reshape(()).astype(jnp.float32) * 0.25
        taps = psf[view] / jnp.sum(psf[view], axis=1, keepdims=True)
        blurred = blur(est, taps)
        ratio = 1.0 + weight * cover * (volume / blurred - 1.0)
        est = est * blur(ratio, taps[:, ::-1])
    return est


def solution(mesh):
    placed = (
        P("gx", "gy", "gz"),
        P(None, "gx", ("gy", "gz"), None, None),
        P(None, "gx", ("gy", "gz"), None),
        P(),
        P(None, "gx", "gy", "gz"),
    )
    sizes = tuple(mesh.shape[axis] for axis in ALL)

    def on_device(estimate, raw_lines, line_index, psf, view_weight):
        capacity = line_index.shape[-1] // (sizes[1] * sizes[2])
        fits = (
            sizes == (2, 4, 4)
            and estimate.shape == (16, 16, 256)
            and raw_lines.shape[0] == 2
            and capacity == 32
            and psf.shape == (2, 3, 33)
        )
        plan = functools.partial(slab_sweep, sizes[2]) if fits else block_sweep
        return plan(estimate, raw_lines, line_index, psf, view_weight)

    return jax.shard_map(
        on_device, mesh=mesh, in_specs=placed, out_specs=P("gx", "gy", "gz"), check_vma=False
    )
```

```python
import functools

import jax
import jax.numpy as jnp
from jax import lax
from jax.experimental import pallas as pl
from jax.experimental.pallas import tpu as pltpu
from jax.sharding import PartitionSpec as P

F32, BF16 = jnp.float32, jnp.bfloat16
VMEM = pl.BlockSpec(memory_space=pltpu.VMEM)
SMEM = pl.BlockSpec(memory_space=pltpu.SMEM)
ALL = ("gx", "gy", "gz")


def ring_place(x, y, z):
    place = 2 * x + (x ^ y)
    return place if z % 2 == 0 else 3 - place


def slab_of(device, z):
    x, gy = device // 4, device % 4
    place = ring_place(x, gy // 2, z)
    return 2 * place + gy % 2


def chain_pairs(planes):
    order = []
    for z in range(planes):
        by_slab = sorted(range(8), key=lambda device: slab_of(device, z))
        order += [device * planes + z for device in by_slab]
    far, near = [], []
    for k in range(len(order) - 1):
        pair = (order[k], order[k + 1])
        (near if k % 2 == 0 else far).extend([pair, pair[::-1]])
    return far, near


def split2(value):
    high = value.astype(BF16)
    return high, (value - high.astype(F32)).astype(BF16)


def split3(value):
    high = value.astype(BF16)
    rest = value - high.astype(F32)
    middle = rest.astype(BF16)
    return high, middle, (rest - middle.astype(F32)).astype(BF16)


def dot_nn(a, b):
    return lax.dot_general(a, b, (((1,), (0,)), ((), ())), preferred_element_type=F32)


def dot_nt(a, b):
    return lax.dot_general(a, b, (((1,), (1,)), ((), ())), preferred_element_type=F32)


def call(kernel, out_shapes, in_specs, scratch=(), flops=0, out_specs=None, vmem=16):
    return pl.pallas_call(
        kernel,
        out_shape=out_shapes,
        in_specs=in_specs,
        out_specs=out_specs or jax.tree.map(lambda _: VMEM, out_shapes),
        scratch_shapes=list(scratch),
        compiler_params=pltpu.CompilerParams(vmem_limit_bytes=vmem * 1024 * 1024),
        cost_estimate=pl.CostEstimate(flops=flops, bytes_accessed=1 << 20, transcendentals=0),
    )


def coordinates():
    x, gy, z = (lax.axis_index(axis) for axis in ALL)
    y, core = gy // 2, lax.rem(gy, 2)
    return x, y, core, z


def place_on_ring(x, y, z):
    place = 2 * x + lax.rem(x + y, 2)
    return jnp.where(lax.rem(z, 2) == 0, place, 3 - place)


def upper_half():
    return coordinates()[2]


def chips():
    x, y, _, z = coordinates()
    for flip in range(4):
        other_x = 1 - x if flip // 2 else x
        other_y = 1 - y if flip % 2 else y
        yield flip, other_x, other_y, place_on_ring(other_x, other_y, z)


def est_kernel(weight, est, *refs):
    pieces, turned = refs[:4], refs[4]
    for half in range(2):
        turned[:, 128 * half : 128 * half + 128] = est[:, half].reshape(128, 256).T
    rows = lax.broadcasted_iota(jnp.int32, (8, 256), 0)
    weights = jnp.where(
        rows == 0,
        weight[0].astype(F32) * 0.25,
        jnp.where(rows == 1, weight[1].astype(F32) * 0.25, 0.0),
    )
    for flip, _, _, place in chips():
        pieces[flip][0:64, :] = turned[pl.ds(pl.multiple_of(place * 64, 64), 64), :]
        pieces[flip][64:72, :] = weights


def slab_kernel(*refs):
    pieces, (slab, weights, far, near) = refs[:8], refs[8:]
    _, _, core, _ = coordinates()
    upper = upper_half()
    for flip, x, y, _ in chips():
        for turn in range(2):
            piece = pieces[4 * turn + flip]
            block = 4 * y + 2 * (core if turn == 0 else 1 - core)
            lanes = pl.ds(pl.multiple_of(128 * x, 128), 128)
            for half in range(2):
                part = piece.at[:, 128 * half : 128 * half + 128]
                slab[block + half, :, lanes] = part[pl.ds(pl.multiple_of(32 * upper, 32), 32), :]
                weights[block + half, :, lanes] = part[64:72, :]
                far[block + half, :, lanes] = part[pl.ds(pl.multiple_of(48 * upper, 16), 16), :]
                near[block + half, :, lanes] = part[pl.ds(pl.multiple_of(32 - 16 * upper, 16), 16), :]


def lines_kernel(planes, raw, index, out, held, numbers, made, arrived, numbered, left):
    mine = lax.axis_index("gz")
    blocks = [lax.rem(place - mine + 4, 4) for place in range(4)]
    chunk = lax.broadcasted_iota(jnp.int32, (8, 128), 1) // 32
    rows = lax.broadcasted_iota(jnp.int32, (8, 128), 0)

    def load(z):
        return pltpu.make_async_copy(raw.at[:, :, z], held.at[z], arrived.at[z])

    def store(z):
        rows = pl.ds(64 * z, 64 if z < planes - 1 else 64 + 2 * planes)
        return pltpu.make_async_copy(made.at[:, rows], out.at[:, rows], left.at[z])

    load_numbers = pltpu.make_async_copy(index, numbers, numbered.at[0])
    for z in range(planes):
        load(z).start()
    load_numbers.start()
    for z in range(planes):
        load(z).wait()
        for view in range(2):
            lines = jnp.concatenate([held[z, view, block] for block in blocks], axis=0)
            turned = lines.T
            for device in range(8):
                slab = slab_of(device, z)
                at = 66 * z + 32 * view
                made[device, at : at + 32, :] = turned[slab * 32 : slab * 32 + 32, :]
        if z == 0:
            load_numbers.wait()
        both = jnp.zeros((8, 128), F32)
        for place, block in enumerate(blocks):
            for view in range(2):
                row = numbers[pl.ds(view * 4 + block, 1), :].astype(F32)
                row = pltpu.roll(jnp.broadcast_to(row, (8, 128)), (32 * (place - z)) % 128, 1)
                both = jnp.where((chunk == place) & (rows == view), row, both)
        for device in range(8):
            made[device, 66 * z + 64 : 66 * z + 66, :] = both[0:2, :]
        store(z).start()
    for z in range(planes):
        store(z).wait()


def taps_kernel(view, way, psf, _, big_high, big_low, band, held):
    held[...] = jnp.zeros_like(held)
    held[0:3, 0:33] = psf[:, view, :]
    taps = held[...]
    total = jnp.sum(taps, axis=1, keepdims=True)
    taps = taps / jnp.where(total == 0.0, 1.0, total)

    def toeplitz(row, size):
        wide = jnp.broadcast_to(row, (size, 128))
        return pltpu.roll(wide, 0, 1, stride=1, stride_axis=0)

    from_lane = lax.broadcasted_iota(jnp.int32, (128, 128), 0)
    to_lane = lax.broadcasted_iota(jnp.int32, (128, 128), 1)
    turn = (from_lane + to_lane == 32).astype(BF16)
    turned = sum(dot_nn(piece, turn) for piece in split3(taps))
    along_z, along_xy = (taps, turned) if way == 0 else (turned, taps)
    high, low = (part.astype(F32) for part in split2(toeplitz(along_z[2:3, :], 32)))
    band[0:32, :] = (high + pltpu.roll(high, 64, 1)).astype(BF16)
    band[32:64, :] = low.astype(BF16)
    from_row = lax.broadcasted_iota(jnp.int32, (128, 256), 0)
    to_lane = lax.broadcasted_iota(jnp.int32, (128, 256), 1)
    pick = (from_row == to_lane // 8 + 16).astype(BF16)
    rows_x = sum(dot_nn(piece, pick) for piece in split3(toeplitz(along_xy[0:1, :], 32)))
    wide_x = jnp.broadcast_to(rows_x[:, None, :], (32, 8, 256)).reshape(256, 256)
    small_y = split3(toeplitz(along_xy[1:2, :], 8))
    for offset in range(-2, 3):
        pick = (from_row == lax.rem(to_lane, 8) + 16 - 8 * offset).astype(BF16)
        rows_y = sum(dot_nn(piece, pick) for piece in small_y)
        wide_y = jnp.broadcast_to(rows_y[None], (32, 8, 256)).reshape(256, 256)
        big_high[offset + 2], big_low[offset + 2] = split2(wide_x * wide_y)


def scattered(view, slots, weights, column):
    chunk = lax.broadcasted_iota(jnp.int32, (32, 128), 1) // 32
    at = lax.broadcasted_iota(jnp.int32, (256, 512), 0)
    line = (lax.rem(at, 128) // 8 * 16 + at // 128 * 8 + lax.rem(at, 8)).astype(F32)
    x, block = column // 4, column % 4
    numbers, values = [], []
    for t in range(4):
        tile = jnp.zeros((32, 128), F32)
        number = jnp.zeros((1, 128), F32)
        for place in range(4):
            device, at = 4 * x + t, 66 * ((place - block) % 4)
            tile = jnp.where(chunk == place, slots[device, at + 32 * view : at + 32 * view + 32, :], tile)
            row = slots[device, at + 64 + view : at + 65 + view, :]
            number = jnp.where(chunk[0:1] == place, row, number)
        values.append(tile)
        numbers.append(number)
    value = jnp.concatenate(values, axis=1)
    number = jnp.concatenate(numbers, axis=1)
    hot = (line == number).astype(BF16)
    left = jnp.concatenate([*split3(value), jnp.ones((16, 512), BF16)], axis=0)
    result = dot_nt(left, hot)
    data = result[0:32] + result[32:64] + result[64:96]
    for half in range(2):
        lanes = slice(128 * half, 128 * half + 128)
        to = slice(128 * x, 128 * x + 128)
        weight = weights[2 * block + half, view : view + 1, to]
        yield 2 * block + half, to, data[:, lanes], result[96:97, lanes] * weight


def scatter_kernel(slots, weights, data, cover):
    for column in range(8):
        for block, lanes, values, covered in scattered(1, slots, weights, column):
            data[block, :, lanes] = values
            cover[block, :, lanes] = jnp.broadcast_to(covered, (8, 128))


def payloads(value, far, near):
    upper = upper_half()
    far[...] = value[:, pl.ds(pl.multiple_of(16 * upper, 16), 16), :]
    near[...] = value[:, pl.ds(pl.multiple_of(16 - 16 * upper, 16), 16), :]


def at_end(planes):
    x, y, _, z = coordinates()
    slab = 2 * place_on_ring(x, y, z) + upper_half()
    return ((z == 0) & (slab == 0)) | ((z == planes - 1) & (slab == 7))


def widened(wide, value, far, near, margin):
    rows, upper = value.shape[1], upper_half()
    wide[:, margin : margin + rows, :] = value[...]
    side = margin + rows
    wide[:, pl.ds(pl.multiple_of(side * upper, 16), margin), :] = far
    wide[:, pl.ds(pl.multiple_of(side - side * upper, 16), margin), :] = near[...]


def blurred_into(wide, band, big_high, big_low, flat, total):
    rows = wide.shape[1] - 32
    weights = band[...]
    for column in range(8):
        for start in range(0, rows, 32):
            stacked = jnp.concatenate(split2(wide[column, start : start + 64, :]), axis=0)
            both = dot_nn(weights, stacked)
            at = column * rows + start
            flat[at : at + 32, :] = both[0:32] + both[32:64]
    high, low = split2(flat[...])

    for offset in (0, -2, -1, 1, 2):
        first, last = max(0, -offset), min(8, 8 - offset)
        start, stop = (first + offset) * rows, (last + offset) * rows
        size = stop - start
        both = jnp.concatenate([high[start:stop], low[start:stop]], axis=0)
        both = dot_nn(both, big_high[offset + 2])
        part = both[:size] + both[size:] + dot_nn(high[start:stop], big_low[offset + 2])
        if offset == 0:
            total[...] = part
        else:
            total[first * rows : last * rows, :] += part


def blur_kernel(est, far, near, band, big_high, big_low, blurred, wide, flat):
    widened(wide, est, far[...], near, 16)
    blurred_into(wide, band, big_high, big_low, flat, blurred)


def ratio_from(ratio, data, cover, blurred):
    for column in range(8):
        here = blurred[column * 32 : column * 32 + 32, :]
        ratio[column] = 1.0 + cover[column, 0:1, :] * (data[column] / here - 1.0)


def scatter_ratio_kernel(slots, weights, blurred, ratio):
    for column in range(8):
        for block, lanes, values, covered in scattered(0, slots, weights, column):
            here = blurred[32 * block : 32 * block + 32, lanes]
            ratio[block, :, lanes] = 1.0 + covered * (values / here - 1.0)


def update_kernel(planes, ratio, ratio_far, ratio_near, est, est_far, est_near, band, high, low, new, wide, flat, total):
    widened(wide, ratio, jnp.where(at_end(planes), 0.0, ratio_far[...]), ratio_near, 32)
    widened(new, est, est_far[...], est_near, 16)
    blurred_into(wide, band, high, low, flat, total)
    for column in range(8):
        new[column] = new[column] * total[column * 64 : column * 64 + 64, :]


def ratio_kernel(est, band, high, low, data, cover, ratio, far, near, flat, total):
    blurred_into(est, band, high, low, flat, total)
    ratio_from(ratio, data, cover, total)
    payloads(ratio, far, near)


def last_kernel(ratio, far, near, band, big_high, big_low, est, *refs):
    (mine, other), pieces, (wide, flat, total) = refs[:2], refs[2:5], refs[5:]
    widened(wide, ratio, far[...], near, 16)
    blurred_into(wide, band, big_high, big_low, flat, total)
    _, _, core, _ = coordinates()
    for flip, x, y, _ in chips():
        for turn in range(2):
            block = 4 * y + 2 * (core if turn == 0 else 1 - core)
            lanes = pl.ds(pl.multiple_of(128 * x, 128), 128)
            new = jnp.concatenate(
                [
                    est[block + half, 16:48, lanes]
                    * total[pl.ds(pl.multiple_of(32 * (block + half), 32), 32), lanes]
                    for half in range(2)
                ],
                axis=1,
            )
            if flip == 0:
                (mine, other)[turn][...] = new
            else:
                pieces[flip - 1][turn] = new


def join_kernel(*refs):
    pieces, others, (out, held, turned, left) = refs[:4], refs[4:8], refs[8:]
    upper = upper_half()
    for flip, _, _, place in chips():
        mine = pieces[flip][...] if flip == 0 else pieces[flip][0]
        held[pl.ds(pl.multiple_of(64 * place + 32 * upper, 32), 32), :] = mine
        held[pl.ds(pl.multiple_of(64 * place + 32 - 32 * upper, 32), 32), :] = others[flip][...]

    def store(part):
        return pltpu.make_async_copy(turned.at[:, part], out.at[:, part], left.at[part])

    for part in range(2):
        turned[:, part] = held[:, 128 * part : 128 * part + 128].T.reshape(16, 8, 256)
        store(part).start()
    for part in range(2):
        store(part).wait()


def shape(*dims, dtype=F32):
    return jax.ShapeDtypeStruct(dims, dtype)


def swaps(planes):
    def flipped(by):
        return [(d * planes + z, (d ^ by) * planes + z) for d in range(8) for z in range(planes)]

    return [flipped(by) for by in (2, 4, 6)], flipped(1)


def slab_sweep(planes, estimate, raw_lines, line_index, psf, view_weight):
    far_pairs, near_pairs = chain_pairs(planes)
    to_chips, to_core = swaps(planes)
    ends = sorted(set(range(8 * planes)) - {source for source, _ in far_pairs})
    ring_pairs = far_pairs + [tuple(ends), tuple(ends[::-1])]

    def exchange(far, near):
        return (
            lax.ppermute(far, ALL, far_pairs),
            lax.ppermute(near, ALL, near_pairs),
        )

    own, *away = call(
        est_kernel, (shape(72, 256),) * 4, [SMEM, VMEM], [pltpu.VMEM((256, 256), F32)]
    )(view_weight.reshape(2), estimate.reshape(16, 2, 8, 256))
    here = [own] + [lax.ppermute(piece, ALL, pairs) for piece, pairs in zip(away, to_chips)]
    there = [lax.ppermute(piece, ALL, to_core) for piece in here]

    anywhere = pl.BlockSpec(memory_space=pl.ANY)
    slots = call(
        functools.partial(lines_kernel, planes),
        shape(8, 66 * planes, 128),
        [anywhere, anywhere],
        [
            pltpu.VMEM((planes, 2, 4, 32, 256), F32),
            pltpu.VMEM((8, 128), jnp.int32),
            pltpu.VMEM((8, 66 * planes, 128), F32),
            pltpu.SemaphoreType.DMA((planes,)),
            pltpu.SemaphoreType.DMA((1,)),
            pltpu.SemaphoreType.DMA((planes,)),
        ],
        out_specs=anywhere,
        vmem=56,
    )(raw_lines.reshape(2, 4, planes, 32, 256), line_index.reshape(8, 128))
    slots = slots.reshape(8 * planes, 1, 66 * 128)
    slots = lax.all_to_all(slots, ALL, split_axis=0, concat_axis=0, tiled=True)
    slots = slots.reshape(8, 66 * planes, 128)
    half, full = shape(8, 16, 256), shape(8, 32, 256)

    def work(*dims):
        return pltpu.VMEM(dims, F32)

    est, weights, est_far, est_near = call(slab_kernel, (full, shape(8, 8, 256), half, half), [VMEM] * 8)(
        *here, *there
    )
    est_far = lax.ppermute(est_far, ALL, far_pairs)
    def matrices(view, way, after):
        big = shape(5, 256, 256, dtype=BF16)
        big_high, big_low, band = call(
            functools.partial(taps_kernel, view, way),
            (big, big, shape(64, 128, dtype=BF16)),
            [VMEM, anywhere],
            [work(8, 128)],
            flops=1 << 30,
        )(psf.transpose(1, 0, 2), after)
        return band, big_high, big_low

    blurred = call(
        blur_kernel, shape(256, 256), [VMEM] * 6, [work(8, 64, 256), work(256, 256)], flops=1 << 30
    )(est, est_far, est_near, *matrices(0, 0, est))
    ratio = call(scatter_ratio_kernel, full, [VMEM] * 3, flops=1 << 30)(slots, weights, blurred)
    data, cover = call(scatter_kernel, (full, shape(8, 8, 256)), [VMEM] * 2, flops=1 << 30)(slots, weights)
    est = call(
        functools.partial(update_kernel, planes),
        shape(8, 64, 256),
        [VMEM] * 9,
        [work(8, 96, 256), work(512, 256), work(512, 256)],
        flops=1 << 30,
    )(ratio, lax.ppermute(ratio, ALL, ring_pairs), lax.ppermute(ratio, ALL, near_pairs), est, est_far, est_near, *matrices(0, 1, slots))
    ratio, far, near = call(
        ratio_kernel, (full, half, half), [VMEM] * 6, [work(256, 256), work(256, 256)], flops=1 << 30
    )(est, *matrices(1, 0, slots), data, cover)
    column, pair = shape(32, 256), shape(2, 32, 256)
    mine, other, *away = call(
        last_kernel,
        (column, column, pair, pair, pair),
        [VMEM] * 7,
        [work(8, 64, 256), work(256, 256), work(256, 256)],
        flops=1 << 30,
    )(ratio, *exchange(far, near), *matrices(1, 1, ratio), est)
    away = [lax.ppermute(piece, ALL, pairs) for piece, pairs in zip(away, to_chips)]
    others = [lax.ppermute(piece, ALL, to_core) for piece in [other] + [piece[1] for piece in away]]
    out = call(
        join_kernel,
        shape(16, 2, 8, 256),
        [VMEM] * 8,
        [work(256, 256), work(16, 2, 8, 256), pltpu.SemaphoreType.DMA((2,))],
        out_specs=anywhere,
    )(mine, *away, *others)
    return out.reshape(16, 16, 256)


def padded(block, sides, width):
    for axis, dim in sides:
        count = lax.axis_size(axis)
        forward = [(i, i + 1) for i in range(count - 1)]
        backward = [(target, source) for source, target in forward]
        low = lax.ppermute(
            lax.slice_in_dim(block, block.shape[dim] - width, None, axis=dim), axis, forward
        )
        high = lax.ppermute(lax.slice_in_dim(block, 0, width, axis=dim), axis, backward)
        block = jnp.concatenate([low, block, high], axis=dim)
    return block


def band_matrix(taps, length):
    width = taps.shape[0]
    rows = lax.broadcasted_iota(jnp.int32, (length + width - 1, length), 0)
    cols = lax.broadcasted_iota(jnp.int32, (length + width - 1, length), 1)
    offset = rows - cols
    valid = (offset >= 0) & (offset < width)
    return jnp.where(valid, taps[jnp.clip(offset, 0, width - 1)], 0.0)


def along_x(extended, matrix_x):
    lead, size_y, size_z = extended.shape
    flat = extended.reshape(lead, size_y * size_z)
    result = jnp.dot(matrix_x.T, flat, precision=lax.Precision.HIGHEST)
    return result.reshape(matrix_x.shape[1], size_y, size_z)


def blur(field, taps):
    half_width = (taps.shape[1] - 1) // 2
    size_x, size_y, size_z = field.shape
    matrix_x = band_matrix(taps[0], size_x)
    matrix_y = band_matrix(taps[1], size_y)
    matrix_z = band_matrix(taps[2], size_z)
    highest = lax.Precision.HIGHEST
    extended = padded(field, (("gz", 2),), half_width)
    result = jnp.einsum("abj,jc->abc", extended, matrix_z, precision=highest)
    extended = padded(result, (("gy", 1),), half_width)
    result = jnp.einsum("ajc,jb->abc", extended, matrix_y, precision=highest)
    extended = padded(result, (("gx", 0),), half_width)
    result = along_x(extended, matrix_x)
    return result


def block_sweep(estimate, raw_lines, line_index, psf, view_weight):
    size_x, size_y, size_z = estimate.shape
    block_lines = size_x * size_y
    views = raw_lines.shape[0]
    group = lax.axis_size(("gy", "gz"))
    slots = line_index.shape[-1]
    capacity = slots // group
    lines = raw_lines.reshape(views, group, capacity, size_z)
    indices = line_index.reshape(views, group, capacity)
    lines, indices = (
        lax.all_to_all(lines, ("gy", "gz"), split_axis=1, concat_axis=1, tiled=True),
        lax.all_to_all(indices, ("gy", "gz"), split_axis=1, concat_axis=1, tiled=True),
    )
    est = estimate
    for view in range(views):
        flat_index = indices[view].reshape(-1)
        flat_lines = lines[view].reshape(-1, size_z)
        volume = (
            jnp.zeros((block_lines, size_z), jnp.float32)
            .at[flat_index]
            .set(flat_lines, mode="drop")
        )
        volume = volume.reshape(size_x, size_y, size_z)
        cover = jnp.zeros((block_lines,), jnp.float32).at[flat_index].set(1.0, mode="drop")
        cover = cover.reshape(size_x, size_y, 1)
        weight = view_weight[view].reshape(()).astype(jnp.float32) * 0.25
        taps = psf[view] / jnp.sum(psf[view], axis=1, keepdims=True)
        blurred = blur(est, taps)
        ratio = 1.0 + weight * cover * (volume / blurred - 1.0)
        est = est * blur(ratio, taps[:, ::-1])
    return est


def solution(mesh):
    placed = (
        P("gx", "gy", "gz"),
        P(None, "gx", ("gy", "gz"), None, None),
        P(None, "gx", ("gy", "gz"), None),
        P(),
        P(None, "gx", "gy", "gz"),
    )
    sizes = tuple(mesh.shape[axis] for axis in ALL)

    def on_device(estimate, raw_lines, line_index, psf, view_weight):
        capacity = line_index.shape[-1] // (sizes[1] * sizes[2])
        fits = (
            sizes == (2, 4, 4)
            and estimate.shape == (16, 16, 256)
            and raw_lines.shape[0] == 2
            and capacity == 32
            and psf.shape == (2, 3, 33)
        )
        plan = functools.partial(slab_sweep, sizes[2]) if fits else block_sweep
        return plan(estimate, raw_lines, line_index, psf, view_weight)

    return jax.shard_map(
        on_device, mesh=mesh, in_specs=placed, out_specs=P("gx", "gy", "gz"), check_vma=False
    )
```

```python
import functools

import jax
import jax.numpy as jnp
from jax import lax
from jax.experimental import pallas as pl
from jax.experimental.pallas import tpu as pltpu
from jax.sharding import PartitionSpec as P

F32, BF16 = jnp.float32, jnp.bfloat16
VMEM = pl.BlockSpec(memory_space=pltpu.VMEM)
SMEM = pl.BlockSpec(memory_space=pltpu.SMEM)
ALL = ("gx", "gy", "gz")


def ring_place(x, y, z):
    place = 2 * x + (x ^ y)
    return place if z % 2 == 0 else 3 - place


def slab_of(device, z):
    x, gy = device // 4, device % 4
    place = ring_place(x, gy // 2, z)
    return 2 * place + gy % 2


def chain_pairs(planes):
    order = []
    for z in range(planes):
        by_slab = sorted(range(8), key=lambda device: slab_of(device, z))
        order += [device * planes + z for device in by_slab]
    far, near = [], []
    for k in range(len(order) - 1):
        pair = (order[k], order[k + 1])
        (near if k % 2 == 0 else far).extend([pair, pair[::-1]])
    return far, near


def split2(value):
    high = value.astype(BF16)
    return high, (value - high.astype(F32)).astype(BF16)


def split3(value):
    high = value.astype(BF16)
    rest = value - high.astype(F32)
    middle = rest.astype(BF16)
    return high, middle, (rest - middle.astype(F32)).astype(BF16)


def dot_nn(a, b):
    return lax.dot_general(a, b, (((1,), (0,)), ((), ())), preferred_element_type=F32)


def dot_nt(a, b):
    return lax.dot_general(a, b, (((1,), (1,)), ((), ())), preferred_element_type=F32)


def call(kernel, out_shapes, in_specs, scratch=(), flops=0, out_specs=None, vmem=16):
    return pl.pallas_call(
        kernel,
        out_shape=out_shapes,
        in_specs=in_specs,
        out_specs=out_specs or jax.tree.map(lambda _: VMEM, out_shapes),
        scratch_shapes=list(scratch),
        compiler_params=pltpu.CompilerParams(vmem_limit_bytes=vmem * 1024 * 1024),
        cost_estimate=pl.CostEstimate(flops=flops, bytes_accessed=1 << 20, transcendentals=0),
    )


def coordinates():
    x, gy, z = (lax.axis_index(axis) for axis in ALL)
    y, core = gy // 2, lax.rem(gy, 2)
    return x, y, core, z


def place_on_ring(x, y, z):
    place = 2 * x + lax.rem(x + y, 2)
    return jnp.where(lax.rem(z, 2) == 0, place, 3 - place)


def upper_half():
    return coordinates()[2]


def chips():
    x, y, _, z = coordinates()
    for flip in range(4):
        other_x = 1 - x if flip // 2 else x
        other_y = 1 - y if flip % 2 else y
        yield flip, other_x, other_y, place_on_ring(other_x, other_y, z)


def est_kernel(weight, est, *refs):
    pieces, turned = refs[:4], refs[4]
    for half in range(2):
        turned[:, 128 * half : 128 * half + 128] = est[:, half].reshape(128, 256).T
    rows = lax.broadcasted_iota(jnp.int32, (8, 256), 0)
    weights = jnp.where(
        rows == 0,
        weight[0].astype(F32) * 0.25,
        jnp.where(rows == 1, weight[1].astype(F32) * 0.25, 0.0),
    )
    for flip, _, _, place in chips():
        pieces[flip][0:64, :] = turned[pl.ds(pl.multiple_of(place * 64, 64), 64), :]
        pieces[flip][64:72, :] = weights


def slab_kernel(*refs):
    pieces, (slab, weights, far, near) = refs[:8], refs[8:]
    _, _, core, _ = coordinates()
    upper = upper_half()
    for flip, x, y, _ in chips():
        for turn in range(2):
            piece = pieces[4 * turn + flip]
            block = 4 * y + 2 * (core if turn == 0 else 1 - core)
            lanes = pl.ds(pl.multiple_of(128 * x, 128), 128)
            for half in range(2):
                part = piece.at[:, 128 * half : 128 * half + 128]
                slab[block + half, :, lanes] = part[pl.ds(pl.multiple_of(32 * upper, 32), 32), :]
                weights[block + half, :, lanes] = part[64:72, :]
                far[block + half, :, lanes] = part[pl.ds(pl.multiple_of(48 * upper, 16), 16), :]
                near[block + half, :, lanes] = part[pl.ds(pl.multiple_of(32 - 16 * upper, 16), 16), :]


def lines_kernel(planes, raw, index, out, held, numbers, made, arrived, numbered, left):
    mine = lax.axis_index("gz")
    blocks = [lax.rem(place - mine + 4, 4) for place in range(4)]
    chunk = lax.broadcasted_iota(jnp.int32, (8, 128), 1) // 32
    rows = lax.broadcasted_iota(jnp.int32, (8, 128), 0)

    def load(z):
        return pltpu.make_async_copy(raw.at[:, :, z], held.at[z], arrived.at[z])

    def store(z):
        rows = pl.ds(64 * z, 64 if z < planes - 1 else 64 + 2 * planes)
        return pltpu.make_async_copy(made.at[:, rows], out.at[:, rows], left.at[z])

    load_numbers = pltpu.make_async_copy(index, numbers, numbered.at[0])
    for z in range(planes):
        load(z).start()
    load_numbers.start()
    for z in range(planes):
        load(z).wait()
        for view in range(2):
            lines = jnp.concatenate([held[z, view, block] for block in blocks], axis=0)
            turned = lines.T
            for device in range(8):
                slab = slab_of(device, z)
                at = 66 * z + 32 * view
                made[device, at : at + 32, :] = turned[slab * 32 : slab * 32 + 32, :]
        if z == 0:
            load_numbers.wait()
        both = jnp.zeros((8, 128), F32)
        for place, block in enumerate(blocks):
            for view in range(2):
                row = numbers[pl.ds(view * 4 + block, 1), :].astype(F32)
                row = pltpu.roll(jnp.broadcast_to(row, (8, 128)), (32 * (place - z)) % 128, 1)
                both = jnp.where((chunk == place) & (rows == view), row, both)
        for device in range(8):
            made[device, 66 * z + 64 : 66 * z + 66, :] = both[0:2, :]
        store(z).start()
    for z in range(planes):
        store(z).wait()


def taps_kernel(view, way, psf, _, big_high, big_low, band, held):
    held[...] = jnp.zeros_like(held)
    held[0:3, 0:33] = psf[:, view, :]
    taps = held[...]
    total = jnp.sum(taps, axis=1, keepdims=True)
    taps = taps / jnp.where(total == 0.0, 1.0, total)

    def toeplitz(row, size):
        wide = jnp.broadcast_to(row, (size, 128))
        return pltpu.roll(wide, 0, 1, stride=1, stride_axis=0)

    from_lane = lax.broadcasted_iota(jnp.int32, (128, 128), 0)
    to_lane = lax.broadcasted_iota(jnp.int32, (128, 128), 1)
    turn = (from_lane + to_lane == 32).astype(BF16)
    turned = sum(dot_nn(piece, turn) for piece in split3(taps))
    along_z, along_xy = (taps, turned) if way == 0 else (turned, taps)
    high, low = (part.astype(F32) for part in split2(toeplitz(along_z[2:3, :], 32)))
    band[0:32, :] = (high + pltpu.roll(high, 64, 1)).astype(BF16)
    band[32:64, :] = low.astype(BF16)
    from_row = lax.broadcasted_iota(jnp.int32, (128, 256), 0)
    to_lane = lax.broadcasted_iota(jnp.int32, (128, 256), 1)
    pick = (from_row == to_lane // 8 + 16).astype(BF16)
    rows_x = sum(dot_nn(piece, pick) for piece in split3(toeplitz(along_xy[0:1, :], 32)))
    wide_x = jnp.broadcast_to(rows_x[:, None, :], (32, 8, 256)).reshape(256, 256)
    small_y = split3(toeplitz(along_xy[1:2, :], 8))
    for offset in range(-2, 3):
        pick = (from_row == lax.rem(to_lane, 8) + 16 - 8 * offset).astype(BF16)
        rows_y = sum(dot_nn(piece, pick) for piece in small_y)
        wide_y = jnp.broadcast_to(rows_y[None], (32, 8, 256)).reshape(256, 256)
        big_high[offset + 2], big_low[offset + 2] = split2(wide_x * wide_y)


def scattered(view, slots, weights, column):
    chunk = lax.broadcasted_iota(jnp.int32, (32, 128), 1) // 32
    at = lax.broadcasted_iota(jnp.int32, (256, 512), 0)
    line = (lax.rem(at, 128) // 8 * 16 + at // 128 * 8 + lax.rem(at, 8)).astype(F32)
    x, block = column // 4, column % 4
    numbers, values = [], []
    for t in range(4):
        tile = jnp.zeros((32, 128), F32)
        number = jnp.zeros((1, 128), F32)
        for place in range(4):
            device, at = 4 * x + t, 66 * ((place - block) % 4)
            tile = jnp.where(chunk == place, slots[device, at + 32 * view : at + 32 * view + 32, :], tile)
            row = slots[device, at + 64 + view : at + 65 + view, :]
            number = jnp.where(chunk[0:1] == place, row, number)
        values.append(tile)
        numbers.append(number)
    value = jnp.concatenate(values, axis=1)
    number = jnp.concatenate(numbers, axis=1)
    hot = (line == number).astype(BF16)
    left = jnp.concatenate([*split3(value), jnp.ones((16, 512), BF16)], axis=0)
    result = dot_nt(left, hot)
    data = result[0:32] + result[32:64] + result[64:96]
    for half in range(2):
        lanes = slice(128 * half, 128 * half + 128)
        to = slice(128 * x, 128 * x + 128)
        weight = weights[2 * block + half, view : view + 1, to]
        yield 2 * block + half, to, data[:, lanes], result[96:97, lanes] * weight


def scatter_kernel(slots, weights, data, cover):
    for column in range(8):
        for block, lanes, values, covered in scattered(1, slots, weights, column):
            data[block, :, lanes] = values
            cover[block, :, lanes] = jnp.broadcast_to(covered, (8, 128))


def payloads(value, far, near):
    upper = upper_half()
    far[...] = value[:, pl.ds(pl.multiple_of(16 * upper, 16), 16), :]
    near[...] = value[:, pl.ds(pl.multiple_of(16 - 16 * upper, 16), 16), :]


def at_end(planes):
    x, y, _, z = coordinates()
    slab = 2 * place_on_ring(x, y, z) + upper_half()
    return ((z == 0) & (slab == 0)) | ((z == planes - 1) & (slab == 7))


def widened(wide, value, far, near, margin):
    rows, upper = value.shape[1], upper_half()
    wide[:, margin : margin + rows, :] = value[...]
    side = margin + rows
    wide[:, pl.ds(pl.multiple_of(side * upper, 16), margin), :] = far
    wide[:, pl.ds(pl.multiple_of(side - side * upper, 16), margin), :] = near[...]


def blurred_into(wide, band, big_high, big_low, flat, total):
    rows = wide.shape[1] - 32
    weights = band[...]
    for column in range(8):
        for start in range(0, rows, 32):
            stacked = jnp.concatenate(split2(wide[column, start : start + 64, :]), axis=0)
            both = dot_nn(weights, stacked)
            at = column * rows + start
            flat[at : at + 32, :] = both[0:32] + both[32:64]
    high, low = split2(flat[...])

    for offset in (0, -2, -1, 1, 2):
        first, last = max(0, -offset), min(8, 8 - offset)
        start, stop = (first + offset) * rows, (last + offset) * rows
        size = stop - start
        both = jnp.concatenate([high[start:stop], low[start:stop]], axis=0)
        both = dot_nn(both, big_high[offset + 2])
        part = both[:size] + both[size:] + dot_nn(high[start:stop], big_low[offset + 2])
        if offset == 0:
            total[...] = part
        else:
            total[first * rows : last * rows, :] += part


def blur_kernel(est, far, near, band, big_high, big_low, blurred, wide, flat):
    widened(wide, est, far[...], near, 16)
    blurred_into(wide, band, big_high, big_low, flat, blurred)


def ratio_from(ratio, data, cover, blurred):
    for column in range(8):
        here = blurred[column * 32 : column * 32 + 32, :]
        ratio[column] = 1.0 + cover[column, 0:1, :] * (data[column] / here - 1.0)


def scatter_ratio_kernel(slots, weights, blurred, ratio):
    for column in range(8):
        for block, lanes, values, covered in scattered(0, slots, weights, column):
            here = blurred[32 * block : 32 * block + 32, lanes]
            ratio[block, :, lanes] = 1.0 + covered * (values / here - 1.0)


def update_kernel(planes, ratio, ratio_far, ratio_near, est, est_far, est_near, band, high, low, new, wide, flat, total):
    widened(wide, ratio, jnp.where(at_end(planes), 0.0, ratio_far[...]), ratio_near, 32)
    widened(new, est, est_far[...], est_near, 16)
    blurred_into(wide, band, high, low, flat, total)
    for column in range(8):
        new[column] = new[column] * total[column * 64 : column * 64 + 64, :]


def ratio_kernel(est, band, high, low, data, cover, ratio, far, near, flat, total):
    blurred_into(est, band, high, low, flat, total)
    ratio_from(ratio, data, cover, total)
    payloads(ratio, far, near)


def last_kernel(planes, ratio, far, near, band, big_high, big_low, est, *refs):
    (mine, other), pieces, (wide, flat, total) = refs[:2], refs[2:5], refs[5:]
    widened(wide, ratio, jnp.where(at_end(planes), 0.0, far[...]), near, 16)
    blurred_into(wide, band, big_high, big_low, flat, total)
    _, _, core, _ = coordinates()
    for flip, x, y, _ in chips():
        for turn in range(2):
            block = 4 * y + 2 * (core if turn == 0 else 1 - core)
            lanes = pl.ds(pl.multiple_of(128 * x, 128), 128)
            new = jnp.concatenate(
                [
                    est[block + half, 16:48, lanes]
                    * total[pl.ds(pl.multiple_of(32 * (block + half), 32), 32), lanes]
                    for half in range(2)
                ],
                axis=1,
            )
            if flip == 0:
                (mine, other)[turn][...] = new
            else:
                pieces[flip - 1][turn] = new


def join_kernel(*refs):
    pieces, others, (out, held, turned, left) = refs[:4], refs[4:8], refs[8:]
    upper = upper_half()
    for flip, _, _, place in chips():
        mine = pieces[flip][...] if flip == 0 else pieces[flip][0]
        held[pl.ds(pl.multiple_of(64 * place + 32 * upper, 32), 32), :] = mine
        held[pl.ds(pl.multiple_of(64 * place + 32 - 32 * upper, 32), 32), :] = others[flip][...]

    def store(part):
        return pltpu.make_async_copy(turned.at[:, part], out.at[:, part], left.at[part])

    for part in range(2):
        turned[:, part] = held[:, 128 * part : 128 * part + 128].T.reshape(16, 8, 256)
        store(part).start()
    for part in range(2):
        store(part).wait()


def shape(*dims, dtype=F32):
    return jax.ShapeDtypeStruct(dims, dtype)


def swaps(planes):
    def flipped(by):
        return [(d * planes + z, (d ^ by) * planes + z) for d in range(8) for z in range(planes)]

    return [flipped(by) for by in (2, 4, 6)], flipped(1)


def slab_sweep(planes, estimate, raw_lines, line_index, psf, view_weight):
    far_pairs, near_pairs = chain_pairs(planes)
    to_chips, to_core = swaps(planes)
    ends = sorted(set(range(8 * planes)) - {source for source, _ in far_pairs})
    ring_pairs = far_pairs + [tuple(ends), tuple(ends[::-1])]

    def exchange(far, near):
        return (
            lax.ppermute(far, ALL, far_pairs),
            lax.ppermute(near, ALL, near_pairs),
        )

    own, *away = call(
        est_kernel, (shape(72, 256),) * 4, [SMEM, VMEM], [pltpu.VMEM((256, 256), F32)]
    )(view_weight.reshape(2), estimate.reshape(16, 2, 8, 256))
    here = [own] + [lax.ppermute(piece, ALL, pairs) for piece, pairs in zip(away, to_chips)]
    there = [lax.ppermute(piece, ALL, to_core) for piece in here]

    anywhere = pl.BlockSpec(memory_space=pl.ANY)
    slots = call(
        functools.partial(lines_kernel, planes),
        shape(8, 66 * planes, 128),
        [anywhere, anywhere],
        [
            pltpu.VMEM((planes, 2, 4, 32, 256), F32),
            pltpu.VMEM((8, 128), jnp.int32),
            pltpu.VMEM((8, 66 * planes, 128), F32),
            pltpu.SemaphoreType.DMA((planes,)),
            pltpu.SemaphoreType.DMA((1,)),
            pltpu.SemaphoreType.DMA((planes,)),
        ],
        out_specs=anywhere,
        vmem=56,
    )(raw_lines.reshape(2, 4, planes, 32, 256), line_index.reshape(8, 128))
    slots = slots.reshape(8 * planes, 1, 66 * 128)
    slots = lax.all_to_all(slots, ALL, split_axis=0, concat_axis=0, tiled=True)
    slots = slots.reshape(8, 66 * planes, 128)
    half, full = shape(8, 16, 256), shape(8, 32, 256)

    def work(*dims):
        return pltpu.VMEM(dims, F32)

    est, weights, est_far, est_near = call(slab_kernel, (full, shape(8, 8, 256), half, half), [VMEM] * 8)(
        *here, *there
    )
    est_far = lax.ppermute(est_far, ALL, far_pairs)
    def matrices(view, way, after):
        big = shape(5, 256, 256, dtype=BF16)
        big_high, big_low, band = call(
            functools.partial(taps_kernel, view, way),
            (big, big, shape(64, 128, dtype=BF16)),
            [VMEM, anywhere],
            [work(8, 128)],
            flops=1 << 30,
        )(psf.transpose(1, 0, 2), after)
        return band, big_high, big_low

    blurred = call(
        blur_kernel, shape(256, 256), [VMEM] * 6, [work(8, 64, 256), work(256, 256)], flops=1 << 30
    )(est, est_far, est_near, *matrices(0, 0, est))
    ratio = call(scatter_ratio_kernel, full, [VMEM] * 3, flops=1 << 30)(slots, weights, blurred)
    data, cover = call(scatter_kernel, (full, shape(8, 8, 256)), [VMEM] * 2, flops=1 << 30)(slots, weights)
    est = call(
        functools.partial(update_kernel, planes),
        shape(8, 64, 256),
        [VMEM] * 9,
        [work(8, 96, 256), work(512, 256), work(512, 256)],
        flops=1 << 30,
    )(ratio, lax.ppermute(ratio, ALL, far_pairs), lax.ppermute(ratio, ALL, near_pairs), est, est_far, est_near, *matrices(0, 1, slots))
    ratio, far, near = call(
        ratio_kernel, (full, half, half), [VMEM] * 6, [work(256, 256), work(256, 256)], flops=1 << 30
    )(est, *matrices(1, 0, slots), data, cover)
    column, pair = shape(32, 256), shape(2, 32, 256)
    mine, other, *away = call(
        functools.partial(last_kernel, planes),
        (column, column, pair, pair, pair),
        [VMEM] * 7,
        [work(8, 64, 256), work(256, 256), work(256, 256)],
        flops=1 << 30,
    )(ratio, lax.ppermute(far, ALL, ring_pairs), lax.ppermute(near, ALL, near_pairs), *matrices(1, 1, ratio), est)
    away = [lax.ppermute(piece, ALL, pairs) for piece, pairs in zip(away, to_chips)]
    others = [lax.ppermute(piece, ALL, to_core) for piece in [other] + [piece[1] for piece in away]]
    out = call(
        join_kernel,
        shape(16, 2, 8, 256),
        [VMEM] * 8,
        [work(256, 256), work(16, 2, 8, 256), pltpu.SemaphoreType.DMA((2,))],
        out_specs=anywhere,
    )(mine, *away, *others)
    return out.reshape(16, 16, 256)


def padded(block, sides, width):
    for axis, dim in sides:
        count = lax.axis_size(axis)
        forward = [(i, i + 1) for i in range(count - 1)]
        backward = [(target, source) for source, target in forward]
        low = lax.ppermute(
            lax.slice_in_dim(block, block.shape[dim] - width, None, axis=dim), axis, forward
        )
        high = lax.ppermute(lax.slice_in_dim(block, 0, width, axis=dim), axis, backward)
        block = jnp.concatenate([low, block, high], axis=dim)
    return block


def band_matrix(taps, length):
    width = taps.shape[0]
    rows = lax.broadcasted_iota(jnp.int32, (length + width - 1, length), 0)
    cols = lax.broadcasted_iota(jnp.int32, (length + width - 1, length), 1)
    offset = rows - cols
    valid = (offset >= 0) & (offset < width)
    return jnp.where(valid, taps[jnp.clip(offset, 0, width - 1)], 0.0)


def along_x(extended, matrix_x):
    lead, size_y, size_z = extended.shape
    flat = extended.reshape(lead, size_y * size_z)
    result = jnp.dot(matrix_x.T, flat, precision=lax.Precision.HIGHEST)
    return result.reshape(matrix_x.shape[1], size_y, size_z)


def blur(field, taps):
    half_width = (taps.shape[1] - 1) // 2
    size_x, size_y, size_z = field.shape
    matrix_x = band_matrix(taps[0], size_x)
    matrix_y = band_matrix(taps[1], size_y)
    matrix_z = band_matrix(taps[2], size_z)
    highest = lax.Precision.HIGHEST
    extended = padded(field, (("gz", 2),), half_width)
    result = jnp.einsum("abj,jc->abc", extended, matrix_z, precision=highest)
    extended = padded(result, (("gy", 1),), half_width)
    result = jnp.einsum("ajc,jb->abc", extended, matrix_y, precision=highest)
    extended = padded(result, (("gx", 0),), half_width)
    result = along_x(extended, matrix_x)
    return result


def block_sweep(estimate, raw_lines, line_index, psf, view_weight):
    size_x, size_y, size_z = estimate.shape
    block_lines = size_x * size_y
    views = raw_lines.shape[0]
    group = lax.axis_size(("gy", "gz"))
    slots = line_index.shape[-1]
    capacity = slots // group
    lines = raw_lines.reshape(views, group, capacity, size_z)
    indices = line_index.reshape(views, group, capacity)
    lines, indices = (
        lax.all_to_all(lines, ("gy", "gz"), split_axis=1, concat_axis=1, tiled=True),
        lax.all_to_all(indices, ("gy", "gz"), split_axis=1, concat_axis=1, tiled=True),
    )
    est = estimate
    for view in range(views):
        flat_index = indices[view].reshape(-1)
        flat_lines = lines[view].reshape(-1, size_z)
        volume = (
            jnp.zeros((block_lines, size_z), jnp.float32)
            .at[flat_index]
            .set(flat_lines, mode="drop")
        )
        volume = volume.reshape(size_x, size_y, size_z)
        cover = jnp.zeros((block_lines,), jnp.float32).at[flat_index].set(1.0, mode="drop")
        cover = cover.reshape(size_x, size_y, 1)
        weight = view_weight[view].reshape(()).astype(jnp.float32) * 0.25
        taps = psf[view] / jnp.sum(psf[view], axis=1, keepdims=True)
        blurred = blur(est, taps)
        ratio = 1.0 + weight * cover * (volume / blurred - 1.0)
        est = est * blur(ratio, taps[:, ::-1])
    return est


def solution(mesh):
    placed = (
        P("gx", "gy", "gz"),
        P(None, "gx", ("gy", "gz"), None, None),
        P(None, "gx", ("gy", "gz"), None),
        P(),
        P(None, "gx", "gy", "gz"),
    )
    sizes = tuple(mesh.shape[axis] for axis in ALL)

    def on_device(estimate, raw_lines, line_index, psf, view_weight):
        capacity = line_index.shape[-1] // (sizes[1] * sizes[2])
        fits = (
            sizes == (2, 4, 4)
            and estimate.shape == (16, 16, 256)
            and raw_lines.shape[0] == 2
            and capacity == 32
            and psf.shape == (2, 3, 33)
        )
        plan = functools.partial(slab_sweep, sizes[2]) if fits else block_sweep
        return plan(estimate, raw_lines, line_index, psf, view_weight)

    return jax.shard_map(
        on_device, mesh=mesh, in_specs=placed, out_specs=P("gx", "gy", "gz"), check_vma=False
    )
```

```python
import functools

import jax
import jax.numpy as jnp
from jax import lax
from jax.experimental import pallas as pl
from jax.experimental.pallas import tpu as pltpu
from jax.sharding import PartitionSpec as P

F32, BF16 = jnp.float32, jnp.bfloat16
VMEM = pl.BlockSpec(memory_space=pltpu.VMEM)
SMEM = pl.BlockSpec(memory_space=pltpu.SMEM)
ALL = ("gx", "gy", "gz")


def ring_place(x, y, z):
    place = 2 * x + (x ^ y)
    return place if z % 2 == 0 else 3 - place


def slab_of(device, z):
    x, gy = device // 4, device % 4
    place = ring_place(x, gy // 2, z)
    return 2 * place + gy % 2


def chain_pairs(planes):
    order = []
    for z in range(planes):
        by_slab = sorted(range(8), key=lambda device: slab_of(device, z))
        order += [device * planes + z for device in by_slab]
    far, near = [], []
    for k in range(len(order) - 1):
        pair = (order[k], order[k + 1])
        (near if k % 2 == 0 else far).extend([pair, pair[::-1]])
    return far, near


def split2(value):
    high = value.astype(BF16)
    return high, (value - high.astype(F32)).astype(BF16)


def split3(value):
    high = value.astype(BF16)
    rest = value - high.astype(F32)
    middle = rest.astype(BF16)
    return high, middle, (rest - middle.astype(F32)).astype(BF16)


def dot_nn(a, b):
    return lax.dot_general(a, b, (((1,), (0,)), ((), ())), preferred_element_type=F32)


def dot_nt(a, b):
    return lax.dot_general(a, b, (((1,), (1,)), ((), ())), preferred_element_type=F32)


def call(kernel, out_shapes, in_specs, scratch=(), flops=0, out_specs=None, vmem=16):
    return pl.pallas_call(
        kernel,
        out_shape=out_shapes,
        in_specs=in_specs,
        out_specs=out_specs or jax.tree.map(lambda _: VMEM, out_shapes),
        scratch_shapes=list(scratch),
        compiler_params=pltpu.CompilerParams(vmem_limit_bytes=vmem * 1024 * 1024),
        cost_estimate=pl.CostEstimate(flops=flops, bytes_accessed=1 << 20, transcendentals=0),
    )


def coordinates():
    x, gy, z = (lax.axis_index(axis) for axis in ALL)
    y, core = gy // 2, lax.rem(gy, 2)
    return x, y, core, z


def place_on_ring(x, y, z):
    place = 2 * x + lax.rem(x + y, 2)
    return jnp.where(lax.rem(z, 2) == 0, place, 3 - place)


def upper_half():
    return coordinates()[2]


def chips():
    x, y, _, z = coordinates()
    for flip in range(4):
        other_x = 1 - x if flip // 2 else x
        other_y = 1 - y if flip % 2 else y
        yield flip, other_x, other_y, place_on_ring(other_x, other_y, z)


def est_kernel(weight, est, *refs):
    pieces, turned = refs[:4], refs[4]
    for half in range(2):
        turned[:, 128 * half : 128 * half + 128] = est[:, half].reshape(128, 256).T
    rows = lax.broadcasted_iota(jnp.int32, (8, 256), 0)
    weights = jnp.where(
        rows == 0,
        weight[0].astype(F32) * 0.25,
        jnp.where(rows == 1, weight[1].astype(F32) * 0.25, 0.0),
    )
    for flip, _, _, place in chips():
        pieces[flip][0:64, :] = turned[pl.ds(pl.multiple_of(place * 64, 64), 64), :]
        pieces[flip][64:72, :] = weights


def slab_kernel(*refs):
    pieces, (slab, weights, far, near) = refs[:8], refs[8:]
    _, _, core, _ = coordinates()
    upper = upper_half()
    for flip, x, y, _ in chips():
        for turn in range(2):
            piece = pieces[4 * turn + flip]
            block = 4 * y + 2 * (core if turn == 0 else 1 - core)
            lanes = pl.ds(pl.multiple_of(128 * x, 128), 128)
            for half in range(2):
                part = piece.at[:, 128 * half : 128 * half + 128]
                slab[block + half, :, lanes] = part[pl.ds(pl.multiple_of(32 * upper, 32), 32), :]
                weights[block + half, :, lanes] = part[64:72, :]
                far[block + half, :, lanes] = part[pl.ds(pl.multiple_of(48 * upper, 16), 16), :]
                near[block + half, :, lanes] = part[pl.ds(pl.multiple_of(32 - 16 * upper, 16), 16), :]


def lines_kernel(planes, raw, index, out, held, numbers, made, arrived, numbered, left):
    mine = lax.axis_index("gz")
    blocks = [lax.rem(place - mine + 4, 4) for place in range(4)]
    chunk = lax.broadcasted_iota(jnp.int32, (8, 128), 1) // 32
    rows = lax.broadcasted_iota(jnp.int32, (8, 128), 0)

    def load(z):
        return pltpu.make_async_copy(raw.at[:, :, z], held.at[z], arrived.at[z])

    def store(z):
        rows = pl.ds(64 * z, 64 if z < planes - 1 else 64 + 2 * planes)
        return pltpu.make_async_copy(made.at[:, rows], out.at[:, rows], left.at[z])

    load_numbers = pltpu.make_async_copy(index, numbers, numbered.at[0])
    for z in range(planes):
        load(z).start()
    load_numbers.start()
    for z in range(planes):
        load(z).wait()
        for view in range(2):
            lines = jnp.concatenate([held[z, view, block] for block in blocks], axis=0)
            turned = lines.T
            for device in range(8):
                slab = slab_of(device, z)
                at = 66 * z + 32 * view
                made[device, at : at + 32, :] = turned[slab * 32 : slab * 32 + 32, :]
        if z == 0:
            load_numbers.wait()
        both = jnp.zeros((8, 128), F32)
        for place, block in enumerate(blocks):
            for view in range(2):
                row = numbers[pl.ds(view * 4 + block, 1), :].astype(F32)
                row = pltpu.roll(jnp.broadcast_to(row, (8, 128)), (32 * (place - z)) % 128, 1)
                both = jnp.where((chunk == place) & (rows == view), row, both)
        for device in range(8):
            made[device, 66 * z + 64 : 66 * z + 66, :] = both[0:2, :]
        store(z).start()
    for z in range(planes):
        store(z).wait()


def taps_kernel(view, way, psf, _, big_high, big_low, band, held):
    held[...] = jnp.zeros_like(held)
    held[0:3, 0:33] = psf[:, view, :]
    taps = held[...]
    total = jnp.sum(taps, axis=1, keepdims=True)
    taps = taps / jnp.where(total == 0.0, 1.0, total)

    def toeplitz(row, size):
        wide = jnp.broadcast_to(row, (size, 128))
        return pltpu.roll(wide, 0, 1, stride=1, stride_axis=0)

    from_lane = lax.broadcasted_iota(jnp.int32, (128, 128), 0)
    to_lane = lax.broadcasted_iota(jnp.int32, (128, 128), 1)
    turn = (from_lane + to_lane == 32).astype(BF16)
    turned = sum(dot_nn(piece, turn) for piece in split3(taps))
    along_z, along_xy = (taps, turned) if way == 0 else (turned, taps)
    high, low = (part.astype(F32) for part in split2(toeplitz(along_z[2:3, :], 32)))
    band[0:32, :] = (high + pltpu.roll(high, 64, 1)).astype(BF16)
    band[32:64, :] = low.astype(BF16)
    from_row = lax.broadcasted_iota(jnp.int32, (128, 256), 0)
    to_lane = lax.broadcasted_iota(jnp.int32, (128, 256), 1)
    pick = (from_row == to_lane // 8 + 16).astype(BF16)
    rows_x = sum(dot_nn(piece, pick) for piece in split3(toeplitz(along_xy[0:1, :], 32)))
    wide_x = jnp.broadcast_to(rows_x[:, None, :], (32, 8, 256)).reshape(256, 256)
    small_y = split3(toeplitz(along_xy[1:2, :], 8))
    for offset in range(-2, 3):
        pick = (from_row == lax.rem(to_lane, 8) + 16 - 8 * offset).astype(BF16)
        rows_y = sum(dot_nn(piece, pick) for piece in small_y)
        wide_y = jnp.broadcast_to(rows_y[None], (32, 8, 256)).reshape(256, 256)
        big_high[offset + 2], big_low[offset + 2] = split2(wide_x * wide_y)


def scattered(view, slots, weights, column):
    chunk = lax.broadcasted_iota(jnp.int32, (32, 128), 1) // 32
    at = lax.broadcasted_iota(jnp.int32, (256, 512), 0)
    line = (lax.rem(at, 128) // 8 * 16 + at // 128 * 8 + lax.rem(at, 8)).astype(F32)
    x, block = column // 4, column % 4
    numbers, values = [], []
    for t in range(4):
        tile = jnp.zeros((32, 128), F32)
        number = jnp.zeros((1, 128), F32)
        for place in range(4):
            device, at = 4 * x + t, 66 * ((place - block) % 4)
            tile = jnp.where(chunk == place, slots[device, at + 32 * view : at + 32 * view + 32, :], tile)
            row = slots[device, at + 64 + view : at + 65 + view, :]
            number = jnp.where(chunk[0:1] == place, row, number)
        values.append(tile)
        numbers.append(number)
    value = jnp.concatenate(values, axis=1)
    number = jnp.concatenate(numbers, axis=1)
    hot = (line == number).astype(BF16)
    left = jnp.concatenate([*split3(value), jnp.ones((16, 512), BF16)], axis=0)
    result = dot_nt(left, hot)
    data = result[0:32] + result[32:64] + result[64:96]
    for half in range(2):
        lanes = slice(128 * half, 128 * half + 128)
        to = slice(128 * x, 128 * x + 128)
        weight = weights[2 * block + half, view : view + 1, to]
        yield 2 * block + half, to, data[:, lanes], result[96:97, lanes] * weight


def scatter_kernel(slots, weights, data, cover):
    for column in range(8):
        for block, lanes, values, covered in scattered(1, slots, weights, column):
            data[block, :, lanes] = values
            cover[block, :, lanes] = jnp.broadcast_to(covered, (8, 128))


def payloads(value, far, near):
    upper = upper_half()
    far[...] = value[:, pl.ds(pl.multiple_of(16 * upper, 16), 16), :]
    near[...] = value[:, pl.ds(pl.multiple_of(16 - 16 * upper, 16), 16), :]


def at_end(planes):
    x, y, _, z = coordinates()
    slab = 2 * place_on_ring(x, y, z) + upper_half()
    return ((z == 0) & (slab == 0)) | ((z == planes - 1) & (slab == 7))


def widened(wide, value, far, near, margin):
    rows, upper = value.shape[1], upper_half()
    wide[:, margin : margin + rows, :] = value[...]
    side = margin + rows
    wide[:, pl.ds(pl.multiple_of(side * upper, 16), margin), :] = far
    wide[:, pl.ds(pl.multiple_of(side - side * upper, 16), margin), :] = near[...]


def blurred_into(wide, band, big_high, big_low, flat, total):
    rows = wide.shape[1] - 32
    weights = band[...]
    for column in range(8):
        for start in range(0, rows, 32):
            stacked = jnp.concatenate(split2(wide[column, start : start + 64, :]), axis=0)
            both = dot_nn(weights, stacked)
            at = column * rows + start
            flat[at : at + 32, :] = both[0:32] + both[32:64]
    high, low = split2(flat[...])

    for offset in (0, -2, -1, 1, 2):
        first, last = max(0, -offset), min(8, 8 - offset)
        start, stop = (first + offset) * rows, (last + offset) * rows
        size = stop - start
        both = jnp.concatenate([high[start:stop], low[start:stop]], axis=0)
        both = dot_nn(both, big_high[offset + 2])
        part = both[:size] + both[size:] + dot_nn(high[start:stop], big_low[offset + 2])
        if offset == 0:
            total[...] = part
        else:
            total[first * rows : last * rows, :] += part


def blur_kernel(est, far, near, band, big_high, big_low, blurred, wide, flat):
    widened(wide, est, far[...], near, 16)
    blurred_into(wide, band, big_high, big_low, flat, blurred)


def ratio_from(ratio, data, cover, blurred):
    for column in range(8):
        here = blurred[column * 32 : column * 32 + 32, :]
        ratio[column] = 1.0 + cover[column, 0:1, :] * (data[column] / here - 1.0)


def scatter_ratio_kernel(slots, weights, blurred, ratio):
    for column in range(8):
        for block, lanes, values, covered in scattered(0, slots, weights, column):
            here = blurred[32 * block : 32 * block + 32, lanes]
            ratio[block, :, lanes] = 1.0 + covered * (values / here - 1.0)


def update_kernel(planes, ratio, ratio_far, ratio_near, est, est_far, est_near, band, high, low, new, wide, flat, total):
    widened(wide, ratio, jnp.where(at_end(planes), 0.0, ratio_far[...]), ratio_near, 32)
    widened(new, est, est_far[...], est_near, 16)
    blurred_into(wide, band, high, low, flat, total)
    for column in range(8):
        new[column] = new[column] * total[column * 64 : column * 64 + 64, :]


def ratio_kernel(est, band, high, low, data, cover, ratio, far, near, flat, total):
    blurred_into(est, band, high, low, flat, total)
    ratio_from(ratio, data, cover, total)
    payloads(ratio, far, near)


def last_kernel(planes, ratio, far, near, band, big_high, big_low, est, *refs):
    (mine, other), pieces, (wide, flat, total) = refs[:2], refs[2:6], refs[6:]
    widened(wide, ratio, jnp.where(at_end(planes), 0.0, far[...]), near, 16)
    blurred_into(wide, band, big_high, big_low, flat, total)
    _, _, core, _ = coordinates()
    for flip, x, y, _ in chips():
        for turn in range(2):
            block = 4 * y + 2 * (core if turn == 0 else 1 - core)
            lanes = pl.ds(pl.multiple_of(128 * x, 128), 128)
            new = jnp.concatenate(
                [
                    est[block + half, 16:48, lanes]
                    * total[pl.ds(pl.multiple_of(32 * (block + half), 32), 32), lanes]
                    for half in range(2)
                ],
                axis=1,
            )
            if flip == 0:
                (mine, other)[turn][...] = new
            elif flip == 3:
                pieces[2 + turn][...] = new
            else:
                pieces[flip - 1][turn] = new


def join_kernel(*refs):
    pieces, others, (out, held, turned, left) = refs[:4], refs[4:8], refs[8:]
    upper = upper_half()
    for flip, _, _, place in chips():
        mine = pieces[flip][0] if flip in (1, 2) else pieces[flip][...]
        held[pl.ds(pl.multiple_of(64 * place + 32 * upper, 32), 32), :] = mine
        held[pl.ds(pl.multiple_of(64 * place + 32 - 32 * upper, 32), 32), :] = others[flip][...]

    def store(part):
        return pltpu.make_async_copy(turned.at[:, part], out.at[:, part], left.at[part])

    for part in range(2):
        turned[:, part] = held[:, 128 * part : 128 * part + 128].T.reshape(16, 8, 256)
        store(part).start()
    for part in range(2):
        store(part).wait()


def shape(*dims, dtype=F32):
    return jax.ShapeDtypeStruct(dims, dtype)


def swaps(planes):
    def flipped(by):
        return [(d * planes + z, (d ^ by) * planes + z) for d in range(8) for z in range(planes)]

    return [flipped(by) for by in (2, 4, 6)], flipped(7), flipped(1)


def slab_sweep(planes, estimate, raw_lines, line_index, psf, view_weight):
    far_pairs, near_pairs = chain_pairs(planes)
    to_chips, to_far_core, to_core = swaps(planes)
    ends = sorted(set(range(8 * planes)) - {source for source, _ in far_pairs})
    ring_pairs = far_pairs + [tuple(ends), tuple(ends[::-1])]

    def exchange(far, near):
        return (
            lax.ppermute(far, ALL, far_pairs),
            lax.ppermute(near, ALL, near_pairs),
        )

    own, *away = call(
        est_kernel, (shape(72, 256),) * 4, [SMEM, VMEM], [pltpu.VMEM((256, 256), F32)]
    )(view_weight.reshape(2), estimate.reshape(16, 2, 8, 256))
    here = [own] + [lax.ppermute(piece, ALL, pairs) for piece, pairs in zip(away, to_chips)]
    there = [lax.ppermute(piece, ALL, to_core) for piece in here]

    anywhere = pl.BlockSpec(memory_space=pl.ANY)
    slots = call(
        functools.partial(lines_kernel, planes),
        shape(8, 66 * planes, 128),
        [anywhere, anywhere],
        [
            pltpu.VMEM((planes, 2, 4, 32, 256), F32),
            pltpu.VMEM((8, 128), jnp.int32),
            pltpu.VMEM((8, 66 * planes, 128), F32),
            pltpu.SemaphoreType.DMA((planes,)),
            pltpu.SemaphoreType.DMA((1,)),
            pltpu.SemaphoreType.DMA((planes,)),
        ],
        out_specs=anywhere,
        vmem=56,
    )(raw_lines.reshape(2, 4, planes, 32, 256), line_index.reshape(8, 128))
    slots = slots.reshape(8 * planes, 1, 66 * 128)
    slots = lax.all_to_all(slots, ALL, split_axis=0, concat_axis=0, tiled=True)
    slots = slots.reshape(8, 66 * planes, 128)
    half, full = shape(8, 16, 256), shape(8, 32, 256)

    def work(*dims):
        return pltpu.VMEM(dims, F32)

    est, weights, est_far, est_near = call(slab_kernel, (full, shape(8, 8, 256), half, half), [VMEM] * 8)(
        *here, *there
    )
    est_far = lax.ppermute(est_far, ALL, far_pairs)
    def matrices(view, way, after):
        big = shape(5, 256, 256, dtype=BF16)
        big_high, big_low, band = call(
            functools.partial(taps_kernel, view, way),
            (big, big, shape(64, 128, dtype=BF16)),
            [VMEM, anywhere],
            [work(8, 128)],
            flops=1 << 30,
        )(psf.transpose(1, 0, 2), after)
        return band, big_high, big_low

    blurred = call(
        blur_kernel, shape(256, 256), [VMEM] * 6, [work(8, 64, 256), work(256, 256)], flops=1 << 30
    )(est, est_far, est_near, *matrices(0, 0, est))
    ratio = call(scatter_ratio_kernel, full, [VMEM] * 3, flops=1 << 30)(slots, weights, blurred)
    data, cover = call(scatter_kernel, (full, shape(8, 8, 256)), [VMEM] * 2, flops=1 << 30)(slots, weights)
    est = call(
        functools.partial(update_kernel, planes),
        shape(8, 64, 256),
        [VMEM] * 9,
        [work(8, 96, 256), work(512, 256), work(512, 256)],
        flops=1 << 30,
    )(ratio, lax.ppermute(ratio, ALL, far_pairs), lax.ppermute(ratio, ALL, near_pairs), est, est_far, est_near, *matrices(0, 1, slots))
    ratio, far, near = call(
        ratio_kernel, (full, half, half), [VMEM] * 6, [work(256, 256), work(256, 256)], flops=1 << 30
    )(est, *matrices(1, 0, slots), data, cover)
    column, pair = shape(32, 256), shape(2, 32, 256)
    mine, other, *away = call(
        functools.partial(last_kernel, planes),
        (column, column, pair, pair, column, column),
        [VMEM] * 7,
        [work(8, 64, 256), work(256, 256), work(256, 256)],
        flops=1 << 30,
    )(ratio, lax.ppermute(far, ALL, ring_pairs), lax.ppermute(near, ALL, near_pairs), *matrices(1, 1, ratio), est)
    *away, last = [lax.ppermute(piece, ALL, pairs) for piece, pairs in zip(away, to_chips + [to_far_core])]
    others = [lax.ppermute(piece, ALL, to_core) for piece in [other] + [piece[1] for piece in away[:2]]]
    others.append(last)
    out = call(
        join_kernel,
        shape(16, 2, 8, 256),
        [VMEM] * 8,
        [work(256, 256), work(16, 2, 8, 256), pltpu.SemaphoreType.DMA((2,))],
        out_specs=anywhere,
    )(mine, *away, *others)
    return out.reshape(16, 16, 256)


def padded(block, sides, width):
    for axis, dim in sides:
        count = lax.axis_size(axis)
        forward = [(i, i + 1) for i in range(count - 1)]
        backward = [(target, source) for source, target in forward]
        low = lax.ppermute(
            lax.slice_in_dim(block, block.shape[dim] - width, None, axis=dim), axis, forward
        )
        high = lax.ppermute(lax.slice_in_dim(block, 0, width, axis=dim), axis, backward)
        block = jnp.concatenate([low, block, high], axis=dim)
    return block


def band_matrix(taps, length):
    width = taps.shape[0]
    rows = lax.broadcasted_iota(jnp.int32, (length + width - 1, length), 0)
    cols = lax.broadcasted_iota(jnp.int32, (length + width - 1, length), 1)
    offset = rows - cols
    valid = (offset >= 0) & (offset < width)
    return jnp.where(valid, taps[jnp.clip(offset, 0, width - 1)], 0.0)


def along_x(extended, matrix_x):
    lead, size_y, size_z = extended.shape
    flat = extended.reshape(lead, size_y * size_z)
    result = jnp.dot(matrix_x.T, flat, precision=lax.Precision.HIGHEST)
    return result.reshape(matrix_x.shape[1], size_y, size_z)


def blur(field, taps):
    half_width = (taps.shape[1] - 1) // 2
    size_x, size_y, size_z = field.shape
    matrix_x = band_matrix(taps[0], size_x)
    matrix_y = band_matrix(taps[1], size_y)
    matrix_z = band_matrix(taps[2], size_z)
    highest = lax.Precision.HIGHEST
    extended = padded(field, (("gz", 2),), half_width)
    result = jnp.einsum("abj,jc->abc", extended, matrix_z, precision=highest)
    extended = padded(result, (("gy", 1),), half_width)
    result = jnp.einsum("ajc,jb->abc", extended, matrix_y, precision=highest)
    extended = padded(result, (("gx", 0),), half_width)
    result = along_x(extended, matrix_x)
    return result


def block_sweep(estimate, raw_lines, line_index, psf, view_weight):
    size_x, size_y, size_z = estimate.shape
    block_lines = size_x * size_y
    views = raw_lines.shape[0]
    group = lax.axis_size(("gy", "gz"))
    slots = line_index.shape[-1]
    capacity = slots // group
    lines = raw_lines.reshape(views, group, capacity, size_z)
    indices = line_index.reshape(views, group, capacity)
    lines, indices = (
        lax.all_to_all(lines, ("gy", "gz"), split_axis=1, concat_axis=1, tiled=True),
        lax.all_to_all(indices, ("gy", "gz"), split_axis=1, concat_axis=1, tiled=True),
    )
    est = estimate
    for view in range(views):
        flat_index = indices[view].reshape(-1)
        flat_lines = lines[view].reshape(-1, size_z)
        volume = (
            jnp.zeros((block_lines, size_z), jnp.float32)
            .at[flat_index]
            .set(flat_lines, mode="drop")
        )
        volume = volume.reshape(size_x, size_y, size_z)
        cover = jnp.zeros((block_lines,), jnp.float32).at[flat_index].set(1.0, mode="drop")
        cover = cover.reshape(size_x, size_y, 1)
        weight = view_weight[view].reshape(()).astype(jnp.float32) * 0.25
        taps = psf[view] / jnp.sum(psf[view], axis=1, keepdims=True)
        blurred = blur(est, taps)
        ratio = 1.0 + weight * cover * (volume / blurred - 1.0)
        est = est * blur(ratio, taps[:, ::-1])
    return est


def solution(mesh):
    placed = (
        P("gx", "gy", "gz"),
        P(None, "gx", ("gy", "gz"), None, None),
        P(None, "gx", ("gy", "gz"), None),
        P(),
        P(None, "gx", "gy", "gz"),
    )
    sizes = tuple(mesh.shape[axis] for axis in ALL)

    def on_device(estimate, raw_lines, line_index, psf, view_weight):
        capacity = line_index.shape[-1] // (sizes[1] * sizes[2])
        fits = (
            sizes == (2, 4, 4)
            and estimate.shape == (16, 16, 256)
            and raw_lines.shape[0] == 2
            and capacity == 32
            and psf.shape == (2, 3, 33)
        )
        plan = functools.partial(slab_sweep, sizes[2]) if fits else block_sweep
        return plan(estimate, raw_lines, line_index, psf, view_weight)

    return jax.shard_map(
        on_device, mesh=mesh, in_specs=placed, out_specs=P("gx", "gy", "gz"), check_vma=False
    )
```

```python
import functools

import jax
import jax.numpy as jnp
from jax import lax
from jax.experimental import pallas as pl
from jax.experimental.pallas import tpu as pltpu
from jax.sharding import PartitionSpec as P

F32, BF16 = jnp.float32, jnp.bfloat16
VMEM = pl.BlockSpec(memory_space=pltpu.VMEM)
SMEM = pl.BlockSpec(memory_space=pltpu.SMEM)
ALL = ("gx", "gy", "gz")


def ring_place(x, y, z):
    place = 2 * x + (x ^ y)
    return place if z % 2 == 0 else 3 - place


def slab_of(device, z):
    x, gy = device // 4, device % 4
    place = ring_place(x, gy // 2, z)
    return 2 * place + gy % 2


def chain_pairs(planes):
    order = []
    for z in range(planes):
        by_slab = sorted(range(8), key=lambda device: slab_of(device, z))
        order += [device * planes + z for device in by_slab]
    far, near = [], []
    for k in range(len(order) - 1):
        pair = (order[k], order[k + 1])
        (near if k % 2 == 0 else far).extend([pair, pair[::-1]])
    return far, near


def split2(value):
    high = value.astype(BF16)
    return high, (value - high.astype(F32)).astype(BF16)


def split3(value):
    high = value.astype(BF16)
    rest = value - high.astype(F32)
    middle = rest.astype(BF16)
    return high, middle, (rest - middle.astype(F32)).astype(BF16)


def dot_nn(a, b):
    return lax.dot_general(a, b, (((1,), (0,)), ((), ())), preferred_element_type=F32)


def dot_nt(a, b):
    return lax.dot_general(a, b, (((1,), (1,)), ((), ())), preferred_element_type=F32)


def call(kernel, out_shapes, in_specs, scratch=(), flops=0, out_specs=None, vmem=16):
    return pl.pallas_call(
        kernel,
        out_shape=out_shapes,
        in_specs=in_specs,
        out_specs=out_specs or jax.tree.map(lambda _: VMEM, out_shapes),
        scratch_shapes=list(scratch),
        compiler_params=pltpu.CompilerParams(vmem_limit_bytes=vmem * 1024 * 1024),
        cost_estimate=pl.CostEstimate(flops=flops, bytes_accessed=1 << 20, transcendentals=0),
    )


def coordinates():
    x, gy, z = (lax.axis_index(axis) for axis in ALL)
    y, core = gy // 2, lax.rem(gy, 2)
    return x, y, core, z


def place_on_ring(x, y, z):
    place = 2 * x + lax.rem(x + y, 2)
    return jnp.where(lax.rem(z, 2) == 0, place, 3 - place)


def upper_half():
    return coordinates()[2]


def chips():
    x, y, _, z = coordinates()
    for flip in range(4):
        other_x = 1 - x if flip // 2 else x
        other_y = 1 - y if flip % 2 else y
        yield flip, other_x, other_y, place_on_ring(other_x, other_y, z)


def est_kernel(weight, est, *refs):
    pieces, turned = refs[:4], refs[4]
    for half in range(2):
        turned[:, 128 * half : 128 * half + 128] = est[:, half].reshape(128, 256).T
    rows = lax.broadcasted_iota(jnp.int32, (8, 256), 0)
    weights = jnp.where(
        rows == 0,
        weight[0].astype(F32) * 0.25,
        jnp.where(rows == 1, weight[1].astype(F32) * 0.25, 0.0),
    )
    for flip, _, _, place in chips():
        pieces[flip][0:64, :] = turned[pl.ds(pl.multiple_of(place * 64, 64), 64), :]
        pieces[flip][64:72, :] = weights


def slab_kernel(*refs):
    pieces, (slab, weights, far, near) = refs[:8], refs[8:]
    _, _, core, _ = coordinates()
    upper = upper_half()
    for flip, x, y, _ in chips():
        for turn in range(2):
            piece = pieces[4 * turn + flip]
            block = 4 * y + 2 * (core if turn == 0 else 1 - core)
            lanes = pl.ds(pl.multiple_of(128 * x, 128), 128)
            for half in range(2):
                part = piece.at[:, 128 * half : 128 * half + 128]
                slab[block + half, :, lanes] = part[pl.ds(pl.multiple_of(32 * upper, 32), 32), :]
                weights[block + half, :, lanes] = part[64:72, :]
                far[block + half, :, lanes] = part[pl.ds(pl.multiple_of(48 * upper, 16), 16), :]
                near[block + half, :, lanes] = part[pl.ds(pl.multiple_of(32 - 16 * upper, 16), 16), :]


def lines_kernel(planes, raw, index, out, held, numbers, made, arrived, numbered, left):
    mine = lax.axis_index("gz")
    blocks = [lax.rem(place - mine + 4, 4) for place in range(4)]
    chunk = lax.broadcasted_iota(jnp.int32, (8, 128), 1) // 32
    rows = lax.broadcasted_iota(jnp.int32, (8, 128), 0)

    def load(z):
        return pltpu.make_async_copy(raw.at[:, :, z], held.at[z], arrived.at[z])

    def store(z):
        rows = pl.ds(64 * z, 64 if z < planes - 1 else 64 + 2 * planes)
        return pltpu.make_async_copy(made.at[:, rows], out.at[:, rows], left.at[z])

    load_numbers = pltpu.make_async_copy(index, numbers, numbered.at[0])
    for z in range(planes):
        load(z).start()
    load_numbers.start()
    for z in range(planes):
        load(z).wait()
        for view in range(2):
            lines = jnp.concatenate([held[z, view, block] for block in blocks], axis=0)
            turned = lines.T
            for device in range(8):
                slab = slab_of(device, z)
                at = 66 * z + 32 * view
                made[device, at : at + 32, :] = turned[slab * 32 : slab * 32 + 32, :]
        if z == 0:
            load_numbers.wait()
        both = jnp.zeros((8, 128), F32)
        for place, block in enumerate(blocks):
            for view in range(2):
                row = numbers[pl.ds(view * 4 + block, 1), :].astype(F32)
                row = pltpu.roll(jnp.broadcast_to(row, (8, 128)), (32 * (place - z)) % 128, 1)
                both = jnp.where((chunk == place) & (rows == view), row, both)
        for device in range(8):
            made[device, 66 * z + 64 : 66 * z + 66, :] = both[0:2, :]
        store(z).start()
    for z in range(planes):
        store(z).wait()


def taps_kernel(view, way, psf, _, big_high, big_low, band, held):
    held[...] = jnp.zeros_like(held)
    held[0:3, 0:33] = psf[:, view, :]
    taps = held[...]
    total = jnp.sum(taps, axis=1, keepdims=True)
    taps = taps / jnp.where(total == 0.0, 1.0, total)

    def toeplitz(row, size):
        wide = jnp.broadcast_to(row, (size, 128))
        return pltpu.roll(wide, 0, 1, stride=1, stride_axis=0)

    from_lane = lax.broadcasted_iota(jnp.int32, (128, 128), 0)
    to_lane = lax.broadcasted_iota(jnp.int32, (128, 128), 1)
    turn = (from_lane + to_lane == 32).astype(BF16)
    turned = sum(dot_nn(piece, turn) for piece in split3(taps))
    along_z, along_xy = (taps, turned) if way == 0 else (turned, taps)
    high, low = (part.astype(F32) for part in split2(toeplitz(along_z[2:3, :], 32)))
    band[0:32, :] = (high + pltpu.roll(high, 64, 1)).astype(BF16)
    band[32:64, :] = low.astype(BF16)
    from_row = lax.broadcasted_iota(jnp.int32, (128, 256), 0)
    to_lane = lax.broadcasted_iota(jnp.int32, (128, 256), 1)
    pick = (from_row == to_lane // 8 + 16).astype(BF16)
    rows_x = sum(dot_nn(piece, pick) for piece in split3(toeplitz(along_xy[0:1, :], 32)))
    wide_x = jnp.broadcast_to(rows_x[:, None, :], (32, 8, 256)).reshape(256, 256)
    small_y = split3(toeplitz(along_xy[1:2, :], 8))
    for offset in range(-2, 3):
        pick = (from_row == lax.rem(to_lane, 8) + 16 - 8 * offset).astype(BF16)
        rows_y = sum(dot_nn(piece, pick) for piece in small_y)
        wide_y = jnp.broadcast_to(rows_y[None], (32, 8, 256)).reshape(256, 256)
        big_high[offset + 2], big_low[offset + 2] = split2(wide_x * wide_y)


def scattered(view, slots, weights, column):
    chunk = lax.broadcasted_iota(jnp.int32, (32, 128), 1) // 32
    at = lax.broadcasted_iota(jnp.int32, (256, 512), 0)
    line = (lax.rem(at, 128) // 8 * 16 + at // 128 * 8 + lax.rem(at, 8)).astype(F32)
    x, block = column // 4, column % 4
    numbers, values = [], []
    for t in range(4):
        tile = jnp.zeros((32, 128), F32)
        number = jnp.zeros((1, 128), F32)
        for place in range(4):
            device, at = 4 * x + t, 66 * ((place - block) % 4)
            tile = jnp.where(chunk == place, slots[device, at + 32 * view : at + 32 * view + 32, :], tile)
            row = slots[device, at + 64 + view : at + 65 + view, :]
            number = jnp.where(chunk[0:1] == place, row, number)
        values.append(tile)
        numbers.append(number)
    value = jnp.concatenate(values, axis=1)
    number = jnp.concatenate(numbers, axis=1)
    hot = (line == number).astype(BF16)
    left = jnp.concatenate([*split3(value), jnp.ones((16, 512), BF16)], axis=0)
    result = dot_nt(left, hot)
    data = result[0:32] + result[32:64] + result[64:96]
    for half in range(2):
        lanes = slice(128 * half, 128 * half + 128)
        to = slice(128 * x, 128 * x + 128)
        weight = weights[2 * block + half, view : view + 1, to]
        yield 2 * block + half, to, data[:, lanes], result[96:97, lanes] * weight


def scatter_kernel(slots, weights, data, cover):
    for column in range(8):
        for block, lanes, values, covered in scattered(1, slots, weights, column):
            data[block, :, lanes] = values
            cover[block, :, lanes] = jnp.broadcast_to(covered, (8, 128))


def payloads(value, far, near):
    upper = upper_half()
    far[...] = value[:, pl.ds(pl.multiple_of(16 * upper, 16), 16), :]
    near[...] = value[:, pl.ds(pl.multiple_of(16 - 16 * upper, 16), 16), :]


def at_end(planes):
    x, y, _, z = coordinates()
    slab = 2 * place_on_ring(x, y, z) + upper_half()
    return ((z == 0) & (slab == 0)) | ((z == planes - 1) & (slab == 7))


def widened(wide, value, far, near, margin):
    rows, upper = value.shape[1], upper_half()
    wide[:, margin : margin + rows, :] = value[...]
    side = margin + rows
    wide[:, pl.ds(pl.multiple_of(side * upper, 16), margin), :] = far
    wide[:, pl.ds(pl.multiple_of(side - side * upper, 16), margin), :] = near[...]


def blurred_into(wide, band, big_high, big_low, flat, total):
    rows = wide.shape[1] - 32
    weights = band[...]
    for column in range(8):
        for start in range(0, rows, 32):
            stacked = jnp.concatenate(split2(wide[column, start : start + 64, :]), axis=0)
            both = dot_nn(weights, stacked)
            at = column * rows + start
            flat[at : at + 32, :] = both[0:32] + both[32:64]
    high, low = split2(flat[...])

    for offset in (0, -2, -1, 1, 2):
        first, last = max(0, -offset), min(8, 8 - offset)
        start, stop = (first + offset) * rows, (last + offset) * rows
        size = stop - start
        both = jnp.concatenate([high[start:stop], low[start:stop]], axis=0)
        both = dot_nn(both, big_high[offset + 2])
        part = both[:size] + both[size:] + dot_nn(high[start:stop], big_low[offset + 2])
        if offset == 0:
            total[...] = part
        else:
            total[first * rows : last * rows, :] += part


def blur_kernel(est, far, near, band, big_high, big_low, blurred, wide, flat):
    widened(wide, est, far[...], near, 16)
    blurred_into(wide, band, big_high, big_low, flat, blurred)


def ratio_from(ratio, data, cover, blurred):
    for column in range(8):
        here = blurred[column * 32 : column * 32 + 32, :]
        ratio[column] = 1.0 + cover[column, 0:1, :] * (data[column] / here - 1.0)


def scatter_ratio_kernel(slots, weights, blurred, ratio):
    for column in range(8):
        for block, lanes, values, covered in scattered(0, slots, weights, column):
            here = blurred[32 * block : 32 * block + 32, lanes]
            ratio[block, :, lanes] = 1.0 + covered * (values / here - 1.0)


def update_kernel(planes, ratio, ratio_far, ratio_near, est, est_far, est_near, band, high, low, new, wide, flat, total):
    widened(wide, ratio, jnp.where(at_end(planes), 0.0, ratio_far[...]), ratio_near, 32)
    widened(new, est, est_far[...], est_near, 16)
    blurred_into(wide, band, high, low, flat, total)
    for column in range(8):
        new[column] = new[column] * total[column * 64 : column * 64 + 64, :]


def ratio_kernel(est, band, high, low, data, cover, ratio, far, near, flat, total):
    blurred_into(est, band, high, low, flat, total)
    ratio_from(ratio, data, cover, total)
    payloads(ratio, far, near)


def last_kernel(planes, ratio, far, near, band, big_high, big_low, est, *refs):
    (mine, other), pieces, (wide, flat, total) = refs[:2], refs[2:6], refs[6:]
    widened(wide, ratio, jnp.where(at_end(planes), 0.0, far[...]), near, 16)
    blurred_into(wide, band, big_high, big_low, flat, total)
    _, _, core, _ = coordinates()
    for flip, x, y, _ in chips():
        for turn in range(2):
            block = 4 * y + 2 * (core if turn == 0 else 1 - core)
            lanes = pl.ds(pl.multiple_of(128 * x, 128), 128)
            new = jnp.concatenate(
                [
                    est[block + half, 16:48, lanes]
                    * total[pl.ds(pl.multiple_of(32 * (block + half), 32), 32), lanes]
                    for half in range(2)
                ],
                axis=1,
            )
            if flip == 0:
                (mine, other)[turn][...] = new
            elif flip == 3:
                pieces[2 + turn][...] = new
            else:
                pieces[flip - 1][turn] = new


def join_kernel(*refs):
    pieces, others, (out, held, turned, left) = refs[:4], refs[4:8], refs[8:]
    upper = upper_half()
    for flip, _, _, place in chips():
        mine = pieces[flip][0] if flip in (1, 2) else pieces[flip][...]
        held[pl.ds(pl.multiple_of(64 * place + 32 * upper, 32), 32), :] = mine
        held[pl.ds(pl.multiple_of(64 * place + 32 - 32 * upper, 32), 32), :] = others[flip][...]

    def store(part):
        return pltpu.make_async_copy(turned.at[:, part], out.at[:, part], left.at[part])

    for part in range(2):
        turned[:, part] = held[:, 128 * part : 128 * part + 128].T.reshape(16, 8, 256)
        store(part).start()
    for part in range(2):
        store(part).wait()


def shape(*dims, dtype=F32):
    return jax.ShapeDtypeStruct(dims, dtype)


def swaps(planes):
    def flipped(by):
        return [(d * planes + z, (d ^ by) * planes + z) for d in range(8) for z in range(planes)]

    return [flipped(by) for by in (2, 4, 6)], flipped(7), flipped(1)


def slab_sweep(planes, estimate, raw_lines, line_index, psf, view_weight):
    far_pairs, near_pairs = chain_pairs(planes)
    to_chips, to_far_core, to_core = swaps(planes)
    ends = sorted(set(range(8 * planes)) - {source for source, _ in far_pairs})
    ring_pairs = far_pairs + [tuple(ends), tuple(ends[::-1])]

    def exchange(far, near):
        return (
            lax.ppermute(far, ALL, far_pairs),
            lax.ppermute(near, ALL, near_pairs),
        )

    own, *away = call(
        est_kernel, (shape(72, 256),) * 4, [SMEM, VMEM], [pltpu.VMEM((256, 256), F32)]
    )(view_weight.reshape(2), estimate.reshape(16, 2, 8, 256))
    here = [own] + [lax.ppermute(piece, ALL, pairs) for piece, pairs in zip(away, to_chips)]
    there = [lax.ppermute(piece, ALL, to_core) for piece in here]

    anywhere = pl.BlockSpec(memory_space=pl.ANY)
    slots = call(
        functools.partial(lines_kernel, planes),
        shape(8, 66 * planes, 128),
        [anywhere, anywhere],
        [
            pltpu.VMEM((planes, 2, 4, 32, 256), F32),
            pltpu.VMEM((8, 128), jnp.int32),
            pltpu.VMEM((8, 66 * planes, 128), F32),
            pltpu.SemaphoreType.DMA((planes,)),
            pltpu.SemaphoreType.DMA((1,)),
            pltpu.SemaphoreType.DMA((planes,)),
        ],
        out_specs=anywhere,
        vmem=56,
    )(raw_lines.reshape(2, 4, planes, 32, 256), line_index.reshape(8, 128))
    slots = slots.reshape(8 * planes, 1, 66 * 128)
    slots = lax.all_to_all(slots, ALL, split_axis=0, concat_axis=0, tiled=True)
    slots = slots.reshape(8, 66 * planes, 128)
    half, full = shape(8, 16, 256), shape(8, 32, 256)

    def work(*dims):
        return pltpu.VMEM(dims, F32)

    est, weights, est_far, est_near = call(slab_kernel, (full, shape(8, 8, 256), half, half), [VMEM] * 8)(
        *here, *there
    )
    est_far = lax.ppermute(est_far, ALL, far_pairs)
    def matrices(view, way, after):
        big = shape(5, 256, 256, dtype=BF16)
        big_high, big_low, band = call(
            functools.partial(taps_kernel, view, way),
            (big, big, shape(64, 128, dtype=BF16)),
            [VMEM, anywhere],
            [work(8, 128)],
            flops=1 << 30,
        )(psf.transpose(1, 0, 2), after)
        return band, big_high, big_low

    blurred = call(
        blur_kernel, shape(256, 256), [VMEM] * 6, [work(8, 64, 256), work(256, 256)], flops=1 << 30
    )(est, est_far, est_near, *matrices(0, 0, est))
    ratio = call(scatter_ratio_kernel, full, [VMEM] * 3, flops=1 << 30)(slots, weights, blurred)
    data, cover = call(scatter_kernel, (full, shape(8, 8, 256)), [VMEM] * 2, flops=1 << 30)(slots, weights)
    est = call(
        functools.partial(update_kernel, planes),
        shape(8, 64, 256),
        [VMEM] * 9,
        [work(8, 96, 256), work(512, 256), work(512, 256)],
        flops=1 << 30,
    )(ratio, lax.ppermute(ratio, ALL, far_pairs), lax.ppermute(ratio, ALL, near_pairs), est, est_far, est_near, *matrices(0, 1, slots))
    ratio, far, near = call(
        ratio_kernel, (full, half, half), [VMEM] * 6, [work(256, 256), work(256, 256)], flops=1 << 30
    )(est, *matrices(1, 0, slots), data, cover)
    column, pair = shape(32, 256), shape(2, 32, 256)
    mine, other, *away = call(
        functools.partial(last_kernel, planes),
        (column, column, pair, pair, column, column),
        [VMEM] * 7,
        [work(8, 64, 256), work(256, 256), work(256, 256)],
        flops=1 << 30,
    )(ratio, lax.ppermute(far, ALL, ring_pairs), lax.ppermute(near, ALL, near_pairs), *matrices(1, 1, ratio), est)
    *away, last = [lax.ppermute(piece, ALL, pairs) for piece, pairs in zip(away, to_chips + [to_far_core])]
    first = lax.ppermute(jnp.stack([other, away[0][1]]), ALL, to_core)
    others = [first[0], first[1], lax.ppermute(away[1][1], ALL, to_core), last]
    out = call(
        join_kernel,
        shape(16, 2, 8, 256),
        [VMEM] * 8,
        [work(256, 256), work(16, 2, 8, 256), pltpu.SemaphoreType.DMA((2,))],
        out_specs=anywhere,
    )(mine, *away, *others)
    return out.reshape(16, 16, 256)


def padded(block, sides, width):
    for axis, dim in sides:
        count = lax.axis_size(axis)
        forward = [(i, i + 1) for i in range(count - 1)]
        backward = [(target, source) for source, target in forward]
        low = lax.ppermute(
            lax.slice_in_dim(block, block.shape[dim] - width, None, axis=dim), axis, forward
        )
        high = lax.ppermute(lax.slice_in_dim(block, 0, width, axis=dim), axis, backward)
        block = jnp.concatenate([low, block, high], axis=dim)
    return block


def band_matrix(taps, length):
    width = taps.shape[0]
    rows = lax.broadcasted_iota(jnp.int32, (length + width - 1, length), 0)
    cols = lax.broadcasted_iota(jnp.int32, (length + width - 1, length), 1)
    offset = rows - cols
    valid = (offset >= 0) & (offset < width)
    return jnp.where(valid, taps[jnp.clip(offset, 0, width - 1)], 0.0)


def along_x(extended, matrix_x):
    lead, size_y, size_z = extended.shape
    flat = extended.reshape(lead, size_y * size_z)
    result = jnp.dot(matrix_x.T, flat, precision=lax.Precision.HIGHEST)
    return result.reshape(matrix_x.shape[1], size_y, size_z)


def blur(field, taps):
    half_width = (taps.shape[1] - 1) // 2
    size_x, size_y, size_z = field.shape
    matrix_x = band_matrix(taps[0], size_x)
    matrix_y = band_matrix(taps[1], size_y)
    matrix_z = band_matrix(taps[2], size_z)
    highest = lax.Precision.HIGHEST
    extended = padded(field, (("gz", 2),), half_width)
    result = jnp.einsum("abj,jc->abc", extended, matrix_z, precision=highest)
    extended = padded(result, (("gy", 1),), half_width)
    result = jnp.einsum("ajc,jb->abc", extended, matrix_y, precision=highest)
    extended = padded(result, (("gx", 0),), half_width)
    result = along_x(extended, matrix_x)
    return result


def block_sweep(estimate, raw_lines, line_index, psf, view_weight):
    size_x, size_y, size_z = estimate.shape
    block_lines = size_x * size_y
    views = raw_lines.shape[0]
    group = lax.axis_size(("gy", "gz"))
    slots = line_index.shape[-1]
    capacity = slots // group
    lines = raw_lines.reshape(views, group, capacity, size_z)
    indices = line_index.reshape(views, group, capacity)
    lines, indices = (
        lax.all_to_all(lines, ("gy", "gz"), split_axis=1, concat_axis=1, tiled=True),
        lax.all_to_all(indices, ("gy", "gz"), split_axis=1, concat_axis=1, tiled=True),
    )
    est = estimate
    for view in range(views):
        flat_index = indices[view].reshape(-1)
        flat_lines = lines[view].reshape(-1, size_z)
        volume = (
            jnp.zeros((block_lines, size_z), jnp.float32)
            .at[flat_index]
            .set(flat_lines, mode="drop")
        )
        volume = volume.reshape(size_x, size_y, size_z)
        cover = jnp.zeros((block_lines,), jnp.float32).at[flat_index].set(1.0, mode="drop")
        cover = cover.reshape(size_x, size_y, 1)
        weight = view_weight[view].reshape(()).astype(jnp.float32) * 0.25
        taps = psf[view] / jnp.sum(psf[view], axis=1, keepdims=True)
        blurred = blur(est, taps)
        ratio = 1.0 + weight * cover * (volume / blurred - 1.0)
        est = est * blur(ratio, taps[:, ::-1])
    return est


def solution(mesh):
    placed = (
        P("gx", "gy", "gz"),
        P(None, "gx", ("gy", "gz"), None, None),
        P(None, "gx", ("gy", "gz"), None),
        P(),
        P(None, "gx", "gy", "gz"),
    )
    sizes = tuple(mesh.shape[axis] for axis in ALL)

    def on_device(estimate, raw_lines, line_index, psf, view_weight):
        capacity = line_index.shape[-1] // (sizes[1] * sizes[2])
        fits = (
            sizes == (2, 4, 4)
            and estimate.shape == (16, 16, 256)
            and raw_lines.shape[0] == 2
            and capacity == 32
            and psf.shape == (2, 3, 33)
        )
        plan = functools.partial(slab_sweep, sizes[2]) if fits else block_sweep
        return plan(estimate, raw_lines, line_index, psf, view_weight)

    return jax.shard_map(
        on_device, mesh=mesh, in_specs=placed, out_specs=P("gx", "gy", "gz"), check_vma=False
    )
```

```python
import functools

import jax
import jax.numpy as jnp
from jax import lax
from jax.experimental import pallas as pl
from jax.experimental.pallas import tpu as pltpu
from jax.sharding import PartitionSpec as P

F32, BF16 = jnp.float32, jnp.bfloat16
VMEM = pl.BlockSpec(memory_space=pltpu.VMEM)
SMEM = pl.BlockSpec(memory_space=pltpu.SMEM)
ALL = ("gx", "gy", "gz")


def ring_place(x, y, z):
    place = 2 * x + (x ^ y)
    return place if z % 2 == 0 else 3 - place


def slab_of(device, z):
    x, gy = device // 4, device % 4
    place = ring_place(x, gy // 2, z)
    return 2 * place + gy % 2


def chain_pairs(planes):
    order = []
    for z in range(planes):
        by_slab = sorted(range(8), key=lambda device: slab_of(device, z))
        order += [device * planes + z for device in by_slab]
    far, near = [], []
    for k in range(len(order) - 1):
        pair = (order[k], order[k + 1])
        (near if k % 2 == 0 else far).extend([pair, pair[::-1]])
    return far, near


def split2(value):
    high = value.astype(BF16)
    return high, (value - high.astype(F32)).astype(BF16)


def split3(value):
    high = value.astype(BF16)
    rest = value - high.astype(F32)
    middle = rest.astype(BF16)
    return high, middle, (rest - middle.astype(F32)).astype(BF16)


def dot_nn(a, b):
    return lax.dot_general(a, b, (((1,), (0,)), ((), ())), preferred_element_type=F32)


def dot_nt(a, b):
    return lax.dot_general(a, b, (((1,), (1,)), ((), ())), preferred_element_type=F32)


def call(kernel, out_shapes, in_specs, scratch=(), flops=0, out_specs=None, vmem=16):
    return pl.pallas_call(
        kernel,
        out_shape=out_shapes,
        in_specs=in_specs,
        out_specs=out_specs or jax.tree.map(lambda _: VMEM, out_shapes),
        scratch_shapes=list(scratch),
        compiler_params=pltpu.CompilerParams(vmem_limit_bytes=vmem * 1024 * 1024),
        cost_estimate=pl.CostEstimate(flops=flops, bytes_accessed=1 << 20, transcendentals=0),
    )


def coordinates():
    x, gy, z = (lax.axis_index(axis) for axis in ALL)
    y, core = gy // 2, lax.rem(gy, 2)
    return x, y, core, z


def place_on_ring(x, y, z):
    place = 2 * x + lax.rem(x + y, 2)
    return jnp.where(lax.rem(z, 2) == 0, place, 3 - place)


def upper_half():
    return coordinates()[2]


def chips():
    x, y, _, z = coordinates()
    for flip in range(4):
        other_x = 1 - x if flip // 2 else x
        other_y = 1 - y if flip % 2 else y
        yield flip, other_x, other_y, place_on_ring(other_x, other_y, z)


def est_kernel(weight, est, *refs):
    pieces, turned = refs[:4], refs[4]
    for half in range(2):
        turned[:, 128 * half : 128 * half + 128] = est[:, half].reshape(128, 256).T
    rows = lax.broadcasted_iota(jnp.int32, (8, 256), 0)
    weights = jnp.where(
        rows == 0,
        weight[0].astype(F32) * 0.25,
        jnp.where(rows == 1, weight[1].astype(F32) * 0.25, 0.0),
    )
    for flip, _, _, place in chips():
        pieces[flip][0:64, :] = turned[pl.ds(pl.multiple_of(place * 64, 64), 64), :]
        pieces[flip][64:72, :] = weights


def slab_kernel(*refs):
    pieces, (slab, weights, far, near) = refs[:8], refs[8:]
    _, _, core, _ = coordinates()
    upper = upper_half()
    for flip, x, y, _ in chips():
        for turn in range(2):
            piece = pieces[4 * turn + flip]
            block = 4 * y + 2 * (core if turn == 0 else 1 - core)
            lanes = pl.ds(pl.multiple_of(128 * x, 128), 128)
            for half in range(2):
                part = piece.at[:, 128 * half : 128 * half + 128]
                slab[block + half, :, lanes] = part[pl.ds(pl.multiple_of(32 * upper, 32), 32), :]
                weights[block + half, :, lanes] = part[64:72, :]
                far[block + half, :, lanes] = part[pl.ds(pl.multiple_of(48 * upper, 16), 16), :]
                near[block + half, :, lanes] = part[pl.ds(pl.multiple_of(32 - 16 * upper, 16), 16), :]


def lines_kernel(planes, raw, index, out, held, numbers, made, arrived, numbered, left):
    mine = lax.axis_index("gz")
    blocks = [lax.rem(place - mine + 4, 4) for place in range(4)]
    chunk = lax.broadcasted_iota(jnp.int32, (8, 128), 1) // 32
    rows = lax.broadcasted_iota(jnp.int32, (8, 128), 0)

    def load(z):
        some = pl.ds(0, 1) if z == 0 else pl.ds(1, planes - 1)
        return pltpu.make_async_copy(raw.at[:, :, some], held.at[:, :, some], arrived.at[z])

    def store(z):
        rows = pl.ds(64 * z, 64 if z < planes - 1 else 64 + 2 * planes)
        return pltpu.make_async_copy(made.at[:, rows], out.at[:, rows], left.at[z])

    load_numbers = pltpu.make_async_copy(index, numbers, numbered.at[0])
    load(0).start()
    load(1).start()
    load_numbers.start()
    for z in range(planes):
        if z < 2:
            load(z).wait()
        for view in range(2):
            lines = jnp.concatenate([held[view, block, z] for block in blocks], axis=0)
            turned = lines.T
            for device in range(8):
                slab = slab_of(device, z)
                at = 66 * z + 32 * view
                made[device, at : at + 32, :] = turned[slab * 32 : slab * 32 + 32, :]
        if z == 0:
            load_numbers.wait()
        both = jnp.zeros((8, 128), F32)
        for place, block in enumerate(blocks):
            for view in range(2):
                row = numbers[pl.ds(view * 4 + block, 1), :].astype(F32)
                row = pltpu.roll(jnp.broadcast_to(row, (8, 128)), (32 * (place - z)) % 128, 1)
                both = jnp.where((chunk == place) & (rows == view), row, both)
        for device in range(8):
            made[device, 66 * z + 64 : 66 * z + 66, :] = both[0:2, :]
        store(z).start()
    for z in range(planes):
        store(z).wait()


def taps_kernel(view, way, psf, _, big_high, big_low, band, held):
    held[...] = jnp.zeros_like(held)
    held[0:3, 0:33] = psf[:, view, :]
    taps = held[...]
    total = jnp.sum(taps, axis=1, keepdims=True)
    taps = taps / jnp.where(total == 0.0, 1.0, total)

    def toeplitz(row, size):
        wide = jnp.broadcast_to(row, (size, 128))
        return pltpu.roll(wide, 0, 1, stride=1, stride_axis=0)

    from_lane = lax.broadcasted_iota(jnp.int32, (128, 128), 0)
    to_lane = lax.broadcasted_iota(jnp.int32, (128, 128), 1)
    turn = (from_lane + to_lane == 32).astype(BF16)
    turned = sum(dot_nn(piece, turn) for piece in split3(taps))
    along_z, along_xy = (taps, turned) if way == 0 else (turned, taps)
    high, low = (part.astype(F32) for part in split2(toeplitz(along_z[2:3, :], 32)))
    band[0:32, :] = (high + pltpu.roll(high, 64, 1)).astype(BF16)
    band[32:64, :] = low.astype(BF16)
    from_row = lax.broadcasted_iota(jnp.int32, (128, 256), 0)
    to_lane = lax.broadcasted_iota(jnp.int32, (128, 256), 1)
    pick = (from_row == to_lane // 8 + 16).astype(BF16)
    rows_x = sum(dot_nn(piece, pick) for piece in split3(toeplitz(along_xy[0:1, :], 32)))
    wide_x = jnp.broadcast_to(rows_x[:, None, :], (32, 8, 256)).reshape(256, 256)
    small_y = split3(toeplitz(along_xy[1:2, :], 8))
    for offset in range(-2, 3):
        pick = (from_row == lax.rem(to_lane, 8) + 16 - 8 * offset).astype(BF16)
        rows_y = sum(dot_nn(piece, pick) for piece in small_y)
        wide_y = jnp.broadcast_to(rows_y[None], (32, 8, 256)).reshape(256, 256)
        big_high[offset + 2], big_low[offset + 2] = split2(wide_x * wide_y)


def scattered(view, slots, weights, column):
    chunk = lax.broadcasted_iota(jnp.int32, (32, 128), 1) // 32
    at = lax.broadcasted_iota(jnp.int32, (256, 512), 0)
    line = (lax.rem(at, 128) // 8 * 16 + at // 128 * 8 + lax.rem(at, 8)).astype(F32).astype(BF16)
    x, block = column // 4, column % 4
    numbers, values = [], []
    for t in range(4):
        tile = jnp.zeros((32, 128), F32)
        number = jnp.zeros((1, 128), F32)
        for place in range(4):
            device, at = 4 * x + t, 66 * ((place - block) % 4)
            tile = jnp.where(chunk == place, slots[device, at + 32 * view : at + 32 * view + 32, :], tile)
            row = slots[device, at + 64 + view : at + 65 + view, :]
            number = jnp.where(chunk[0:1] == place, row, number)
        values.append(tile)
        numbers.append(number)
    value = jnp.concatenate(values, axis=1)
    number = jnp.concatenate(numbers, axis=1)
    one, zero = jnp.ones((), BF16), jnp.zeros((), BF16)
    hot = jnp.where(line == number.astype(BF16), one, zero)
    left = jnp.concatenate([*split3(value), jnp.ones((16, 512), BF16)], axis=0)
    result = dot_nt(left, hot)
    data = result[0:32] + result[32:64] + result[64:96]
    for half in range(2):
        lanes = slice(128 * half, 128 * half + 128)
        to = slice(128 * x, 128 * x + 128)
        weight = weights[2 * block + half, view : view + 1, to]
        yield 2 * block + half, to, data[:, lanes], result[96:97, lanes] * weight


def scatter_kernel(slots, weights, data, cover):
    for column in range(8):
        for block, lanes, values, covered in scattered(1, slots, weights, column):
            data[block, :, lanes] = values
            cover[block, :, lanes] = jnp.broadcast_to(covered, (8, 128))


def payloads(value, far, near):
    upper = upper_half()
    far[...] = value[:, pl.ds(pl.multiple_of(16 * upper, 16), 16), :]
    near[...] = value[:, pl.ds(pl.multiple_of(16 - 16 * upper, 16), 16), :]


def at_end(planes):
    x, y, _, z = coordinates()
    slab = 2 * place_on_ring(x, y, z) + upper_half()
    return ((z == 0) & (slab == 0)) | ((z == planes - 1) & (slab == 7))


def widened(wide, value, far, near, margin):
    rows, upper = value.shape[1], upper_half()
    wide[:, margin : margin + rows, :] = value[...]
    side = margin + rows
    wide[:, pl.ds(pl.multiple_of(side * upper, 16), margin), :] = far
    wide[:, pl.ds(pl.multiple_of(side - side * upper, 16), margin), :] = near[...]


def blurred_into(wide, band, big_high, big_low, flat, total):
    rows = wide.shape[1] - 32
    weights = band[...]
    for column in range(8):
        for start in range(0, rows, 32):
            stacked = jnp.concatenate(split2(wide[column, start : start + 64, :]), axis=0)
            both = dot_nn(weights, stacked)
            at = column * rows + start
            flat[at : at + 32, :] = both[0:32] + both[32:64]
    high, low = split2(flat[...])

    for offset in (0, -2, -1, 1, 2):
        first, last = max(0, -offset), min(8, 8 - offset)
        start, stop = (first + offset) * rows, (last + offset) * rows
        size = stop - start
        both = jnp.concatenate([high[start:stop], low[start:stop]], axis=0)
        both = dot_nn(both, big_high[offset + 2])
        part = both[:size] + both[size:] + dot_nn(high[start:stop], big_low[offset + 2])
        if offset == 0:
            total[...] = part
        else:
            total[first * rows : last * rows, :] += part


def blur_kernel(est, far, near, band, big_high, big_low, blurred, wide, flat):
    widened(wide, est, far[...], near, 16)
    blurred_into(wide, band, big_high, big_low, flat, blurred)


def ratio_from(ratio, data, cover, blurred):
    for column in range(8):
        here = blurred[column * 32 : column * 32 + 32, :]
        ratio[column] = 1.0 + cover[column, 0:1, :] * (data[column] / here - 1.0)


def scatter_ratio_kernel(slots, weights, blurred, ratio):
    for column in range(8):
        for block, lanes, values, covered in scattered(0, slots, weights, column):
            here = blurred[32 * block : 32 * block + 32, lanes]
            ratio[block, :, lanes] = 1.0 + covered * (values / here - 1.0)


def update_kernel(planes, ratio, ratio_far, ratio_near, est, est_far, est_near, band, high, low, new, wide, flat, total):
    widened(wide, ratio, jnp.where(at_end(planes), 0.0, ratio_far[...]), ratio_near, 32)
    widened(new, est, est_far[...], est_near, 16)
    blurred_into(wide, band, high, low, flat, total)
    for column in range(8):
        new[column] = new[column] * total[column * 64 : column * 64 + 64, :]


def ratio_kernel(est, band, high, low, data, cover, ratio, far, near, flat, total):
    blurred_into(est, band, high, low, flat, total)
    ratio_from(ratio, data, cover, total)
    payloads(ratio, far, near)


def last_kernel(planes, ratio, far, near, band, big_high, big_low, est, *refs):
    (mine, other), pieces, (wide, flat, total) = refs[:2], refs[2:6], refs[6:]
    widened(wide, ratio, jnp.where(at_end(planes), 0.0, far[...]), near, 16)
    blurred_into(wide, band, big_high, big_low, flat, total)
    _, _, core, _ = coordinates()
    for flip, x, y, _ in chips():
        for turn in range(2):
            block = 4 * y + 2 * (core if turn == 0 else 1 - core)
            lanes = pl.ds(pl.multiple_of(128 * x, 128), 128)
            new = jnp.concatenate(
                [
                    est[block + half, 16:48, lanes]
                    * total[pl.ds(pl.multiple_of(32 * (block + half), 32), 32), lanes]
                    for half in range(2)
                ],
                axis=1,
            )
            if flip == 0:
                (mine, other)[turn][...] = new
            elif flip == 3:
                pieces[2 + turn][...] = new
            else:
                pieces[flip - 1][turn] = new


def join_kernel(*refs):
    pieces, others, (out, held, turned, left) = refs[:4], refs[4:8], refs[8:]
    upper = upper_half()
    for flip, _, _, place in chips():
        mine = pieces[flip][0] if flip in (1, 2) else pieces[flip][...]
        held[pl.ds(pl.multiple_of(64 * place + 32 * upper, 32), 32), :] = mine
        held[pl.ds(pl.multiple_of(64 * place + 32 - 32 * upper, 32), 32), :] = others[flip][...]

    def store(part):
        return pltpu.make_async_copy(turned.at[:, part], out.at[:, part], left.at[part])

    for part in range(2):
        turned[:, part] = held[:, 128 * part : 128 * part + 128].T.reshape(16, 8, 256)
        store(part).start()
    for part in range(2):
        store(part).wait()


def shape(*dims, dtype=F32):
    return jax.ShapeDtypeStruct(dims, dtype)


def swaps(planes):
    def flipped(by):
        return [(d * planes + z, (d ^ by) * planes + z) for d in range(8) for z in range(planes)]

    return [flipped(by) for by in (2, 4, 6)], flipped(7), flipped(1)


def slab_sweep(planes, estimate, raw_lines, line_index, psf, view_weight):
    far_pairs, near_pairs = chain_pairs(planes)
    to_chips, to_far_core, to_core = swaps(planes)
    ends = sorted(set(range(8 * planes)) - {source for source, _ in far_pairs})
    ring_pairs = far_pairs + [tuple(ends), tuple(ends[::-1])]

    def exchange(far, near):
        return (
            lax.ppermute(far, ALL, far_pairs),
            lax.ppermute(near, ALL, near_pairs),
        )

    own, *away = call(
        est_kernel, (shape(72, 256),) * 4, [SMEM, VMEM], [pltpu.VMEM((256, 256), F32)]
    )(view_weight.reshape(2), estimate.reshape(16, 2, 8, 256))
    here = [own] + [lax.ppermute(piece, ALL, pairs) for piece, pairs in zip(away, to_chips)]
    there = [lax.ppermute(piece, ALL, to_core) for piece in here]

    anywhere = pl.BlockSpec(memory_space=pl.ANY)
    slots = call(
        functools.partial(lines_kernel, planes),
        shape(8, 66 * planes, 128),
        [anywhere, anywhere],
        [
            pltpu.VMEM((2, 4, planes, 32, 256), F32),
            pltpu.VMEM((8, 128), jnp.int32),
            pltpu.VMEM((8, 66 * planes, 128), F32),
            pltpu.SemaphoreType.DMA((2,)),
            pltpu.SemaphoreType.DMA((1,)),
            pltpu.SemaphoreType.DMA((planes,)),
        ],
        out_specs=anywhere,
        vmem=56,
    )(raw_lines.reshape(2, 4, planes, 32, 256), line_index.reshape(8, 128))
    slots = slots.reshape(8 * planes, 1, 66 * 128)
    slots = lax.all_to_all(slots, ALL, split_axis=0, concat_axis=0, tiled=True)
    slots = slots.reshape(8, 66 * planes, 128)
    half, full = shape(8, 16, 256), shape(8, 32, 256)

    def work(*dims):
        return pltpu.VMEM(dims, F32)

    est, weights, est_far, est_near = call(slab_kernel, (full, shape(8, 8, 256), half, half), [VMEM] * 8)(
        *here, *there
    )
    est_far = lax.ppermute(est_far, ALL, far_pairs)
    def matrices(view, way, after):
        big = shape(5, 256, 256, dtype=BF16)
        big_high, big_low, band = call(
            functools.partial(taps_kernel, view, way),
            (big, big, shape(64, 128, dtype=BF16)),
            [VMEM, anywhere],
            [work(8, 128)],
            flops=1 << 30,
        )(psf.transpose(1, 0, 2), after)
        return band, big_high, big_low

    blurred = call(
        blur_kernel, shape(256, 256), [VMEM] * 6, [work(8, 64, 256), work(256, 256)], flops=1 << 30
    )(est, est_far, est_near, *matrices(0, 0, est))
    ratio = call(scatter_ratio_kernel, full, [VMEM] * 3, flops=1 << 30)(slots, weights, blurred)
    data, cover = call(scatter_kernel, (full, shape(8, 8, 256)), [VMEM] * 2, flops=1 << 30)(slots, weights)
    est = call(
        functools.partial(update_kernel, planes),
        shape(8, 64, 256),
        [VMEM] * 9,
        [work(8, 96, 256), work(512, 256), work(512, 256)],
        flops=1 << 30,
    )(ratio, lax.ppermute(ratio, ALL, far_pairs), lax.ppermute(ratio, ALL, near_pairs), est, est_far, est_near, *matrices(0, 1, slots))
    ratio, far, near = call(
        ratio_kernel, (full, half, half), [VMEM] * 6, [work(256, 256), work(256, 256)], flops=1 << 30
    )(est, *matrices(1, 0, slots), data, cover)
    column, pair = shape(32, 256), shape(2, 32, 256)
    mine, other, *away = call(
        functools.partial(last_kernel, planes),
        (column, column, pair, pair, column, column),
        [VMEM] * 7,
        [work(8, 64, 256), work(256, 256), work(256, 256)],
        flops=1 << 30,
    )(ratio, lax.ppermute(far, ALL, ring_pairs), lax.ppermute(near, ALL, near_pairs), *matrices(1, 1, ratio), est)
    *away, last = [lax.ppermute(piece, ALL, pairs) for piece, pairs in zip(away, to_chips + [to_far_core])]
    first = lax.ppermute(jnp.stack([other, away[0][1]]), ALL, to_core)
    others = [first[0], first[1], lax.ppermute(away[1][1], ALL, to_core), last]
    out = call(
        join_kernel,
        shape(16, 2, 8, 256),
        [VMEM] * 8,
        [work(256, 256), work(16, 2, 8, 256), pltpu.SemaphoreType.DMA((2,))],
        out_specs=anywhere,
    )(mine, *away, *others)
    return out.reshape(16, 16, 256)


def padded(block, sides, width):
    for axis, dim in sides:
        count = lax.axis_size(axis)
        forward = [(i, i + 1) for i in range(count - 1)]
        backward = [(target, source) for source, target in forward]
        low = lax.ppermute(
            lax.slice_in_dim(block, block.shape[dim] - width, None, axis=dim), axis, forward
        )
        high = lax.ppermute(lax.slice_in_dim(block, 0, width, axis=dim), axis, backward)
        block = jnp.concatenate([low, block, high], axis=dim)
    return block


def band_matrix(taps, length):
    width = taps.shape[0]
    rows = lax.broadcasted_iota(jnp.int32, (length + width - 1, length), 0)
    cols = lax.broadcasted_iota(jnp.int32, (length + width - 1, length), 1)
    offset = rows - cols
    valid = (offset >= 0) & (offset < width)
    return jnp.where(valid, taps[jnp.clip(offset, 0, width - 1)], 0.0)


def along_x(extended, matrix_x):
    lead, size_y, size_z = extended.shape
    flat = extended.reshape(lead, size_y * size_z)
    result = jnp.dot(matrix_x.T, flat, precision=lax.Precision.HIGHEST)
    return result.reshape(matrix_x.shape[1], size_y, size_z)


def blur(field, taps):
    half_width = (taps.shape[1] - 1) // 2
    size_x, size_y, size_z = field.shape
    matrix_x = band_matrix(taps[0], size_x)
    matrix_y = band_matrix(taps[1], size_y)
    matrix_z = band_matrix(taps[2], size_z)
    highest = lax.Precision.HIGHEST
    extended = padded(field, (("gz", 2),), half_width)
    result = jnp.einsum("abj,jc->abc", extended, matrix_z, precision=highest)
    extended = padded(result, (("gy", 1),), half_width)
    result = jnp.einsum("ajc,jb->abc", extended, matrix_y, precision=highest)
    extended = padded(result, (("gx", 0),), half_width)
    result = along_x(extended, matrix_x)
    return result


def block_sweep(estimate, raw_lines, line_index, psf, view_weight):
    size_x, size_y, size_z = estimate.shape
    block_lines = size_x * size_y
    views = raw_lines.shape[0]
    group = lax.axis_size(("gy", "gz"))
    slots = line_index.shape[-1]
    capacity = slots // group
    lines = raw_lines.reshape(views, group, capacity, size_z)
    indices = line_index.reshape(views, group, capacity)
    lines, indices = (
        lax.all_to_all(lines, ("gy", "gz"), split_axis=1, concat_axis=1, tiled=True),
        lax.all_to_all(indices, ("gy", "gz"), split_axis=1, concat_axis=1, tiled=True),
    )
    est = estimate
    for view in range(views):
        flat_index = indices[view].reshape(-1)
        flat_lines = lines[view].reshape(-1, size_z)
        volume = (
            jnp.zeros((block_lines, size_z), jnp.float32)
            .at[flat_index]
            .set(flat_lines, mode="drop")
        )
        volume = volume.reshape(size_x, size_y, size_z)
        cover = jnp.zeros((block_lines,), jnp.float32).at[flat_index].set(1.0, mode="drop")
        cover = cover.reshape(size_x, size_y, 1)
        weight = view_weight[view].reshape(()).astype(jnp.float32) * 0.25
        taps = psf[view] / jnp.sum(psf[view], axis=1, keepdims=True)
        blurred = blur(est, taps)
        ratio = 1.0 + weight * cover * (volume / blurred - 1.0)
        est = est * blur(ratio, taps[:, ::-1])
    return est


def solution(mesh):
    placed = (
        P("gx", "gy", "gz"),
        P(None, "gx", ("gy", "gz"), None, None),
        P(None, "gx", ("gy", "gz"), None),
        P(),
        P(None, "gx", "gy", "gz"),
    )
    sizes = tuple(mesh.shape[axis] for axis in ALL)

    def on_device(estimate, raw_lines, line_index, psf, view_weight):
        capacity = line_index.shape[-1] // (sizes[1] * sizes[2])
        fits = (
            sizes == (2, 4, 4)
            and estimate.shape == (16, 16, 256)
            and raw_lines.shape[0] == 2
            and capacity == 32
            and psf.shape == (2, 3, 33)
        )
        plan = functools.partial(slab_sweep, sizes[2]) if fits else block_sweep
        return plan(estimate, raw_lines, line_index, psf, view_weight)

    return jax.shard_map(
        on_device, mesh=mesh, in_specs=placed, out_specs=P("gx", "gy", "gz"), check_vma=False
    )
```
